32 devices in a mesh: grp: 2 (over x), slab: 16 (over z, y, core).
Axes of the slice: x: 2, y: 2, z: 4, core: 2. Of those that a mesh axis runs over, the one named last changes fastest.
Arguments:
- directions: float32 [8, 64, 256, 128], P('grp', 'slab'), parts along dimension 0, may hold values from -36 to 36
- eigen_basis: float32 [32, 64, 256, 128], P('grp', 'slab'), parts along dimension 0, may hold values from -11 to 11
- flow_first: float32 [64, 256, 128], P('slab'), may hold values from -0.15 to 0.15
- flow_second: float32 [64, 256, 128], P('slab'), may hold values from -0.15 to 0.15
- flow_depth: float32 [64, 256, 128], P('slab'), may hold values from -0.15 to 0.15
- face_codes: int32 [4], replicated, may hold values from 0 to 1
- sensor_cells: int32 [131072], P(('grp', 'slab')), parts along dimension 0, may hold values from 0 to 131071
- sensor_weight: float32 [131072], P(('grp', 'slab')), parts along dimension 0, may hold values from 0.5 to 4
Outputs:
- new_directions: float32 [8, 64, 256, 128], P('grp', 'slab'), parts along dimension 0
- coeffs: float32 [32, 4], P('grp'), parts along dimension 0
The draws below stay inside these ranges and needn't reach their ends.
There are 2 independent parts, one for each index of `grp`. The reference program is written for one: setup_inputs(seed, part) draws one part's arguments, and reference() takes and returns one part's arrays. A program takes and returns all parts, laid end to end along the dimension named above; an argument that names none is the same for every part. Nothing has to cross between parts.
Inputs may be any that keep to these rules, and one draw needn't show every extreme that they name: `face_codes`: 0 marks a face with zero boundary values, 1 a closed face. `sensor_cells`: block b of 4096 entries lies in planes b * 4 to (b + 1) * 4 - 1 and holds offsets counted from that block's first cell.
All inputs are finite; a program needn't handle non-finite values.
Results may differ from the reference program's by a relative error of at most 0.00015.
Values sent between devices are 32-bit elements; how exact they have to be, the bound alone decides.
No kernel may reach another device: no remote copies, remote signals or barrier semaphores. Data moves between devices by JAX's collectives and lax.ppermute only.
A program may use at most 128 MiB of HBM per device.

```python
import math
import jax
import jax.numpy as jnp
from jax import lax

NX = 256
NY = 128
CZ = 4
DIRS = 4
RANK = 16
OBS_DEV = 4096
STEPS = 2
SWEEPS = 3
NZ = 64
NOBS = 65536


def shared_normals(key):
    return jax.random.truncated_normal(key, -6.0, 6.0, (DIRS, NZ, NX, NY), jnp.float32)


def draw_directions(key, part):
    common = shared_normals(key)
    height = jnp.arange(NZ, dtype=jnp.float32) / max(NZ - 1, 1)
    rising = jnp.exp(height * math.log(3.0))[None, :, None, None]
    return common * rising


def draw_eigen_basis(key, part):
    common = shared_normals(key)
    key = jax.random.fold_in(key, 5)
    independent = jax.random.truncated_normal(key, -6.0, 6.0, (RANK, NZ, NX, NY), jnp.float32)
    return 0.8 * jnp.tile(common, (RANK // DIRS, 1, 1, 1)) + independent


def place_ends(drawn, stream_key, least, high):
    longest = drawn.shape.index(max(drawn.shape))
    spots = []
    for shift in (0, 1):
        where = [jax.random.randint(jax.random.fold_in(stream_key, axis), (), 0, length) for axis, length in enumerate(drawn.shape)]
        where[longest] = (where[longest] + shift) % drawn.shape[longest]
        spots.append(tuple(where))
    return drawn.at[spots[0]].set(least).at[spots[1]].set(high)


def shard_levels(stream_key, shape, shards, low, top_value):
    factor_of = 1.0
    for dim, parts in shards:
        steps = jax.random.uniform(jax.random.fold_in(jax.random.fold_in(stream_key, 6), dim), (parts,), jnp.float32, low / len(shards), top_value / len(shards))
        factor_of = factor_of * jnp.repeat(jnp.exp(steps), shape[dim] // parts).reshape((-1,) + (1,) * (len(shape) - 1 - dim))
    return factor_of


def setup_inputs(seed: int = 0, part: int = 0) -> dict:
    streams_of = jax.random.split(jax.random.key(seed), 9)
    own_keys = jax.random.split(jax.random.fold_in(streams_of[8], part), 9)
    directions = draw_directions(jax.random.fold_in(jax.random.fold_in(streams_of[8], part), 71), part)
    eigen_basis = draw_eigen_basis(jax.random.fold_in(jax.random.fold_in(streams_of[8], part), 71), part)
    flow_first = jnp.clip(jax.random.uniform(streams_of[2], (NZ, NX, NY), jnp.float32, -0.15, 0.15) * shard_levels(streams_of[2], (NZ, NX, NY), ((0, 16),), -0.4, 0.0), -0.15, 0.15)
    flow_second = jnp.clip(jax.random.uniform(streams_of[3], (NZ, NX, NY), jnp.float32, -0.15, 0.15) * shard_levels(streams_of[3], (NZ, NX, NY), ((0, 16),), -0.4, 0.0), -0.15, 0.15)
    flow_depth = jnp.clip(jax.random.uniform(streams_of[4], (NZ, NX, NY), jnp.float32, -0.15, 0.15) * shard_levels(streams_of[4], (NZ, NX, NY), ((0, 16),), -0.4, 0.0), -0.15, 0.15)
    face_codes = place_ends(jax.random.randint(streams_of[5], (4,), 0, 2), jax.random.fold_in(streams_of[5], 1), 0, 1).astype(jnp.int32)
    sensor_cells = place_ends(jax.random.randint(own_keys[6], (NOBS,), 0, CZ * NX * NY), jax.random.fold_in(own_keys[6], 1), 0, (CZ * NX * NY) - 1).astype(jnp.int32)
    sensor_weight = jnp.clip(jnp.exp(math.log(4.0) - 2.0794415 * jax.random.uniform(own_keys[7], (NOBS,), jnp.float32) ** shard_levels(own_keys[7], (NOBS,), ((0, 16),), -0.2, 0.2)), 0.5, 4.0)
    return dict(directions=directions, eigen_basis=eigen_basis, flow_first=flow_first, flow_second=flow_second, flow_depth=flow_depth, face_codes=face_codes, sensor_cells=sensor_cells, sensor_weight=sensor_weight)


DIFFUSION = 0.2
GAMMA = 0.5

def lower_along(values, dimension):
    length = values.shape[dimension]
    leading = jnp.zeros_like(lax.slice_in_dim(values, 0, 1, axis=dimension))
    return jnp.concatenate([leading, lax.slice_in_dim(values, 0, length - 1, axis=dimension)], dimension)

def end_factors(code_start, code_end, length):
    position = jnp.arange(length)
    open_start = jnp.where(code_start == 0, 1.0, 0.0).astype(jnp.float32)
    open_end = jnp.where(code_end == 0, 1.0, 0.0).astype(jnp.float32)
    at_start = jnp.where(position == 0, open_start, 1.0).astype(jnp.float32)
    at_end = jnp.where(position == length - 1, open_end, 1.0).astype(jnp.float32)
    return (at_start, at_end)

def diagonal_of(flows, face_codes):
    flow_first, first_below, flow_second, second_below, flow_depth, depth_below = flows
    start_one, end_one = end_factors(face_codes[0], face_codes[1], flow_first.shape[1])
    start_two, end_two = end_factors(face_codes[2], face_codes[3], flow_first.shape[2])
    start_one = start_one[None, :, None]
    end_one = end_one[None, :, None]
    start_two = start_two[None, None, :]
    end_two = end_two[None, None, :]
    diagonal = 1.0 + end_one * (DIFFUSION + jax.nn.relu(flow_first))
    diagonal = diagonal + start_one * (DIFFUSION + jax.nn.relu(-first_below))
    diagonal = diagonal + end_two * (DIFFUSION + jax.nn.relu(flow_second))
    diagonal = diagonal + start_two * (DIFFUSION + jax.nn.relu(-second_below))
    diagonal = diagonal + (DIFFUSION + jax.nn.relu(flow_depth))
    diagonal = diagonal + (DIFFUSION + jax.nn.relu(-depth_below))
    return diagonal

def neighbor_sum(padded, flows, adjoint):
    flow_first, first_below, flow_second, second_below, flow_depth, depth_below = flows
    orient = 1.0 if adjoint else -1.0
    middle = padded[:, 1:-1]
    along_first = jnp.pad(middle, ((0, 0), (0, 0), (1, 1), (0, 0)))
    along_second = jnp.pad(middle, ((0, 0), (0, 0), (0, 0), (1, 1)))
    summed = (DIFFUSION + jax.nn.relu(orient * flow_first)) * along_first[:, :, 2:]
    summed = summed + (DIFFUSION + jax.nn.relu(-orient * first_below)) * along_first[:, :, :-2]
    summed = summed + (DIFFUSION + jax.nn.relu(orient * flow_second)) * along_second[:, :, :, 2:]
    summed = summed + (DIFFUSION + jax.nn.relu(-orient * second_below)) * along_second[:, :, :, :-2]
    summed = summed + (DIFFUSION + jax.nn.relu(orient * flow_depth)) * padded[:, 2:]
    summed = summed + (DIFFUSION + jax.nn.relu(-orient * depth_below)) * padded[:, :-2]
    return summed

def jacobi_solve(rhs, flows, diagonal, adjoint):
    iterate = rhs
    for repeat in range(SWEEPS):
        padded = jnp.pad(iterate, ((0, 0), (1, 1), (0, 0), (0, 0)))
        iterate = (rhs + neighbor_sum(padded, flows, adjoint)) / diagonal
    return iterate

def basis_coefficients(gram_matrix, projections):
    factor_lower = jnp.linalg.cholesky(gram_matrix)
    partial_value = lax.linalg.triangular_solve(factor_lower, projections, left_side=True, lower=True)
    return lax.linalg.triangular_solve(factor_lower, partial_value, left_side=True, lower=True, transpose_a=True)

def reference(directions, eigen_basis, flow_first, flow_second, flow_depth, face_codes, sensor_cells, sensor_weight):
    first_below = lower_along(flow_first, 1)
    second_below = lower_along(flow_second, 2)
    depth_below = lower_along(flow_depth, 0)
    flows = (flow_first, first_below, flow_second, second_below, flow_depth, depth_below)
    diagonal = diagonal_of(flows, face_codes)
    state = jnp.zeros_like(directions)
    for moment in range(STEPS):
        state = jacobi_solve(state + directions, flows, diagonal, False)
    slab_cells = CZ * NX * NY
    offsets = (jnp.arange(NOBS) // OBS_DEV).astype(jnp.int32) * slab_cells
    location = sensor_cells.astype(jnp.int32) + offsets.astype(jnp.int32)
    cell_weight = jnp.zeros((NZ * NX * NY,), sensor_weight.dtype).at[location].add(sensor_weight)
    forcing = state * cell_weight.reshape(state.shape[1:])[None]
    adjoint_state = forcing
    summed = jnp.zeros_like(directions)
    for moment in range(STEPS):
        adjoint_state = jacobi_solve(adjoint_state, flows, diagonal, True)
        summed = summed + adjoint_state
    image = summed + GAMMA * directions
    basis_flat = eigen_basis.reshape(RANK, -1)
    image_flat = image.reshape(DIRS, -1)
    gram_matrix = jnp.dot(basis_flat, basis_flat.T, precision=lax.Precision.HIGHEST)
    projections = jnp.dot(basis_flat, image_flat.T, precision=lax.Precision.HIGHEST)
    coeffs = basis_coefficients(gram_matrix, projections)
    remainder = image_flat - jnp.dot(coeffs.T, basis_flat, precision=lax.Precision.HIGHEST)
    energy = lax.optimization_barrier(jnp.sum(remainder * remainder, axis=1))
    factor = lax.rsqrt(energy / (NZ * NX * NY) + 1e-06)
    new_directions = (remainder * factor[:, None]).reshape(directions.shape)
    return (new_directions, coeffs)
```

```python
import functools

import jax
import jax.numpy as jnp
from jax import lax
from jax.experimental import pallas as pl
from jax.experimental.pallas import tpu as pltpu
from jax.sharding import PartitionSpec as P

STEPS = 2
SWEEPS = 3


DIFFUSION = 0.2
GAMMA = 0.5


def from_behind(value, axis, steps):
    count = lax.axis_size(axis)
    first, last = (max(0, -steps), min(count, count - steps))
    return lax.ppermute(value, axis, [(source, source + steps) for source in range(first, last)])


def extended(cells, sides, width):
    for axis, dim in sides:
        count = lax.axis_size(axis)
        ends = count - 1
        head = lax.slice_in_dim(cells, 0, width, axis=dim)
        tail = lax.slice_in_dim(cells, cells.shape[dim] - width, cells.shape[dim], axis=dim)
        cells = jnp.concatenate(
            [
                lax.ppermute(tail, axis, [(i, (i + 1) % count) for i in range(ends)]),
                cells,
                lax.ppermute(head, axis, [((i + 1) % count, i) for i in range(ends)]),
            ],
            axis=dim,
        )
    return cells


def lower_along(values, dimension):
    length = values.shape[dimension]
    leading = jnp.zeros_like(lax.slice_in_dim(values, 0, 1, axis=dimension))
    return jnp.concatenate(
        [leading, lax.slice_in_dim(values, 0, length - 1, axis=dimension)], dimension
    )


def end_factors(code_start, code_end, length):
    position = jnp.arange(length)
    open_start = jnp.where(code_start == 0, 1.0, 0.0).astype(jnp.float32)
    open_end = jnp.where(code_end == 0, 1.0, 0.0).astype(jnp.float32)
    at_start = jnp.where(position == 0, open_start, 1.0)
    at_end = jnp.where(position == length - 1, open_end, 1.0)
    return (at_start, at_end)


def diagonal_of(flows, face_codes):
    flow_first, first_below, flow_second, second_below, flow_depth, depth_below = flows
    start_one, end_one = end_factors(face_codes[0], face_codes[1], flow_first.shape[1])
    start_two, end_two = end_factors(face_codes[2], face_codes[3], flow_first.shape[2])
    start_one = start_one[None, :, None]
    end_one = end_one[None, :, None]
    start_two = start_two[None, None, :]
    end_two = end_two[None, None, :]
    diagonal = 1.0 + end_one * (DIFFUSION + jax.nn.relu(flow_first))
    diagonal = diagonal + start_one * (DIFFUSION + jax.nn.relu(-first_below))
    diagonal = diagonal + end_two * (DIFFUSION + jax.nn.relu(flow_second))
    diagonal = diagonal + start_two * (DIFFUSION + jax.nn.relu(-second_below))
    diagonal = diagonal + (DIFFUSION + jax.nn.relu(flow_depth))
    diagonal = diagonal + (DIFFUSION + jax.nn.relu(-depth_below))
    return diagonal


def neighbor_sum(padded, flows, adjoint):
    flow_first, first_below, flow_second, second_below, flow_depth, depth_below = flows
    orient = 1.0 if adjoint else -1.0
    middle = padded[:, 1:-1]
    along_first = jnp.pad(middle, ((0, 0), (0, 0), (1, 1), (0, 0)))
    along_second = jnp.pad(middle, ((0, 0), (0, 0), (0, 0), (1, 1)))
    summed = (DIFFUSION + jax.nn.relu(orient * flow_first)) * along_first[:, :, 2:]
    summed = summed + (DIFFUSION + jax.nn.relu(-orient * first_below)) * along_first[:, :, :-2]
    summed = summed + (DIFFUSION + jax.nn.relu(orient * flow_second)) * along_second[:, :, :, 2:]
    summed = summed + (DIFFUSION + jax.nn.relu(-orient * second_below)) * along_second[:, :, :, :-2]
    summed = summed + (DIFFUSION + jax.nn.relu(orient * flow_depth)) * padded[:, 2:]
    summed = summed + (DIFFUSION + jax.nn.relu(-orient * depth_below)) * padded[:, :-2]
    return summed


LANES = 128
EXACT = lax.Precision.HIGHEST


def lane_sums(stack):
    ones = jnp.ones((8, LANES), jnp.float32)
    return lax.dot_general(
        ones, stack, (((1,), (1,)), ((), ())), precision=EXACT, preferred_element_type=jnp.float32
    )


def gram_kernel(basis_ref, out_ref, acc_ref):
    rank = basis_ref.shape[0]
    rows = basis_ref.shape[1]
    step = pl.program_id(0)
    tile = 4

    @pl.when(step == 0)
    def _():
        acc_ref[...] = jnp.zeros_like(acc_ref)

    for i0 in range(0, rank, tile):
        for j0 in range(i0, rank, tile):
            pairs = [(i, j) for i in range(i0, i0 + tile) for j in range(j0, j0 + tile) if i <= j]

            def add(k, sums, i0=i0, j0=j0, pairs=pairs):
                at = pl.ds(pl.multiple_of(k * 8, 8), 8)
                left = {i: basis_ref[i, at, :] for i in range(i0, i0 + tile)}
                right = left if i0 == j0 else {j: basis_ref[j, at, :] for j in range(j0, j0 + tile)}
                return [s + left[i] * right[j] for s, (i, j) in zip(sums, pairs)]

            sums = [jnp.zeros((8, LANES), jnp.float32) for _ in pairs]
            sums = lax.fori_loop(0, rows // 8, add, sums, unroll=4)
            for (i, j), s in zip(pairs, sums):
                acc_ref[i, j] += s

    @pl.when(step == pl.num_programs(0) - 1)
    def _():
        row = lax.broadcasted_iota(jnp.int32, (rank, rank), 0)
        col = lax.broadcasted_iota(jnp.int32, (rank, rank), 1)
        gram = jnp.zeros((rank, rank), jnp.float32)
        for i in range(rank):
            sums = lane_sums(jnp.sum(acc_ref[i], axis=1))
            gram = jnp.where(row == i, jnp.broadcast_to(sums[0:1, :], (rank, rank)), gram)
        upper = jnp.where(col >= row, gram, 0.0)
        strict = jnp.where(col > row, gram, 0.0)
        whole = upper + strict.T
        for r in range(out_ref.shape[0] // rank):
            out_ref[r * rank : (r + 1) * rank, 0:rank] = whole


def gram_parts(basis, count):
    rank, rows, _ = basis.shape
    chunk = 128
    return pl.pallas_call(
        gram_kernel,
        grid=(rows // chunk,),
        in_specs=[pl.BlockSpec((rank, chunk, LANES), lambda k: (0, k, 0))],
        out_specs=pl.BlockSpec((count * rank, LANES), lambda k: (0, 0)),
        out_shape=jax.ShapeDtypeStruct((count * rank, LANES), jnp.float32),
        scratch_shapes=[pltpu.VMEM((rank, rank, 8, LANES), jnp.float32)],
        compiler_params=pltpu.CompilerParams(vmem_limit_bytes=32 << 20),
        cost_estimate=pl.CostEstimate(
            flops=rank * rank * rows * LANES, bytes_accessed=rank * rows * LANES * 4, transcendentals=0
        ),
        name="gram",
    )(basis)


def spread(tile, count):
    return lax.all_to_all(tile, "slab", 0, 0, tiled=True) if count > 1 else tile


def projection_kernel(basis_ref, image_ref, out_ref, acc_ref):
    rank = basis_ref.shape[0]
    dirs, rows, _ = image_ref.shape
    step = pl.program_id(0)
    tile = 8

    @pl.when(step == 0)
    def _():
        acc_ref[...] = jnp.zeros_like(acc_ref)

    for i0 in range(0, rank, tile):

        def add(k, sums, i0=i0):
            at = pl.ds(pl.multiple_of(k * 8, 8), 8)
            image = [image_ref[d, at, :] for d in range(dirs)]
            out = []
            for i in range(tile):
                q = basis_ref[i0 + i, at, :]
                out += [sums[i * dirs + d] + q * image[d] for d in range(dirs)]
            return out

        sums = [jnp.zeros((8, LANES), jnp.float32) for _ in range(tile * dirs)]
        sums = lax.fori_loop(0, rows // 8, add, sums, unroll=4)
        for i in range(tile):
            for d in range(dirs):
                acc_ref[d, i0 + i] += sums[i * dirs + d]

    @pl.when(step == pl.num_programs(0) - 1)
    def _():
        row = lax.broadcasted_iota(jnp.int32, (8, rank), 0)
        table = jnp.zeros((8, rank), jnp.float32)
        for d in range(dirs):
            table = jnp.where(row == d, lane_sums(jnp.sum(acc_ref[d], axis=1)), table)
        for r in range(out_ref.shape[0] // 8):
            out_ref[r * 8 : (r + 1) * 8, 0:rank] = table


def projection_parts(basis, image, count):
    rank, rows, _ = basis.shape
    dirs = image.shape[0]
    chunk = 128
    return pl.pallas_call(
        projection_kernel,
        grid=(rows // chunk,),
        in_specs=[
            pl.BlockSpec((rank, chunk, LANES), lambda k: (0, k, 0)),
            pl.BlockSpec((dirs, chunk, LANES), lambda k: (0, k, 0)),
        ],
        out_specs=pl.BlockSpec((count * 8, LANES), lambda k: (0, 0)),
        out_shape=jax.ShapeDtypeStruct((count * 8, LANES), jnp.float32),
        scratch_shapes=[pltpu.VMEM((dirs, rank, 8, LANES), jnp.float32)],
        compiler_params=pltpu.CompilerParams(vmem_limit_bytes=32 << 20),
        cost_estimate=pl.CostEstimate(
            flops=2 * rank * dirs * rows * LANES,
            bytes_accessed=(rank + dirs) * rows * LANES * 4,
            transcendentals=0,
        ),
        name="projections",
    )(basis, image)


def summed_tile(parts_ref):
    total = parts_ref[0:8, :]
    for r in range(1, parts_ref.shape[0] // 8):
        total = total + parts_ref[r * 8 : (r + 1) * 8, :]
    return total


def remainder_kernel(
    parts_ref, inverse_ref, basis_ref, image_ref, rem_ref, coeffs_ref, out_ref, splat_ref, energy_ref
):
    rank = basis_ref.shape[0]
    dirs, rows, _ = image_ref.shape
    step = pl.program_id(0)
    tile = 4

    @pl.when(step == 0)
    def _():
        table = summed_tile(parts_ref)[:, 0:rank]
        inverse = inverse_ref[...]
        half = lax.dot_general(
            table, inverse, (((1,), (1,)), ((), ())), precision=EXACT,
            preferred_element_type=jnp.float32,
        )
        flat = lax.dot_general(
            half, inverse, (((1,), (0,)), ((), ())), precision=EXACT,
            preferred_element_type=jnp.float32,
        )
        coeffs_ref[...] = flat.T[:, 0:dirs]
        for d in range(dirs):
            for j in range(rank):
                splat_ref[d * rank + j] = jnp.broadcast_to(flat[d : d + 1, j : j + 1], (8, LANES))
        energy_ref[...] = jnp.zeros_like(energy_ref)

    for j0 in range(0, rank, tile):
        last = j0 + tile == rank
        weights = [[splat_ref[d * rank + j] for j in range(j0, j0 + tile)] for d in range(dirs)]

        def take(k, energy, j0=j0, last=last, weights=weights):
            at = pl.ds(pl.multiple_of(k * 8, 8), 8)
            basis = [basis_ref[j, at, :] for j in range(j0, j0 + tile)]
            out = []
            for d in range(dirs):
                left = image_ref[d, at, :] if j0 == 0 else rem_ref[d, at, :]
                parts = [w * q for w, q in zip(weights[d], basis)]
                left = left - ((parts[0] + parts[1]) + (parts[2] + parts[3]))
                rem_ref[d, at, :] = left
                out.append(energy[d] + left * left if last else energy[d])
            return out

        energy = [jnp.zeros((8, LANES), jnp.float32) for _ in range(dirs)]
        energy = lax.fori_loop(0, rows // 8, take, energy, unroll=4)
        if last:
            for d in range(dirs):
                energy_ref[d] += energy[d]

    @pl.when(step == pl.num_programs(0) - 1)
    def _():
        row = lax.broadcasted_iota(jnp.int32, (8, LANES), 0)
        tile_out = jnp.zeros((8, LANES), jnp.float32)
        for d in range(dirs):
            total = jnp.sum(jnp.sum(energy_ref[d], axis=0, keepdims=True), axis=1, keepdims=True)
            tile_out = jnp.where(row == d, jnp.broadcast_to(total, (8, LANES)), tile_out)
        for r in range(out_ref.shape[0] // 8):
            out_ref[r * 8 : (r + 1) * 8, :] = tile_out


def remainders(parts, inverse, basis, image, count):
    rank, rows, _ = basis.shape
    dirs = image.shape[0]
    chunk = 128
    whole = lambda *shape: pl.BlockSpec(shape, lambda k: (0,) * len(shape))
    return pl.pallas_call(
        remainder_kernel,
        grid=(rows // chunk,),
        in_specs=[
            whole(count * 8, LANES),
            whole(rank, rank),
            pl.BlockSpec((rank, chunk, LANES), lambda k: (0, k, 0)),
            pl.BlockSpec((dirs, chunk, LANES), lambda k: (0, k, 0)),
        ],
        out_specs=[
            pl.BlockSpec((dirs, chunk, LANES), lambda k: (0, k, 0)),
            whole(rank, dirs),
            whole(count * 8, LANES),
        ],
        out_shape=[
            jax.ShapeDtypeStruct((dirs, rows, LANES), jnp.float32),
            jax.ShapeDtypeStruct((rank, dirs), jnp.float32),
            jax.ShapeDtypeStruct((count * 8, LANES), jnp.float32),
        ],
        scratch_shapes=[
            pltpu.VMEM((dirs * rank, 8, LANES), jnp.float32),
            pltpu.VMEM((dirs, 8, LANES), jnp.float32),
        ],
        compiler_params=pltpu.CompilerParams(vmem_limit_bytes=32 << 20),
        cost_estimate=pl.CostEstimate(
            flops=2 * rank * dirs * rows * LANES,
            bytes_accessed=(rank + 2 * dirs) * rows * LANES * 4,
            transcendentals=0,
        ),
        name="remainder",
    )(parts, inverse, basis, image)


def scale_kernel(cells, parts_ref, rem_ref, new_ref):
    energy = summed_tile(parts_ref)
    value = energy / cells + 1e-06
    root = lax.rsqrt(value)
    root = root * (1.5 - (0.5 * value * root) * root)
    for d in range(rem_ref.shape[0]):
        new_ref[d] = rem_ref[d] * root[d : d + 1, :]


def scaled(parts, rem, cells, count):
    dirs, rows, _ = rem.shape
    chunk = 256
    return pl.pallas_call(
        functools.partial(scale_kernel, cells),
        grid=(rows // chunk,),
        in_specs=[
            pl.BlockSpec((count * 8, LANES), lambda k: (0, 0)),
            pl.BlockSpec((dirs, chunk, LANES), lambda k: (0, k, 0)),
        ],
        out_specs=pl.BlockSpec((dirs, chunk, LANES), lambda k: (0, k, 0)),
        out_shape=jax.ShapeDtypeStruct((dirs, rows, LANES), jnp.float32),
        compiler_params=pltpu.CompilerParams(vmem_limit_bytes=32 << 20),
        name="scale",
    )(parts, rem)


def sensor_kernel(first_row, planes, width, cells_ref, weight_ref, out_ref):
    height = out_ref.shape[0] // planes
    first = first_row if isinstance(first_row, int) else first_row()
    sensors = cells_ref.shape[1]
    chunk = 512
    targets = out_ref.shape[0]
    rows = lax.broadcasted_iota(jnp.int32, (targets, chunk), 0)
    lanes = lax.broadcasted_iota(jnp.int32, (LANES, chunk), 0)
    total = jnp.zeros((targets, 3 * LANES), jnp.float32)
    for k in range(sensors // chunk):
        cell = cells_ref[0:1, k * chunk : (k + 1) * chunk]
        weight = weight_ref[0:1, k * chunk : (k + 1) * chunk]
        line = cell // LANES
        lane = cell - line * LANES
        plane = line // width
        row = line - plane * width - first
        inside = (row >= 0) & (row < height)
        target = jnp.where(inside, plane * height + row, -1)
        high = weight.astype(jnp.bfloat16).astype(jnp.float32)
        rest = weight - high
        middle = rest.astype(jnp.bfloat16).astype(jnp.float32)
        low = rest - middle
        hot = jnp.where(rows == target, 1.0, 0.0).astype(jnp.bfloat16)
        here = lanes == lane
        parts = [jnp.where(here, part, 0.0).astype(jnp.bfloat16) for part in (high, middle, low)]
        total += lax.dot_general(
            hot, jnp.concatenate(parts, 0), (((1,), (1,)), ((), ())),
            preferred_element_type=jnp.float32,
        )
    out_ref[...] = total[:, 0:LANES] + total[:, LANES : 2 * LANES] + total[:, 2 * LANES :]


def sensor_weights(cells, weights, planes, width):
    targets = planes * width
    return pl.pallas_call(
        functools.partial(sensor_kernel, 0, planes, width),
        out_shape=jax.ShapeDtypeStruct((targets, LANES), jnp.float32),
        compiler_params=pltpu.CompilerParams(vmem_limit_bytes=32 << 20),
        name="sensors",
    )(cells[None], weights[None])


def body(
    directions,
    eigen_basis,
    flow_first,
    flow_second,
    flow_depth,
    face_codes,
    sensor_cells,
    sensor_weight,
):
    planes = directions.shape[1]
    slab_count = lax.axis_size("slab")
    top_faces = from_behind(flow_depth[-1:], "slab", 1)
    depth_below = jnp.concatenate([top_faces, flow_depth[:-1]], 0)
    first_below = lower_along(flow_first, 1)
    second_below = lower_along(flow_second, 2)
    flows = (flow_first, first_below, flow_second, second_below, flow_depth, depth_below)
    diagonal = diagonal_of(flows, face_codes)

    def solve(rhs, adjoint):
        iterate = rhs
        for repeat in range(SWEEPS):
            padded = extended(iterate, (("slab", 1),), 1)
            iterate = (rhs + neighbor_sum(padded, flows, adjoint)) / diagonal
        return iterate

    rank = eigen_basis.shape[0]
    dirs, _, width, _ = directions.shape
    basis = eigen_basis.reshape(rank, planes * width, LANES)
    gram = spread(gram_parts(basis, slab_count), slab_count)
    gram = jnp.sum(gram.reshape(slab_count, rank, LANES), 0)[:, :rank]
    factor_lower = jnp.linalg.cholesky(gram)
    inverse = lax.linalg.triangular_solve(
        factor_lower, jnp.eye(rank, dtype=jnp.float32), left_side=True, lower=True
    )
    cell_weight = sensor_weights(sensor_cells, sensor_weight, planes, width)
    state = jnp.zeros_like(directions)
    for moment in range(STEPS):
        state = solve(state + directions, False)
    forcing = state * cell_weight.reshape(state.shape[1:])[None]
    adjoint_state = forcing
    summed = jnp.zeros_like(directions)
    for moment in range(STEPS):
        adjoint_state = solve(adjoint_state, True)
        summed = summed + adjoint_state
    image = (summed + GAMMA * directions).reshape(dirs, planes * width, LANES)
    parts = spread(projection_parts(basis, image, slab_count), slab_count)
    rem, coeffs, parts = remainders(parts, inverse, basis, image, slab_count)
    total_cells = planes * slab_count * width * LANES
    new_directions = scaled(spread(parts, slab_count), rem, total_cells, slab_count)
    return (new_directions.reshape(directions.shape), coeffs)


def solution(mesh):
    return jax.shard_map(
        body,
        mesh=mesh,
        in_specs=(
            P("grp", "slab", None, None),
            P("grp", "slab", None, None),
            P("slab", None, None),
            P("slab", None, None),
            P("slab", None, None),
            P(),
            P(("grp", "slab")),
            P(("grp", "slab")),
        ),
        out_specs=(P("grp", "slab", None, None), P("grp", None)),
        check_vma=False,
    )
```

```python
import functools
import math

import jax
import jax.numpy as jnp
from jax import lax
from jax.experimental import pallas as pl
from jax.experimental.pallas import tpu as pltpu
from jax.sharding import PartitionSpec as P

STEPS = 2
SWEEPS = 3
GROUPS = 2


DIFFUSION = 0.2
GAMMA = 0.5

LANES = 128
EXACT = lax.Precision.HIGHEST


def lane_sums(stack):
    ones = jnp.ones((8, LANES), jnp.float32)
    return lax.dot_general(
        ones, stack, (((1,), (1,)), ((), ())), precision=EXACT, preferred_element_type=jnp.float32
    )


def gram_kernel(basis_ref, out_ref, acc_ref):
    rank = basis_ref.shape[0]
    rows = basis_ref.shape[1]
    step = pl.program_id(0)
    tile = 4

    @pl.when(step == 0)
    def _():
        acc_ref[...] = jnp.zeros_like(acc_ref)

    for i0 in range(0, rank, tile):
        for j0 in range(i0, rank, tile):
            pairs = [(i, j) for i in range(i0, i0 + tile) for j in range(j0, j0 + tile) if i <= j]

            def add(k, sums, i0=i0, j0=j0, pairs=pairs):
                at = pl.ds(pl.multiple_of(k * 8, 8), 8)
                left = {i: basis_ref[i, at, :] for i in range(i0, i0 + tile)}
                right = left if i0 == j0 else {j: basis_ref[j, at, :] for j in range(j0, j0 + tile)}
                return [s + left[i] * right[j] for s, (i, j) in zip(sums, pairs)]

            sums = [jnp.zeros((8, LANES), jnp.float32) for _ in pairs]
            sums = lax.fori_loop(0, rows // 8, add, sums, unroll=4)
            for (i, j), s in zip(pairs, sums):
                acc_ref[i, j] += s

    @pl.when(step == pl.num_programs(0) - 1)
    def _():
        row = lax.broadcasted_iota(jnp.int32, (rank, rank), 0)
        col = lax.broadcasted_iota(jnp.int32, (rank, rank), 1)
        gram = jnp.zeros((rank, rank), jnp.float32)
        for i in range(rank):
            sums = lane_sums(jnp.sum(acc_ref[i], axis=1))
            gram = jnp.where(row == i, jnp.broadcast_to(sums[0:1, :], (rank, rank)), gram)
        upper = jnp.where(col >= row, gram, 0.0)
        strict = jnp.where(col > row, gram, 0.0)
        whole = upper + strict.T
        for r in range(out_ref.shape[0] // 8):
            for k in range(0, rank, 8):
                out_ref[r * 8 : (r + 1) * 8, k * rank // 8 : (k + 8) * rank // 8] = whole[k : k + 8]


def gram_parts(basis, count):
    rank, rows, _ = basis.shape
    chunk = 128
    return pl.pallas_call(
        gram_kernel,
        grid=(rows // chunk,),
        in_specs=[pl.BlockSpec((rank, chunk, LANES), lambda k: (0, k, 0))],
        out_specs=pl.BlockSpec((count * 8, LANES), lambda k: (0, 0)),
        out_shape=jax.ShapeDtypeStruct((count * 8, LANES), jnp.float32),
        scratch_shapes=[pltpu.VMEM((rank, rank, 8, LANES), jnp.float32)],
        compiler_params=pltpu.CompilerParams(vmem_limit_bytes=16 << 20),
        cost_estimate=pl.CostEstimate(
            flops=rank * rank * rows * LANES, bytes_accessed=rank * rows * LANES * 4, transcendentals=0
        ),
        name="gram",
    )(basis)


def spread(tile, count):
    return lax.all_to_all(tile, "slab", 0, 0, tiled=True) if count > 1 else tile


def projection_kernel(groups, where_ref, basis_ref, dirs_ref, *refs):
    halves, (out_ref, image_ref, acc_ref) = refs[: 2 * groups], refs[2 * groups :]
    rank = basis_ref.shape[0]
    dirs, rows, _ = image_ref.shape
    step = pl.program_id(0)
    tile = 8
    each = dirs // groups

    @pl.when(step == 0)
    def _():
        acc_ref[...] = jnp.zeros_like(acc_ref)

    for side in range(2):

        @pl.when((step < pl.num_programs(0) // 2) == (side == 0))
        def _(side=side):
            for d in range(dirs):
                image_ref[d] = halves[2 * (d // each) + side][d % each, 0] + GAMMA * dirs_ref[d]

    for i0 in range(0, rank, tile):

        def add(k, sums, i0=i0):
            at = pl.ds(pl.multiple_of(k * 8, 8), 8)
            image = [image_ref[d, at, :] for d in range(dirs)]
            out = []
            for i in range(tile):
                q = basis_ref[i0 + i, at, :]
                out += [sums[i * dirs + d] + q * image[d] for d in range(dirs)]
            return out

        sums = [jnp.zeros((8, LANES), jnp.float32) for _ in range(tile * dirs)]
        sums = lax.fori_loop(0, rows // 8, add, sums, unroll=4)
        for i in range(tile):
            for d in range(dirs):
                acc_ref[d, i0 + i] += sums[i * dirs + d]

    @pl.when(step == pl.num_programs(0) - 1)
    def _():
        row = lax.broadcasted_iota(jnp.int32, (8, rank), 0)
        table = jnp.zeros((8, rank), jnp.float32)
        for d in range(dirs):
            table = jnp.where(row == d, lane_sums(jnp.sum(acc_ref[d], axis=1)), table)
        for r in range(out_ref.shape[0] // 8):
            out_ref[r * 8 : (r + 1) * 8, 0:rank] = table


def projection_parts(where, basis, directions, returned, count):
    rank, rows, _ = basis.shape
    dirs, planes, width, _ = directions.shape
    half = width // 2
    groups = len(returned)

    def line(k, where_ref):
        part = jnp.where(k < planes, where_ref[1], 1 - where_ref[1])
        return (0, 2 * lax.rem(k, planes) + part, 0)

    def side(which):
        def index(k, where_ref):
            at = jnp.minimum(k, planes - 1) if which == 0 else jnp.maximum(k - planes, 0)
            return (0, at, 0, 0)

        return pl.BlockSpec((dirs // groups, 1, half, LANES), index)

    return pl.pallas_call(
        functools.partial(projection_kernel, groups),
        grid_spec=pltpu.PrefetchScalarGridSpec(
            num_scalar_prefetch=1,
            grid=(2 * planes,),
            in_specs=[
                pl.BlockSpec((rank, half, LANES), line),
                pl.BlockSpec((dirs, half, LANES), line),
            ]
            + [side(which) for _ in returned for which in range(2)],
            out_specs=[
                pl.BlockSpec((count * 8, LANES), lambda k, where_ref: (0, 0)),
                pl.BlockSpec((dirs, half, LANES), line),
            ],
            scratch_shapes=[pltpu.VMEM((dirs, rank, 8, LANES), jnp.float32)],
        ),
        out_shape=[
            jax.ShapeDtypeStruct((count * 8, LANES), jnp.float32),
            jax.ShapeDtypeStruct((dirs, rows, LANES), jnp.float32),
        ],
        compiler_params=pltpu.CompilerParams(vmem_limit_bytes=16 << 20),
        cost_estimate=pl.CostEstimate(
            flops=2 * rank * dirs * rows * LANES,
            bytes_accessed=(rank + 3 * dirs) * rows * LANES * 4,
            transcendentals=0,
        ),
        name="projections",
    )(where, basis, directions.reshape(dirs, rows, LANES), *[h for pair in returned for h in pair])


def summed_tile(parts_ref):
    total = parts_ref[0:8, :]
    for r in range(1, parts_ref.shape[0] // 8):
        total = total + parts_ref[r * 8 : (r + 1) * 8, :]
    return total


def remainder_kernel(
    parts_ref, inverse_ref, basis_ref, image_ref, rem_ref, coeffs_ref, out_ref, splat_ref, energy_ref
):
    rank = basis_ref.shape[0]
    dirs, rows, _ = image_ref.shape
    step = pl.program_id(0)
    tile = 4

    @pl.when(step == 0)
    def _():
        table = summed_tile(parts_ref)[:, 0:rank]
        inverse = inverse_ref[...]
        half = lax.dot_general(
            table, inverse, (((1,), (1,)), ((), ())), precision=EXACT,
            preferred_element_type=jnp.float32,
        )
        flat = lax.dot_general(
            half, inverse, (((1,), (0,)), ((), ())), precision=EXACT,
            preferred_element_type=jnp.float32,
        )
        coeffs_ref[...] = flat.T[:, 0:dirs]
        for d in range(dirs):
            for j in range(rank):
                splat_ref[d * rank + j] = jnp.broadcast_to(flat[d : d + 1, j : j + 1], (8, LANES))
        energy_ref[...] = jnp.zeros_like(energy_ref)

    for j0 in range(0, rank, tile):
        last = j0 + tile == rank
        weights = [[splat_ref[d * rank + j] for j in range(j0, j0 + tile)] for d in range(dirs)]

        def take(k, energy, j0=j0, last=last, weights=weights):
            at = pl.ds(pl.multiple_of(k * 8, 8), 8)
            basis = [basis_ref[j, at, :] for j in range(j0, j0 + tile)]
            out = []
            for d in range(dirs):
                left = image_ref[d, at, :] if j0 == 0 else rem_ref[d, at, :]
                parts = [w * q for w, q in zip(weights[d], basis)]
                left = left - ((parts[0] + parts[1]) + (parts[2] + parts[3]))
                rem_ref[d, at, :] = left
                out.append(energy[d] + left * left if last else energy[d])
            return out

        energy = [jnp.zeros((8, LANES), jnp.float32) for _ in range(dirs)]
        energy = lax.fori_loop(0, rows // 8, take, energy, unroll=4)
        if last:
            for d in range(dirs):
                energy_ref[d] += energy[d]

    @pl.when(step == pl.num_programs(0) - 1)
    def _():
        row = lax.broadcasted_iota(jnp.int32, (8, LANES), 0)
        tile_out = jnp.zeros((8, LANES), jnp.float32)
        for d in range(dirs):
            total = jnp.sum(jnp.sum(energy_ref[d], axis=0, keepdims=True), axis=1, keepdims=True)
            tile_out = jnp.where(row == d, jnp.broadcast_to(total, (8, LANES)), tile_out)
        for r in range(out_ref.shape[0] // 8):
            out_ref[r * 8 : (r + 1) * 8, :] = tile_out


def remainders(parts, inverse, basis, image, count):
    rank, rows, _ = basis.shape
    dirs = image.shape[0]
    chunk = 128
    whole = lambda *shape: pl.BlockSpec(shape, lambda k: (0,) * len(shape))
    return pl.pallas_call(
        remainder_kernel,
        grid=(rows // chunk,),
        in_specs=[
            whole(count * 8, LANES),
            whole(rank, rank),
            pl.BlockSpec((rank, chunk, LANES), lambda k: (0, k, 0)),
            pl.BlockSpec((dirs, chunk, LANES), lambda k: (0, k, 0)),
        ],
        out_specs=[
            pl.BlockSpec((dirs, chunk, LANES), lambda k: (0, k, 0)),
            whole(rank, dirs),
            whole(count * 8, LANES),
        ],
        out_shape=[
            jax.ShapeDtypeStruct((dirs, rows, LANES), jnp.float32),
            jax.ShapeDtypeStruct((rank, dirs), jnp.float32),
            jax.ShapeDtypeStruct((count * 8, LANES), jnp.float32),
        ],
        scratch_shapes=[
            pltpu.VMEM((dirs * rank, 8, LANES), jnp.float32),
            pltpu.VMEM((dirs, 8, LANES), jnp.float32),
        ],
        compiler_params=pltpu.CompilerParams(vmem_limit_bytes=16 << 20),
        cost_estimate=pl.CostEstimate(
            flops=2 * rank * dirs * rows * LANES,
            bytes_accessed=(rank + 2 * dirs) * rows * LANES * 4,
            transcendentals=0,
        ),
        name="remainder",
    )(parts, inverse, basis, image)


def scale_kernel(cells, parts_ref, rem_ref, new_ref):
    energy = summed_tile(parts_ref)
    value = energy / cells + 1e-06
    root = lax.rsqrt(value)
    root = root * (1.5 - (0.5 * value * root) * root)
    for d in range(rem_ref.shape[0]):
        new_ref[d] = rem_ref[d] * root[d : d + 1, :]


def scaled(parts, rem, cells, count):
    dirs, rows, _ = rem.shape
    chunk = 256
    return pl.pallas_call(
        functools.partial(scale_kernel, cells),
        grid=(rows // chunk,),
        in_specs=[
            pl.BlockSpec((count * 8, LANES), lambda k: (0, 0)),
            pl.BlockSpec((dirs, chunk, LANES), lambda k: (0, k, 0)),
        ],
        out_specs=pl.BlockSpec((dirs, chunk, LANES), lambda k: (0, k, 0)),
        out_shape=jax.ShapeDtypeStruct((dirs, rows, LANES), jnp.float32),
        compiler_params=pltpu.CompilerParams(vmem_limit_bytes=16 << 20),
        name="scale",
    )(parts, rem)


SPARE = 16
REACH = STEPS * SWEEPS
PAD = 8


def quad(count):
    own, other, above = [], [], []
    for s in range(count):
        q, a, b = s // 4, s // 2 % 2, s % 2
        own.append((s, 4 * q + 2 * b + a))
        other.append((s, 4 * q + 2 * (1 - b) + a))
        up = s + 1 if b == 0 else s + 3
        if up < count:
            above.append((s, up))
    return own, other, above


def back(pairs):
    return [(target, source) for source, target in pairs]


def cut_kernel(where_ref, *refs):
    sources, own_ref, other_ref = refs[:-2], refs[-2], refs[-1]
    height = own_ref.shape[2]
    width = sources[0].shape[-2]
    b = where_ref[1]
    for ref, part in ((own_ref, b), (other_ref, 1 - b)):
        start = pl.multiple_of(part * (width - height), 16)
        k = 0
        for source in sources:
            if len(source.shape) == 3:
                ref[k] = source[:, pl.ds(start, height), :]
                k += 1
            else:
                for d in range(source.shape[0]):
                    ref[k] = source[d, :, pl.ds(start, height), :]
                    k += 1


SMEM = pl.BlockSpec(memory_space=pltpu.SMEM)
VMEM = pl.BlockSpec(memory_space=pltpu.VMEM)


def call(kernel, name, ins, outs, scratch=(), limit=20, flops=0):
    moved = sum(x.size * 4 for x in ins[1:]) + sum(4 * math.prod(s) for s in outs)
    return pl.pallas_call(
        kernel,
        in_specs=[SMEM] + [VMEM] * (len(ins) - 1),
        out_specs=[VMEM] * len(outs),
        out_shape=[jax.ShapeDtypeStruct(s, jnp.float32) for s in outs],
        scratch_shapes=list(scratch),
        compiler_params=pltpu.CompilerParams(vmem_limit_bytes=limit << 20),
        cost_estimate=pl.CostEstimate(flops=flops, bytes_accessed=moved, transcendentals=0),
        name=name,
    )(*ins)


def pack_kernel(where_ref, own_ref, other_ref, up_ref, down_ref):
    planes = own_ref.shape[1]
    reach = up_ref.shape[1]
    skip = 2 * planes - reach

    def join(first, second):
        up_ref[:, 0 : planes - skip] = first[:, skip:]
        up_ref[:, planes - skip :] = second[...]
        down_ref[:, 0:planes] = first[...]
        down_ref[:, planes:] = second[:, 0 : reach - planes]

    @pl.when(where_ref[0] == 0)
    def _():
        join(own_ref, other_ref)

    @pl.when(where_ref[0] == 1)
    def _():
        join(other_ref, own_ref)


def sensor_kernel(width, where_ref, own_ref, other_ref, out_ref):
    a = where_ref[0]
    _, planes, height, _ = out_ref.shape
    first = a * (width - height)
    sensors = own_ref.shape[1]
    chunk = 512
    targets = planes * height
    rows = lax.broadcasted_iota(jnp.int32, (targets, chunk), 0)
    lanes = lax.broadcasted_iota(jnp.int32, (LANES, chunk), 0)
    for ref, at in ((own_ref, a), (other_ref, 1 - a)):
        total = jnp.zeros((targets, 3 * LANES), jnp.float32)
        for k in range(sensors // chunk):
            cell = ref[0:1, k * chunk : (k + 1) * chunk].astype(jnp.int32)
            weight = ref[1:2, k * chunk : (k + 1) * chunk]
            line = cell // LANES
            lane = cell - line * LANES
            plane = line // width
            row = line - plane * width - first
            inside = (row >= 0) & (row < height)
            target = jnp.where(inside, plane * height + row, -1)
            high = weight.astype(jnp.bfloat16).astype(jnp.float32)
            rest = weight - high
            middle = rest.astype(jnp.bfloat16).astype(jnp.float32)
            low = rest - middle
            hot = jnp.where(rows == target, 1.0, 0.0).astype(jnp.bfloat16)
            here = lanes == lane
            parts = [jnp.where(here, part, 0.0).astype(jnp.bfloat16) for part in (high, middle, low)]
            total += lax.dot_general(
                hot,
                jnp.concatenate(parts, 0),
                (((1,), (1,)), ((), ())),
                preferred_element_type=jnp.float32,
            )
        total = total[:, 0:LANES] + total[:, LANES : 2 * LANES] + total[:, 2 * LANES :]
        out_ref[at] = total.reshape(planes, height, LANES)


def relu(x):
    return jnp.maximum(x, 0.0)


def solve_kernel(adjoint, width, where_ref, f_up, f_down, f_lo, f_hi, v_up, v_down, v_lo, v_hi, *refs):
    if adjoint:
        first_out, second_out, flow, coef, rhs, start, ping, pong = refs
        weight_ref = None
    else:
        weight_ref, up_out, down_out, flow, coef, rhs, start, ping, pong = refs
    dirs, reach, height, _ = v_up.shape
    depth = rhs.shape[1]
    own = depth - 2 * reach
    chunks = height // 8
    a, at_bottom, at_top = where_ref[0], where_ref[2], where_ref[3]
    code = [where_ref[4 + k] for k in range(4)]

    def gather(into, up, down, lo, hi, rows):
        into[:, 0:reach, rows, :] = lo[...]
        into[:, reach : 2 * reach, rows, :] = down[...]
        into[:, 2 * reach : reach + own, rows, :] = up[:, 2 * reach - own :]
        into[:, reach + own :, rows, :] = hi[...]

    gather(flow, f_up, f_down, f_lo, f_hi, pl.ds(0, height))
    gather(start, v_up, v_down, v_lo, v_hi, pl.ds(PAD, height))
    for ref in (start, ping, pong):
        for d in range(dirs):
            for p in range(depth):
                ref[d, p, 0:PAD, :] = jnp.zeros((PAD, LANES), jnp.float32)
                ref[d, p, PAD + height :, :] = jnp.zeros((PAD, LANES), jnp.float32)

    shape = (height, LANES)
    row = lax.broadcasted_iota(jnp.int32, shape, 0) + a * (width - height)
    lane = lax.broadcasted_iota(jnp.int32, shape, 1)
    opened = [jnp.where(c == 0, 1.0, 0.0).astype(jnp.float32) for c in code]
    low_one = jnp.where(row == 0, opened[0], 1.0)
    high_one = jnp.where(row == width - 1, opened[1], 1.0)
    low_two = jnp.where(lane == 0, opened[2], 1.0)
    high_two = jnp.where(lane == LANES - 1, opened[3], 1.0)

    def coefficients(p, carry):
        one, two, three = flow[0, p], flow[1, p], flow[2, p]
        one_below = jnp.where(row == 0, 0.0, pltpu.roll(one, 1, 0))
        two_below = jnp.where(lane == 0, 0.0, pltpu.roll(two, 1, 1))
        three_below = flow[2, p - 1]
        up = [DIFFUSION + relu(x) for x in (one, two, three)]
        down = [DIFFUSION + relu(-x) for x in (one_below, two_below, three_below)]
        diagonal = 1.0 + high_one * up[0] + low_one * down[0] + high_two * up[1]
        diagonal = diagonal + low_two * down[1] + up[2] + down[2]
        outside = ((p < reach) & (at_bottom == 1)) | ((p >= reach + own) & (at_top == 1))
        inverse = jnp.where(outside, 0.0, 1.0) / diagonal
        if not adjoint:
            up = [DIFFUSION + relu(-x) for x in (one, two, three)]
            down = [DIFFUSION + relu(x) for x in (one_below, two_below, three_below)]
        coef[0, p] = up[0] * inverse
        coef[1, p] = down[0] * inverse
        coef[2, p] = jnp.where(lane == LANES - 1, 0.0, up[1] * inverse)
        coef[3, p] = jnp.where(lane == 0, 0.0, down[1] * inverse)
        coef[4, p] = up[2] * inverse
        coef[5, p] = down[2] * inverse
        coef[6, p] = inverse
        return carry

    lax.fori_loop(1, depth - 1, coefficients, 0)

    def sweep(source, lead, planes, offset, count, store):
        def at_plane(p, carry):
            for r in range(count):
                here = pl.ds(offset + r * 8, 8)
                c = [coef[k, p, here, :] for k in range(7 if lead else 6)]
                base = offset + PAD + r * 8
                for d in range(dirs):
                    value = source[d, p, pl.ds(base, 8), :]
                    if lead:
                        total = value * c[6]
                        rhs[d, p, here, :] = total
                    else:
                        total = rhs[d, p, here, :]
                    total = total + c[0] * source[d, p, pl.ds(base + 1, 8), :]
                    total = total + c[1] * source[d, p, pl.ds(base - 1, 8), :]
                    total = total + c[2] * pltpu.roll(value, LANES - 1, 1)
                    total = total + c[3] * pltpu.roll(value, 1, 1)
                    total = total + c[4] * source[d, p + 1, pl.ds(base, 8), :]
                    total = total + c[5] * source[d, p - 1, pl.ds(base, 8), :]
                    store(d, p, base, r, total)
            return carry

        for low, high in planes:
            lax.fori_loop(low, high, at_plane, 0)

    def into(ref):
        def store(d, p, base, r, total):
            ref[d, p, pl.ds(base, 8), :] = total

        return store

    def again(d, p, base, r, total):
        if not adjoint:
            total = total + start[d, p, pl.ds(base, 8), :]
        start[d, p, pl.ds(base, 8), :] = total

    def full(source, lead, step, store):
        sweep(source, lead, [(1 + step, depth - 1 - step)], 0, chunks, store)

    full(start, True, 0, into(ping))
    full(ping, False, 1, into(pong))
    full(pong, False, 2, again)
    full(start, True, 3, into(ping))
    full(ping, False, 4, into(pong))

    if adjoint:
        kept = 2 * (height - SPARE) // 2 // 8
        half = own // 2
        shift = pl.multiple_of(a * SPARE, 8)
        for out, side in ((first_out, a), (second_out, 1 - a)):
            low = reach + side * half

            def finish(d, p, base, r, total, out=out, low=low):
                out[d, p - low, r * 8 : r * 8 + 8, :] = total + start[d, p, pl.ds(base, 8), :]

            sweep(pong, False, [(low, low + half)], shift, kept, finish)
    else:

        def emit(kinds):
            def finish(d, p, base, r, total):
                i = p - reach
                total = total * weight_ref[i // (own // 2), i % (own // 2), r * 8 : r * 8 + 8, :]
                if "d" in kinds:
                    down_out[d, i, r * 8 : r * 8 + 8, :] = total
                if "u" in kinds:
                    up_out[d, i - (own - reach), r * 8 : r * 8 + 8, :] = total

            return finish

        for low, high, kinds in ((0, own - reach, "d"), (own - reach, reach, "du"), (reach, own, "u")):
            sweep(pong, False, [(reach + low, reach + high)], 0, chunks, emit(kinds))


def solves(adjoint, width, where, flows, values, weight=None):
    dirs, reach, height, _ = values[0].shape
    blocks = 2 * (where[1])
    depth = blocks + 2 * reach
    ins = [where[0], *flows, *values]
    if adjoint:
        outs = [(dirs, blocks // 2, height - SPARE, LANES)] * 2
    else:
        ins.append(weight)
        outs = [values[0].shape] * 2
    padded = (dirs, depth, height + 2 * PAD, LANES)
    scratch = [
        pltpu.VMEM((3, depth, height, LANES), jnp.float32),
        pltpu.VMEM((7, depth, height, LANES), jnp.float32),
        pltpu.VMEM((dirs, depth, height, LANES), jnp.float32),
    ] + [pltpu.VMEM(padded, jnp.float32)] * 3
    name = "adjoint" if adjoint else "forward"
    return call(
        functools.partial(solve_kernel, adjoint, width), name, ins, outs, scratch, 48,
        flops=6 * 14 * dirs * depth * height * LANES,
    )


def body(
    directions,
    eigen_basis,
    flow_first,
    flow_second,
    flow_depth,
    face_codes,
    sensor_cells,
    sensor_weight,
):
    dirs, planes, width, _ = directions.shape
    rank = eigen_basis.shape[0]
    count = lax.axis_size("slab")
    height = width // 2 + SPARE
    own, other, above = quad(count)
    me = lax.axis_index("slab")
    a, b = me // 2 % 2, me % 2
    place = [a, b, (me - 2 * a == 0), (me + 2 * (1 - a) == count - 1)]
    where = jnp.concatenate([jnp.stack([x.astype(jnp.int32) for x in place]), face_codes])
    both = (where, planes)

    def regroup(first, second):
        return lax.ppermute(first, "slab", own), lax.ppermute(second, "slab", other)

    def cut(arrays, parts):
        return call(cut_kernel, "cut", [where, *arrays], [(parts, planes, height, LANES)] * 2)

    def beyond(up, down):
        return up, down, lax.ppermute(up, "slab", above), lax.ppermute(down, "slab", back(above))

    def pack(pair):
        shape = (pair[0].shape[0], REACH, height, LANES)
        return call(pack_kernel, "pack", [where, *pair], [shape] * 2)

    flows = regroup(*cut([flow_first, flow_second, flow_depth], 3))
    groups = [directions[k : k + dirs // GROUPS] for k in range(0, dirs, dirs // GROUPS)]
    moved = [regroup(*cut([g], dirs // GROUPS)) for g in groups]
    sensors = jnp.stack([sensor_cells.astype(jnp.float32), sensor_weight])
    sensors = regroup(sensors, sensors)

    basis = eigen_basis.reshape(rank, planes * width, LANES)
    gram = spread(gram_parts(basis, count), count)
    gram = jnp.sum(gram.reshape(count, 8, LANES), 0)
    gram = jnp.concatenate([gram[:, k : k + rank] for k in range(0, rank * rank // 8, rank)], 0)
    factor_lower = jnp.linalg.cholesky(gram)
    inverse = lax.linalg.triangular_solve(
        factor_lower, jnp.eye(rank, dtype=jnp.float32), left_side=True, lower=True
    )
    (weight,) = call(
        functools.partial(sensor_kernel, width), "sensors", [where, *sensors],
        [(2, planes, height, LANES)], limit=32,
    )
    flows = beyond(*pack(flows))
    values = [beyond(*pack(m)) for m in moved]
    forcing = [beyond(*solves(False, width, both, flows, v, weight)) for v in values]
    summed = [solves(True, width, both, flows, f) for f in forcing]
    returned = [
        (lax.ppermute(s[0], "slab", back(own)), lax.ppermute(s[1], "slab", back(other)))
        for s in summed
    ]
    parts, image = projection_parts(where, basis, directions, returned, count)
    parts = spread(parts, count)
    rem, coeffs, parts = remainders(parts, inverse, basis, image, count)
    new_directions = scaled(spread(parts, count), rem, planes * count * width * LANES, count)
    return (new_directions.reshape(directions.shape), coeffs)


def solution(mesh):
    return jax.shard_map(
        body,
        mesh=mesh,
        in_specs=(
            P("grp", "slab", None, None),
            P("grp", "slab", None, None),
            P("slab", None, None),
            P("slab", None, None),
            P("slab", None, None),
            P(),
            P(("grp", "slab")),
            P(("grp", "slab")),
        ),
        out_specs=(P("grp", "slab", None, None), P("grp", None)),
        check_vma=False,
    )
```

```python
import functools

import jax
import jax.numpy as jnp
from jax import lax
from jax.experimental import pallas as pl
from jax.experimental.pallas import tpu as pltpu
from jax.sharding import PartitionSpec as P

STEPS = 2
SWEEPS = 3
GROUPS = 2
SPARE = 16
REACH = STEPS * SWEEPS


DIFFUSION = 0.2
GAMMA = 0.5
LANES = 128
EXACT = lax.Precision.HIGHEST
SMEM = pl.BlockSpec(memory_space=pltpu.SMEM)
VMEM = pl.BlockSpec(memory_space=pltpu.VMEM)
ANY = pl.BlockSpec(memory_space=pl.ANY)
VECTOR = 150


def floats(*shape):
    return jax.ShapeDtypeStruct(shape, jnp.float32)


def cost(flops, moved):
    return pl.CostEstimate(flops=int(flops), bytes_accessed=int(moved), transcendentals=0)


def lane_sums(stack):
    ones = jnp.ones((8, LANES), jnp.float32)
    return lax.dot_general(
        ones, stack, (((1,), (1,)), ((), ())), precision=EXACT, preferred_element_type=jnp.float32
    )


def gram_kernel(where_ref, basis_ref, out_ref, where_out, acc_ref):
    rank = basis_ref.shape[0]
    rows = basis_ref.shape[1]
    step = pl.program_id(0)
    tile = 4

    @pl.when(step == 0)
    def _():
        acc_ref[...] = jnp.zeros_like(acc_ref)
        for k in range(where_ref.shape[0]):
            where_out[k] = where_ref[k]

    for i0 in range(0, rank, tile):
        for j0 in range(i0, rank, tile):
            pairs = [(i, j) for i in range(i0, i0 + tile) for j in range(j0, j0 + tile) if i <= j]

            def add(k, sums, i0=i0, j0=j0, pairs=pairs):
                at = pl.ds(pl.multiple_of(k * 8, 8), 8)
                left = {i: basis_ref[i, at, :] for i in range(i0, i0 + tile)}
                right = left if i0 == j0 else {j: basis_ref[j, at, :] for j in range(j0, j0 + tile)}
                return [s + left[i] * right[j] for s, (i, j) in zip(sums, pairs)]

            sums = [jnp.zeros((8, LANES), jnp.float32) for _ in pairs]
            sums = lax.fori_loop(0, rows // 8, add, sums, unroll=8)
            for (i, j), s in zip(pairs, sums):
                acc_ref[i, j] += s

    @pl.when(step == pl.num_programs(0) - 1)
    def _():
        row = lax.broadcasted_iota(jnp.int32, (rank, rank), 0)
        col = lax.broadcasted_iota(jnp.int32, (rank, rank), 1)
        gram = jnp.zeros((rank, rank), jnp.float32)
        for i in range(rank):
            sums = lane_sums(jnp.sum(acc_ref[i], axis=1))
            gram = jnp.where(row == i, jnp.broadcast_to(sums[0:1, :], (rank, rank)), gram)
        upper = jnp.where(col >= row, gram, 0.0)
        strict = jnp.where(col > row, gram, 0.0)
        whole = upper + strict.T
        out_ref[...] = jnp.zeros_like(out_ref)
        for k in range(0, rank, 8):
            at = rank + k * rank // 8
            out_ref[:, at : at + rank] = whole[k : k + 8]


def gram_tile(where, basis):
    rank, rows, _ = basis.shape
    chunk = 128
    return pl.pallas_call(
        gram_kernel,
        grid=(rows // chunk,),
        in_specs=[SMEM, pl.BlockSpec((rank, chunk, LANES), lambda k: (0, k, 0))],
        out_specs=[pl.BlockSpec((8, LANES), lambda k: (0, 0)), SMEM],
        out_shape=[floats(8, LANES), jax.ShapeDtypeStruct(where.shape, where.dtype)],
        scratch_shapes=[pltpu.VMEM((rank, rank, 8, LANES), jnp.float32)],
        compiler_params=pltpu.CompilerParams(vmem_limit_bytes=16 << 20),
        cost_estimate=cost(VECTOR * rank * rank * rows * LANES, rank * rows * LANES * 4),
        name="gram",
    )(where, basis)


def spread(tile, count):
    return lax.all_to_all(tile, "slab", 0, 0, tiled=True) if count > 1 else tile


def projection_kernel(dirs, first, last, where_ref, basis_ref, dirs_ref, own_ref, other_ref, tile_ref, out_ref, image_ref, acc_ref):
    rank = basis_ref.shape[0]
    rows = image_ref.shape[1]
    step = pl.program_id(0)
    tile = 8

    @pl.when(step == 0)
    def _():
        acc_ref[...] = jnp.zeros_like(acc_ref)

    for side, ref in enumerate((own_ref, other_ref)):

        @pl.when((step < pl.num_programs(0) // 2) == (side == 0))
        def _(ref=ref):
            for d in range(dirs):
                image_ref[d] = ref[d, 0] + GAMMA * dirs_ref[d]

    for i0 in range(0, rank, tile):

        def add(k, sums, i0=i0):
            at = pl.ds(pl.multiple_of(k * 8, 8), 8)
            image = [image_ref[d, at, :] for d in range(dirs)]
            out = []
            for i in range(tile):
                q = basis_ref[i0 + i, at, :]
                out += [sums[i * dirs + d] + q * image[d] for d in range(dirs)]
            return out

        sums = [jnp.zeros((8, LANES), jnp.float32) for _ in range(tile * dirs)]
        sums = lax.fori_loop(0, rows // 8, add, sums, unroll=8)
        for i in range(tile):
            for d in range(dirs):
                acc_ref[d, i0 + i] += sums[i * dirs + d]

    @pl.when(step == pl.num_programs(0) - 1)
    def _():
        row = lax.broadcasted_iota(jnp.int32, (8, LANES), 0)
        lane = lax.broadcasted_iota(jnp.int32, (8, LANES), 1)
        table = tile_ref[...]
        for d in range(dirs):
            sums = jnp.sum(acc_ref[d], axis=1)
            sums = jnp.concatenate([sums, jnp.zeros((LANES - rank, LANES), jnp.float32)], 0)
            table = jnp.where((row == first + d) & (lane < rank), lane_sums(sums), table)
        for r in range(out_ref.shape[0] // 8):
            out_ref[r * 8 : (r + 1) * 8, :] = table


def projections(where, basis, directions, first, halves, tile, count):
    rank, rows, _ = basis.shape
    _, planes, width, _ = directions.shape
    dirs = halves[0].shape[0]
    half = width // 2

    def line(k, where_ref):
        part = jnp.where(k < planes, where_ref[1], 1 - where_ref[1])
        return 2 * lax.rem(k, planes) + part

    def side(which):
        def index(k, where_ref):
            return (0, jnp.minimum(k, planes - 1) if which == 0 else jnp.maximum(k - planes, 0), 0, 0)

        return pl.BlockSpec((dirs, 1, half, LANES), index)

    return pl.pallas_call(
        functools.partial(projection_kernel, dirs, first, count > 1),
        grid_spec=pltpu.PrefetchScalarGridSpec(
            num_scalar_prefetch=1,
            grid=(2 * planes,),
            in_specs=[
                pl.BlockSpec((rank, half, LANES), lambda k, w: (0, line(k, w), 0)),
                pl.BlockSpec((dirs, half, LANES), lambda k, w: (first // dirs, line(k, w), 0)),
                side(0),
                side(1),
                pl.BlockSpec((8, LANES), lambda k, w: (0, 0)),
            ],
            out_specs=[
                pl.BlockSpec((count * 8, LANES), lambda k, w: (0, 0)),
                pl.BlockSpec((dirs, half, LANES), lambda k, w: (0, line(k, w), 0)),
            ],
            scratch_shapes=[pltpu.VMEM((dirs, rank, 8, LANES), jnp.float32)],
        ),
        out_shape=[floats(count * 8, LANES), floats(dirs, rows, LANES)],
        compiler_params=pltpu.CompilerParams(vmem_limit_bytes=52 << 20),
        cost_estimate=cost(
            VECTOR * 2 * rank * dirs * rows * LANES, (rank + 3 * dirs) * rows * LANES * 4
        ),
        name="projections",
    )(where, basis, directions.reshape(-1, rows, LANES), *halves, tile)


def summed_tile(parts_ref):
    tiles = [parts_ref[r : r + 8, :] for r in range(0, parts_ref.shape[0], 8)]
    while len(tiles) > 1:
        tiles = [sum(tiles[k : k + 2]) for k in range(0, len(tiles), 2)]
    return tiles[0]


def solved(tile, rank):
    gram = [tile[:, rank + k * rank // 8 :][:, :rank] for k in range(0, rank, 8)]
    table = jnp.concatenate(
        [
            jnp.concatenate(gram, 0),
            tile[:, 0:rank].T,
            jnp.zeros((rank, LANES - rank - 8), jnp.float32),
        ],
        1,
    )
    row = lax.broadcasted_iota(jnp.int32, (rank, LANES), 0)
    for k in range(rank):
        scaled_row = table[k : k + 1, :] / table[k : k + 1, k : k + 1]
        table = jnp.where(row == k, scaled_row, table - table[:, k : k + 1] * scaled_row)
    return table


def remainder_kernel(dirs, parts_ref, basis_ref, *refs):
    groups = len(refs) - 5
    images, (rem_ref, coeffs_ref, out_ref, splat_ref, energy_ref) = refs[:groups], refs[groups:]
    each = dirs // groups
    rank = basis_ref.shape[0]
    rows = rem_ref.shape[1]
    step = pl.program_id(0)
    tile = 4

    @pl.when(step == 0)
    def _():
        table = solved(summed_tile(parts_ref), rank)
        coeffs_ref[...] = table[:, rank : rank + dirs]
        for d in range(dirs):
            for j in range(rank):
                splat_ref[d * rank + j] = jnp.broadcast_to(
                    table[j : j + 1, rank + d : rank + d + 1], (8, LANES)
                )
        energy_ref[...] = jnp.zeros_like(energy_ref)

    for j0 in range(0, rank, tile):
        last = j0 + tile == rank
        weights = [[splat_ref[d * rank + j] for j in range(j0, j0 + tile)] for d in range(dirs)]

        def take(k, energy, j0=j0, last=last, weights=weights):
            at = pl.ds(pl.multiple_of(k * 8, 8), 8)
            basis = [basis_ref[j, at, :] for j in range(j0, j0 + tile)]
            out = []
            for d in range(dirs):
                left = images[d // each][d % each, at, :] if j0 == 0 else rem_ref[d, at, :]
                parts = [w * q for w, q in zip(weights[d], basis)]
                left = left - ((parts[0] + parts[1]) + (parts[2] + parts[3]))
                rem_ref[d, at, :] = left
                out.append(energy[d] + left * left if last else energy[d])
            return out

        energy = [jnp.zeros((8, LANES), jnp.float32) for _ in range(dirs)]
        energy = lax.fori_loop(0, rows // 8, take, energy, unroll=4)
        if last:
            for d in range(dirs):
                energy_ref[d] += energy[d]

    @pl.when(step == pl.num_programs(0) - 1)
    def _():
        row = lax.broadcasted_iota(jnp.int32, (8, LANES), 0)
        tile_out = jnp.zeros((8, LANES), jnp.float32)
        for d in range(dirs):
            total = jnp.sum(jnp.sum(energy_ref[d], axis=0, keepdims=True), axis=1, keepdims=True)
            tile_out = jnp.where(row == d, jnp.broadcast_to(total, (8, LANES)), tile_out)
        for r in range(out_ref.shape[0] // 8):
            out_ref[r * 8 : (r + 1) * 8, :] = tile_out


def remainders(parts, basis, images, count):
    rank, rows, _ = basis.shape
    dirs = sum(i.shape[0] for i in images)
    chunk = 128
    whole = lambda *shape: pl.BlockSpec(shape, lambda k: (0,) * len(shape))
    line = lambda n: pl.BlockSpec((n, chunk, LANES), lambda k: (0, k, 0))
    return pl.pallas_call(
        functools.partial(remainder_kernel, dirs),
        grid=(rows // chunk,),
        in_specs=[whole(count * 8, LANES), line(rank)] + [line(i.shape[0]) for i in images],
        out_specs=[line(dirs), whole(rank, dirs), whole(count * 8, LANES)],
        out_shape=[floats(dirs, rows, LANES), floats(rank, dirs), floats(count * 8, LANES)],
        scratch_shapes=[
            pltpu.VMEM((dirs * rank, 8, LANES), jnp.float32),
            pltpu.VMEM((dirs, 8, LANES), jnp.float32),
        ],
        compiler_params=pltpu.CompilerParams(vmem_limit_bytes=52 << 20),
        cost_estimate=cost(
            VECTOR * 2 * rank * dirs * rows * LANES, (rank + 2 * dirs) * rows * LANES * 4
        ),
        name="remainder",
    )(parts, basis, *images)


def scale_kernel(cells, parts_ref, rem_ref, new_ref):
    energy = summed_tile(parts_ref)
    value = energy / cells + 1e-06
    root = lax.rsqrt(value)
    root = root * (1.5 - (0.5 * value * root) * root)
    for d in range(rem_ref.shape[0]):
        new_ref[d] = rem_ref[d] * root[d : d + 1, :]


def scaled(parts, rem, cells, count):
    dirs, rows, _ = rem.shape
    chunk = 256
    return pl.pallas_call(
        functools.partial(scale_kernel, cells),
        grid=(rows // chunk,),
        in_specs=[
            pl.BlockSpec((count * 8, LANES), lambda k: (0, 0)),
            pl.BlockSpec((dirs, chunk, LANES), lambda k: (0, k, 0)),
        ],
        out_specs=pl.BlockSpec((dirs, chunk, LANES), lambda k: (0, k, 0)),
        out_shape=floats(dirs, rows, LANES),
        compiler_params=pltpu.CompilerParams(vmem_limit_bytes=16 << 20),
        name="scale",
    )(parts, rem)


def quad(count):
    own, other, above = [], [], []
    for s in range(count):
        q, a, b = s // 4, s // 2 % 2, s % 2
        own.append((s, 4 * q + 2 * b + a))
        other.append((s, 4 * q + 2 * (1 - b) + a))
        up = s + 1 if b == 0 else s + 3
        if up < count:
            above.append((s, up))
    return own, other, above


def back(pairs):
    return [(target, source) for source, target in pairs]


def call(kernel, name, ins, outs, scratch=(), limit=16, work=0, specs=None, grid=()):
    moved = sum(x.size * 4 for x in ins[1:]) + sum(o.size * 4 for o in outs)
    return pl.pallas_call(
        kernel,
        grid=grid,
        in_specs=[SMEM] + (specs or [VMEM] * (len(ins) - 1)),
        out_specs=[VMEM] * len(outs),
        out_shape=outs,
        scratch_shapes=list(scratch),
        compiler_params=pltpu.CompilerParams(vmem_limit_bytes=limit << 20),
        cost_estimate=cost(VECTOR * work, moved),
        name=name,
    )(*ins)


def cut_kernel(height, where_ref, *refs):
    sources, own_ref, other_ref = refs[:-2], refs[-2], refs[-1]
    b = where_ref[1]
    for ref, part in ((own_ref, b), (other_ref, 1 - b)):
        k = 0
        for source in sources:
            if len(source.shape) == 2:
                rows = source.shape[0]
                ref[k : k + rows, :] = source[...].astype(jnp.float32)
                k += rows
                continue
            start = pl.multiple_of(part * (source.shape[-2] - height), 16)
            for d in range(source.shape[0] if len(source.shape) == 4 else 1):
                block = source.at[d] if len(source.shape) == 4 else source
                for p in range(block.shape[0]):
                    ref[k : k + height, :] = block[p, pl.ds(start, height), :]
                    k += height


def pack_kernel(planes, where_ref, own_ref, other_ref, up_ref, down_ref):
    count, reach, height, _ = up_ref.shape
    skip = 2 * planes - reach

    def join(first, second):
        for d in range(count):
            for p in range(2 * planes):
                ref = first if p < planes else second
                at = (d * planes + p % planes) * height
                value = ref[at : at + height, :]
                if p >= skip:
                    up_ref[d, p - skip] = value
                if p < reach:
                    down_ref[d, p] = value

    @pl.when(where_ref[0] == 0)
    def _():
        join(own_ref, other_ref)

    @pl.when(where_ref[0] == 1)
    def _():
        join(other_ref, own_ref)


def sensor_kernel(width, skip, where_ref, own_ref, other_ref, out_ref):
    a = where_ref[0]
    _, planes, height, _ = out_ref.shape
    first = a * (width - height)
    count = (own_ref.shape[0] - skip) // 2
    group = 4
    chunk = group * LANES
    targets = planes * height
    rows = lax.broadcasted_iota(jnp.int32, (targets, chunk), 0)
    lanes = lax.broadcasted_iota(jnp.int32, (LANES, chunk), 0)
    for ref, at in ((own_ref, a), (other_ref, 1 - a)):
        total = jnp.zeros((targets, 3 * LANES), jnp.float32)
        for k in range(skip, skip + count, group):
            take = lambda at: jnp.concatenate([ref[at + g : at + g + 1, :] for g in range(group)], 1)
            cell = take(k).astype(jnp.int32)
            weight = take(count + k)
            line = cell // LANES
            lane = cell - line * LANES
            plane = line // width
            row = line - plane * width - first
            inside = (row >= 0) & (row < height)
            target = jnp.where(inside, plane * height + row, -1)
            high = weight.astype(jnp.bfloat16).astype(jnp.float32)
            rest = weight - high
            middle = rest.astype(jnp.bfloat16).astype(jnp.float32)
            low = rest - middle
            hot = jnp.where(rows == target, 1.0, 0.0).astype(jnp.bfloat16)
            here = lanes == lane
            parts = [jnp.where(here, part, 0.0).astype(jnp.bfloat16) for part in (high, middle, low)]
            total += lax.dot_general(
                hot,
                jnp.concatenate(parts, 0),
                (((1,), (1,)), ((), ())),
                preferred_element_type=jnp.float32,
            )
        total = total[:, 0:LANES] + total[:, LANES : 2 * LANES] + total[:, 2 * LANES :]
        out_ref[at] = total.reshape(planes, height, LANES)


def solve_kernel(adjoint, width, where_ref, *refs):
    flow_parts, value_parts = refs[0:4], refs[4:8]
    if adjoint:
        outs, (flow, coef, rhs, start, ping, pong, sems) = refs[8:10], refs[10:]
    else:
        weight_ref, outs, (flow, coef, rhs, start, ping, pong, sems) = refs[8], refs[9:11], refs[11:]
    dirs, depth, height, _ = rhs.shape
    reach = REACH
    own = depth - 2 * reach
    chunks = height // 8
    a, at_bottom, at_top = where_ref[0], where_ref[2], where_ref[3]
    code = [where_ref[4 + k] for k in range(4)]

    def arrivals(parts, into, first):
        up, down, lo, hi = parts
        moves = (
            (lo, into.at[:, 0:reach]),
            (down, into.at[:, reach : 2 * reach]),
            (up.at[:, 2 * reach - own : reach], into.at[:, 2 * reach : reach + own]),
            (hi, into.at[:, reach + own : depth]),
        )
        return [pltpu.make_async_copy(s, t, sems.at[first + k]) for k, (s, t) in enumerate(moves)]

    flow_moves = arrivals(flow_parts, flow, 0)
    value_moves = arrivals(value_parts, start, 4)
    for move in flow_moves + value_moves:
        move.start()

    shape = (8, LANES)
    sub = lax.broadcasted_iota(jnp.int32, shape, 0)
    lane = lax.broadcasted_iota(jnp.int32, shape, 1)
    top_sub, bottom_sub = sub == 7, sub == 0
    last_lane, first_lane = lane == LANES - 1, lane == 0
    zero = jnp.zeros(shape, jnp.float32)
    opened = [jnp.where(c == 0, 1.0, 0.0).astype(jnp.float32) for c in code]
    low_one = jnp.where(bottom_sub & (a == 0), opened[0], 1.0)
    high_one = jnp.where(top_sub & (a == 1), opened[1], 1.0)
    low_two = jnp.where(first_lane, opened[2], 1.0)
    high_two = jnp.where(last_lane, opened[3], 1.0)

    def both(x):
        positive = DIFFUSION + jnp.maximum(x, 0.0)
        return positive, positive - x

    def coefficients(p, carry):
        outside = ((p < reach) & (at_bottom == 1)) | ((p >= reach + own) & (at_top == 1))
        inside = jnp.where(outside, 0.0, 1.0)
        turned = zero
        for r in range(chunks):
            here = slice(r * 8, r * 8 + 8)
            one, two, three = flow[0, p, here, :], flow[1, p, here, :], flow[2, p, here, :]
            one_turned = pltpu.roll(one, 1, 0)
            one_below = jnp.where(bottom_sub, turned, one_turned)
            turned = one_turned
            two_below = jnp.where(first_lane, 0.0, pltpu.roll(two, 1, 1))
            up = [both(x) for x in (one, two, three)]
            down = [both(x) for x in (one_below, two_below, flow[2, p - 1, here, :])]
            first = up[0][0] if r < chunks - 1 else high_one * up[0][0]
            second = down[0][1] if r > 0 else low_one * down[0][1]
            diagonal = (1.0 + first) + (second + high_two * up[1][0])
            diagonal = diagonal + (low_two * down[1][1] + (up[2][0] + down[2][1]))
            inverse = inside / diagonal
            which = 0 if adjoint else 1
            coef[0, p, here, :] = up[0][which] * inverse
            coef[1, p, here, :] = down[0][1 - which] * inverse
            coef[2, p, here, :] = jnp.where(last_lane, 0.0, up[1][which] * inverse)
            coef[3, p, here, :] = jnp.where(first_lane, 0.0, down[1][1 - which] * inverse)
            coef[4, p, here, :] = up[2][which] * inverse
            coef[5, p, here, :] = down[2][1 - which] * inverse
            coef[6, p, here, :] = inverse
        return carry

    for move in flow_moves:
        move.wait()
    lax.fori_loop(1, depth - 1, coefficients, 0)
    for move in value_moves:
        move.wait()

    def sweep(source, lead, low, high, offset, count, store):
        def rows(r):
            return pl.ds(offset + r * 8, 8)

        def at_plane(p, carry):
            value = [source[d, p, rows(0), :] for d in range(dirs)]
            up = [pltpu.roll(v, 7, 0) for v in value]
            down = [pltpu.roll(v, 1, 0) for v in value]
            before = [zero] * dirs
            if count < chunks:
                for d in range(dirs):
                    outer = source[d, p, pl.ds(pl.multiple_of(jnp.maximum(offset - 8, 0), 8), 8), :]
                    before[d] = jnp.where(a == 0, 0.0, pltpu.roll(outer, 1, 0))
            for r in range(count):
                c = [coef[k, p, rows(r), :] for k in range(7 if lead else 6)]
                for d in range(dirs):
                    if r + 1 < count:
                        following = source[d, p, rows(r + 1), :]
                        next_up, next_down = pltpu.roll(following, 7, 0), pltpu.roll(following, 1, 0)
                    elif count < chunks:
                        at = pl.multiple_of(jnp.minimum(offset + count * 8, height - 8), 8)
                        following = source[d, p, pl.ds(at, 8), :]
                        next_up, next_down = jnp.where(a == 1, 0.0, pltpu.roll(following, 7, 0)), zero
                    else:
                        following, next_up, next_down = zero, zero, zero
                    if lead:
                        total = value[d] * c[6]
                        rhs[d, p, rows(r), :] = total
                    else:
                        total = rhs[d, p, rows(r), :]
                    total = total + c[4] * source[d, p + 1, rows(r), :]
                    total = total + c[5] * source[d, p - 1, rows(r), :]
                    total = total + c[0] * jnp.where(top_sub, next_up, up[d])
                    total = total + c[1] * jnp.where(bottom_sub, before[d], down[d])
                    total = total + c[2] * pltpu.roll(value[d], LANES - 1, 1)
                    total = total + c[3] * pltpu.roll(value[d], 1, 1)
                    store(d, p, rows(r), r, total)
                    value[d], up[d], before[d], down[d] = following, next_up, down[d], next_down
            return carry

        lax.fori_loop(low, high, at_plane, 0)

    def into(ref):
        def store(d, p, here, r, total):
            ref[d, p, here, :] = total

        return store

    def again(d, p, here, r, total):
        start[d, p, here, :] = total if adjoint else total + start[d, p, here, :]

    def full(source, lead, step, store):
        sweep(source, lead, 1 + step, depth - 1 - step, 0, chunks, store)

    full(start, True, 0, into(ping))
    full(ping, False, 1, into(pong))
    full(pong, False, 2, again)
    full(start, True, 3, into(ping))
    full(ping, False, 4, into(pong))

    half = own // 2
    if adjoint:
        for out, side in zip(outs, (a, 1 - a)):
            low = reach + side * half

            def finish(d, p, here, r, total, out=out, low=low):
                out[d, p - low, r * 8 : r * 8 + 8, :] = total + start[d, p, here, :]

            shift = pl.multiple_of(a * SPARE, 8)
            sweep(pong, False, low, low + half, shift, (height - SPARE) // 8, finish)
    else:
        up_out, down_out = outs

        def emit(kinds):
            def finish(d, p, here, r, total):
                i = p - reach
                total = total * weight_ref[i // half, i % half, here, :]
                if "d" in kinds:
                    down_out[d, i, here, :] = total
                if "u" in kinds:
                    up_out[d, i - (own - reach), here, :] = total

            return finish

        for low, high, kinds in ((0, own - reach, "d"), (own - reach, reach, "du"), (reach, own, "u")):
            sweep(pong, False, reach + low, reach + high, 0, chunks, emit(kinds))


def solves(adjoint, width, where, planes, flows, values, weight=None):
    dirs, reach, height, _ = values[0].shape
    depth = 2 * planes + 2 * reach
    ins = [where, *flows, *values]
    specs = [ANY] * 8
    if adjoint:
        outs = [floats(dirs, planes, height - SPARE, LANES)] * 2
    else:
        ins.append(weight)
        specs.append(VMEM)
        outs = [floats(*values[0].shape)] * 2
    scratch = [pltpu.VMEM((n, depth, height, LANES), jnp.float32) for n in (3, 7) + (dirs,) * 4]
    scratch.append(pltpu.SemaphoreType.DMA((8,)))
    return call(
        functools.partial(solve_kernel, adjoint, width),
        "adjoint" if adjoint else "forward",
        ins, outs, scratch, 36, 6 * 20 * dirs * depth * height * LANES, specs,
    )


def body(
    directions,
    eigen_basis,
    flow_first,
    flow_second,
    flow_depth,
    face_codes,
    sensor_cells,
    sensor_weight,
):
    dirs, planes, width, _ = directions.shape
    rank = eigen_basis.shape[0]
    count = lax.axis_size("slab")
    height = width // 2 + SPARE
    own, other, above = quad(count)
    me = lax.axis_index("slab")
    a, b = me // 2 % 2, me % 2
    place = [a, b, (me - 2 * a == 0), (me + 2 * (1 - a) == count - 1)]
    where = jnp.concatenate([jnp.stack([x.astype(jnp.int32) for x in place]), face_codes])
    each = dirs // GROUPS

    def regroup(first, second):
        return lax.ppermute(first, "slab", own), lax.ppermute(second, "slab", other)

    def cut(arrays, rows, group=None):
        specs, grid = [VMEM] * len(arrays), ()
        if group is not None:
            arrays, specs = [directions, *arrays], [group_of(group), *specs]
            grid = (1,)
        outs = [floats(rows, LANES)] * 2
        return call(functools.partial(cut_kernel, height), "cut", [where, *arrays], outs, specs=specs, grid=grid)

    def group_of(k):
        return pl.BlockSpec((each, planes, width, LANES), lambda _: (k, 0, 0, 0))

    def beyond(up, down):
        return up, down, lax.ppermute(up, "slab", above), lax.ppermute(down, "slab", back(above))

    def pack(scalars, pair, parts):
        outs = [floats(parts, REACH, height, LANES)] * 2
        return call(functools.partial(pack_kernel, planes), "pack", [scalars, *pair], outs)

    sensors = [x.reshape(-1, LANES) for x in (sensor_cells, sensor_weight)]
    listed = 2 * sensors[0].shape[0]
    block = planes * height
    flows = regroup(*cut([flow_first, flow_second, flow_depth], 3 * block))
    moved = [regroup(*cut(sensors, each * block + listed, 0))]
    moved += [regroup(*cut([], each * block, k)) for k in range(1, GROUPS)]

    basis = eigen_basis.reshape(rank, planes * width, LANES)
    tile, later = gram_tile(where, basis)
    flows = beyond(*pack(later, flows, 3))
    (weight,) = call(
        functools.partial(sensor_kernel, width, each * block), "sensors",
        [later, *moved[0]], [floats(2, planes, height, LANES)], work=planes * height * listed * 20,
    )
    values = [beyond(*pack(later, m, each)) for m in moved]
    forcing = [beyond(*solves(False, width, where, planes, flows, v, weight)) for v in values]
    summed = [solves(True, width, where, planes, flows, f) for f in forcing]
    returned = [
        (lax.ppermute(s[0], "slab", back(own)), lax.ppermute(s[1], "slab", back(other)))
        for s in summed
    ]
    images = []
    for k, halves in enumerate(returned):
        copies = count if k == GROUPS - 1 else 1
        tile, image = projections(where, basis, directions, k * each, halves, tile, copies)
        images.append(image)
    rem, coeffs, parts = remainders(spread(tile, count), basis, images, count)
    new_directions = scaled(spread(parts, count), rem, planes * count * width * LANES, count)
    return (new_directions.reshape(directions.shape), coeffs)


def solution(mesh):
    return jax.shard_map(
        body,
        mesh=mesh,
        in_specs=(
            P("grp", "slab", None, None),
            P("grp", "slab", None, None),
            P("slab", None, None),
            P("slab", None, None),
            P("slab", None, None),
            P(),
            P(("grp", "slab")),
            P(("grp", "slab")),
        ),
        out_specs=(P("grp", "slab", None, None), P("grp", None)),
        check_vma=False,
    )
```

```python
import functools

import jax
import jax.numpy as jnp
from jax import lax
from jax.experimental import pallas as pl
from jax.experimental.pallas import tpu as pltpu
from jax.sharding import PartitionSpec as P

STEPS = 2
SWEEPS = 3
GROUPS = 2
SPARE = 16
REACH = STEPS * SWEEPS


DIFFUSION = 0.2
GAMMA = 0.5
LANES = 128
PIECES = 8
EXACT = lax.Precision.HIGHEST
SMEM = pl.BlockSpec(memory_space=pltpu.SMEM)
VMEM = pl.BlockSpec(memory_space=pltpu.VMEM)
ANY = pl.BlockSpec(memory_space=pl.ANY)
VECTOR = 150


def floats(*shape):
    return jax.ShapeDtypeStruct(shape, jnp.float32)


def cost(flops, moved):
    return pl.CostEstimate(flops=int(flops), bytes_accessed=int(moved), transcendentals=0)


def lane_sums(stack):
    ones = jnp.ones((8, LANES), jnp.float32)
    return lax.dot_general(
        ones, stack, (((1,), (1,)), ((), ())), precision=EXACT, preferred_element_type=jnp.float32
    )


def chunks_of(source, into, sems, pieces):
    rows = source.shape[1] // pieces
    return [
        pltpu.make_async_copy(
            source.at[:, pl.ds(k * rows, rows)], into.at[:, pl.ds(k * rows, rows)], sems.at[k]
        )
        for k in range(pieces)
    ]


def gram_kernel(where_ref, basis_hbm, out_ref, where_out, basis_ref, acc_ref, sems):
    rank, rows, _ = basis_ref.shape
    tile = 4
    moves = chunks_of(basis_hbm, basis_ref, sems, PIECES)
    for move in moves:
        move.start()
    for k in range(where_ref.shape[0]):
        where_out[k] = where_ref[k]
    acc_ref[...] = jnp.zeros_like(acc_ref)
    part = rows // PIECES
    for piece, move in enumerate(moves):
        move.wait()
        for i0 in range(0, rank, tile):
            for j0 in range(i0, rank, tile):
                pairs = [(i, j) for i in range(i0, i0 + tile) for j in range(j0, j0 + tile) if i <= j]

                def add(k, sums, i0=i0, j0=j0, pairs=pairs, piece=piece):
                    at = pl.ds(pl.multiple_of(piece * part + k * 8, 8), 8)
                    left = {i: basis_ref[i, at, :] for i in range(i0, i0 + tile)}
                    right = left if i0 == j0 else {j: basis_ref[j, at, :] for j in range(j0, j0 + tile)}
                    return [s + left[i] * right[j] for s, (i, j) in zip(sums, pairs)]

                sums = [jnp.zeros((8, LANES), jnp.float32) for _ in pairs]
                sums = lax.fori_loop(0, part // 8, add, sums, unroll=8)
                for (i, j), s in zip(pairs, sums):
                    acc_ref[i, j] += s

    row = lax.broadcasted_iota(jnp.int32, (rank, rank), 0)
    col = lax.broadcasted_iota(jnp.int32, (rank, rank), 1)
    gram = jnp.zeros((rank, rank), jnp.float32)
    for i in range(rank):
        sums = lane_sums(jnp.sum(acc_ref[i], axis=1))
        gram = jnp.where(row == i, jnp.broadcast_to(sums[0:1, :], (rank, rank)), gram)
    upper = jnp.where(col >= row, gram, 0.0)
    strict = jnp.where(col > row, gram, 0.0)
    whole = upper + strict.T
    out_ref[...] = jnp.zeros_like(out_ref)
    for k in range(0, rank, 8):
        at = rank + k * rank // 8
        out_ref[:, at : at + rank] = whole[k : k + 8]


def gram_tile(where, basis):
    rank, rows, _ = basis.shape
    return call(
        gram_kernel, "gram", [where, basis],
        [floats(8, LANES), jax.ShapeDtypeStruct(where.shape, where.dtype)],
        [
            pltpu.VMEM(basis.shape, jnp.float32),
            pltpu.VMEM((rank, rank, 8, LANES), jnp.float32),
            pltpu.SemaphoreType.DMA((PIECES,)),
        ],
        54, rank * rank * rows * LANES, [ANY], [VMEM, SMEM],
    )


def spread(tile, count):
    return lax.all_to_all(tile, "slab", 0, 0, tiled=True) if count > 1 else tile


def projection_kernel(
    first, where_ref, basis_hbm, dirs_hbm, own_hbm, other_hbm, tile_ref,
    out_ref, image_ref, basis_ref, dirs_ref, halves_ref, sems, side_sems,
):
    rank = basis_ref.shape[0]
    dirs, rows, _ = image_ref.shape
    planes, half = halves_ref.shape[2:4]
    b = where_ref[1]
    sides = [
        pltpu.make_async_copy(own_hbm, halves_ref.at[0], side_sems.at[0]),
        pltpu.make_async_copy(other_hbm, halves_ref.at[1], side_sems.at[1]),
        pltpu.make_async_copy(dirs_hbm.at[pl.ds(first, dirs)], dirs_ref, side_sems.at[2]),
    ]
    moves = chunks_of(basis_hbm, basis_ref, sems, PIECES)
    for move in sides + moves:
        move.start()
    for move in sides:
        move.wait()
    sums = [jnp.zeros((8, LANES), jnp.float32) for _ in range(rank * dirs)]
    for k in range(2 * planes):
        plane, part = k // 2, k % 2
        which = jnp.where(b == part, 0, 1)
        low = k * half
        piece = rows // PIECES
        for m in range(low // piece, -(-(low + half) // piece)):
            if m * piece >= low:
                moves[m].wait()

        def add(r, sums, plane=plane, which=which, low=low):
            at = pl.ds(pl.multiple_of(low + r * 8, 8), 8)
            here = pl.ds(pl.multiple_of(r * 8, 8), 8)
            image = []
            for d in range(dirs):
                value = halves_ref[which, d, plane, here, :] + GAMMA * dirs_ref[d, at, :]
                image_ref[d, at, :] = value
                image.append(value)
            out = []
            for i in range(rank):
                q = basis_ref[i, at, :]
                out += [sums[i * dirs + d] + q * image[d] for d in range(dirs)]
            return out

        sums = lax.fori_loop(0, half // 8, add, sums, unroll=4)

    row = lax.broadcasted_iota(jnp.int32, (8, LANES), 0)
    lane = lax.broadcasted_iota(jnp.int32, (8, LANES), 1)
    table = tile_ref[...]
    for d in range(dirs):
        lines = [jnp.sum(sums[i * dirs + d], axis=0, keepdims=True) for i in range(rank)]
        lines = jnp.concatenate(lines + [jnp.zeros((LANES - rank, LANES), jnp.float32)], 0)
        table = jnp.where((row == first + d) & (lane < rank), lane_sums(lines), table)
    for r in range(out_ref.shape[0] // 8):
        out_ref[r * 8 : (r + 1) * 8, :] = table


def projections(where, basis, directions, first, halves, tile, count):
    rank, rows, _ = basis.shape
    dirs = halves[0].shape[0]
    return call(
        functools.partial(projection_kernel, first), "projections",
        [where, basis, directions.reshape(-1, rows, LANES), *halves, tile],
        [floats(count * 8, LANES), floats(dirs, rows, LANES)],
        [
            pltpu.VMEM(basis.shape, jnp.float32),
            pltpu.VMEM((dirs, rows, LANES), jnp.float32),
            pltpu.VMEM((2, *halves[0].shape), jnp.float32),
            pltpu.SemaphoreType.DMA((PIECES,)),
            pltpu.SemaphoreType.DMA((3,)),
        ],
        52, 2 * rank * dirs * rows * LANES, [ANY] * 4 + [VMEM],
    )


def summed_tile(parts_ref):
    tiles = [parts_ref[r : r + 8, :] for r in range(0, parts_ref.shape[0], 8)]
    while len(tiles) > 1:
        tiles = [sum(tiles[k : k + 2]) for k in range(0, len(tiles), 2)]
    return tiles[0]


def solved(tile, rank):
    gram = [tile[:, rank + k * rank // 8 :][:, :rank] for k in range(0, rank, 8)]
    table = jnp.concatenate(
        [
            jnp.concatenate(gram, 0),
            tile[:, 0:rank].T,
            jnp.zeros((rank, LANES - rank - 8), jnp.float32),
        ],
        1,
    )
    row = lax.broadcasted_iota(jnp.int32, (rank, LANES), 0)
    for k in range(rank):
        scaled_row = table[k : k + 1, :] / table[k : k + 1, k : k + 1]
        table = jnp.where(row == k, scaled_row, table - table[:, k : k + 1] * scaled_row)
    return table


def remainder_kernel(dirs, parts_ref, basis_hbm, *refs):
    groups = len(refs) - 8
    images, (rem_ref, coeffs_ref, out_ref, basis_ref, image_ref, splat_ref, sems, side_sems) = (
        refs[:groups], refs[groups:]
    )
    each = dirs // groups
    rank, rows, _ = basis_ref.shape
    tile = 4
    sides = [
        pltpu.make_async_copy(image, image_ref.at[pl.ds(k * each, each)], side_sems.at[k])
        for k, image in enumerate(images)
    ]
    moves = chunks_of(basis_hbm, basis_ref, sems, PIECES)
    for move in sides + moves:
        move.start()
    table = solved(summed_tile(parts_ref), rank)
    coeffs_ref[...] = table[:, rank : rank + dirs]
    for d in range(dirs):
        for j in range(rank):
            splat_ref[d * rank + j] = jnp.broadcast_to(
                table[j : j + 1, rank + d : rank + d + 1], (8, LANES)
            )
    for move in sides:
        move.wait()
    energy = [jnp.zeros((8, LANES), jnp.float32) for _ in range(dirs)]
    part = rows // PIECES
    for piece, move in enumerate(moves):
        move.wait()
        for j0 in range(0, rank, tile):
            last = j0 + tile == rank
            weights = [[splat_ref[d * rank + j] for j in range(j0, j0 + tile)] for d in range(dirs)]

            def take(k, energy, j0=j0, last=last, weights=weights, piece=piece):
                at = pl.ds(pl.multiple_of(piece * part + k * 8, 8), 8)
                basis = [basis_ref[j, at, :] for j in range(j0, j0 + tile)]
                out = []
                for d in range(dirs):
                    left = image_ref[d, at, :] if j0 == 0 else rem_ref[d, at, :]
                    parts = [w * q for w, q in zip(weights[d], basis)]
                    left = left - ((parts[0] + parts[1]) + (parts[2] + parts[3]))
                    rem_ref[d, at, :] = left
                    out.append(energy[d] + left * left if last else energy[d])
                return out

            energy = lax.fori_loop(0, part // 8, take, energy, unroll=4)

    row = lax.broadcasted_iota(jnp.int32, (8, LANES), 0)
    tile_out = jnp.zeros((8, LANES), jnp.float32)
    for d in range(dirs):
        total = jnp.sum(jnp.sum(energy[d], axis=0, keepdims=True), axis=1, keepdims=True)
        tile_out = jnp.where(row == d, jnp.broadcast_to(total, (8, LANES)), tile_out)
    for r in range(out_ref.shape[0] // 8):
        out_ref[r * 8 : (r + 1) * 8, :] = tile_out


def remainders(parts, basis, images, count):
    rank, rows, _ = basis.shape
    dirs = sum(i.shape[0] for i in images)
    return call(
        functools.partial(remainder_kernel, dirs), "remainder", [parts, basis, *images],
        [floats(dirs, rows, LANES), floats(rank, dirs), floats(count * 8, LANES)],
        [
            pltpu.VMEM(basis.shape, jnp.float32),
            pltpu.VMEM((dirs, rows, LANES), jnp.float32),
            pltpu.VMEM((dirs * rank, 8, LANES), jnp.float32),
            pltpu.SemaphoreType.DMA((PIECES,)),
            pltpu.SemaphoreType.DMA((len(images),)),
        ],
        52, 2 * rank * dirs * rows * LANES, [ANY] * (1 + len(images)), first=VMEM,
    )


def scale_kernel(cells, parts_ref, rem_ref, new_ref):
    energy = summed_tile(parts_ref)
    value = energy / cells + 1e-06
    root = lax.rsqrt(value)
    root = root * (1.5 - (0.5 * value * root) * root)
    for d in range(rem_ref.shape[0]):
        new_ref[d] = rem_ref[d] * root[d : d + 1, :]


def scaled(parts, rem, cells, count):
    dirs, rows, _ = rem.shape
    chunk = 256
    return pl.pallas_call(
        functools.partial(scale_kernel, cells),
        grid=(rows // chunk,),
        in_specs=[
            pl.BlockSpec((count * 8, LANES), lambda k: (0, 0)),
            pl.BlockSpec((dirs, chunk, LANES), lambda k: (0, k, 0)),
        ],
        out_specs=pl.BlockSpec((dirs, chunk, LANES), lambda k: (0, k, 0)),
        out_shape=floats(dirs, rows, LANES),
        compiler_params=pltpu.CompilerParams(vmem_limit_bytes=16 << 20),
        name="scale",
    )(parts, rem)


def quad(count):
    own, other, above = [], [], []
    for s in range(count):
        q, a, b = s // 4, s // 2 % 2, s % 2
        own.append((s, 4 * q + 2 * b + a))
        other.append((s, 4 * q + 2 * (1 - b) + a))
        up = s + 1 if b == 0 else s + 3
        if up < count:
            above.append((s, up))
    return own, other, above


def back(pairs):
    return [(target, source) for source, target in pairs]


def call(kernel, name, ins, outs, scratch=(), limit=16, work=0, specs=None, out_specs=None, first=SMEM):
    moved = sum(x.size * 4 for x in ins[1:]) + sum(o.size * 4 for o in outs)
    return pl.pallas_call(
        kernel,
        in_specs=[first] + (specs or [VMEM] * (len(ins) - 1)),
        out_specs=out_specs or [VMEM] * len(outs),
        out_shape=outs,
        scratch_shapes=list(scratch),
        compiler_params=pltpu.CompilerParams(vmem_limit_bytes=limit << 20),
        cost_estimate=cost(VECTOR * work, moved),
        name=name,
    )(*ins)


def cut_kernel(height, group, listed, where_ref, *refs):
    lists, fields = refs[:listed], refs[listed:-4]
    own_ref, other_ref, list_ref, sems = refs[-4:]
    b = where_ref[1]
    moves = []

    def move(source, target):
        moves.append(pltpu.make_async_copy(source, target, sems.at[len(moves)]))
        moves[-1].start()

    k = 0
    for field in fields:
        start = pl.multiple_of(b * (field.shape[-2] - height), 16)
        rest = pl.multiple_of((1 - b) * (field.shape[-2] - height), 16)
        for d in group:
            for p in range(field.shape[-3]):
                at = (p,) if len(field.shape) == 3 else (d, p)
                for ref, low in ((own_ref, start), (other_ref, rest)):
                    move(field.at[(*at, pl.ds(low, height))], ref.at[pl.ds(k, height)])
                k += height
    low = 0
    for entries in lists:
        list_ref[low : low + entries.shape[0], :] = entries[...].astype(jnp.float32)
        low += entries.shape[0]
    if lists:
        for ref in (own_ref, other_ref):
            move(list_ref, ref.at[pl.ds(k, low)])
    for m in moves:
        m.wait()


def pack_kernel(planes, where_ref, own_ref, other_ref, up_ref, down_ref):
    count, reach, height, _ = up_ref.shape
    skip = 2 * planes - reach

    def join(first, second):
        for d in range(count):
            for p in range(2 * planes):
                ref = first if p < planes else second
                at = (d * planes + p % planes) * height
                value = ref[at : at + height, :]
                if p >= skip:
                    up_ref[d, p - skip] = value
                if p < reach:
                    down_ref[d, p] = value

    @pl.when(where_ref[0] == 0)
    def _():
        join(own_ref, other_ref)

    @pl.when(where_ref[0] == 1)
    def _():
        join(other_ref, own_ref)


def sensor_kernel(width, skip, where_ref, own_ref, other_ref, out_ref, where_out):
    for k in range(where_ref.shape[0]):
        where_out[k] = where_ref[k]
    a = where_ref[0]
    _, planes, height, _ = out_ref.shape
    first = a * (width - height)
    count = (own_ref.shape[0] - skip) // 2
    group = 4
    chunk = group * LANES
    targets = planes * height
    rows = lax.broadcasted_iota(jnp.int32, (targets, chunk), 0)
    lanes = lax.broadcasted_iota(jnp.int32, (LANES, chunk), 0)
    for ref, at in ((own_ref, a), (other_ref, 1 - a)):
        total = jnp.zeros((targets, 3 * LANES), jnp.float32)
        for k in range(skip, skip + count, group):
            take = lambda at: jnp.concatenate([ref[at + g : at + g + 1, :] for g in range(group)], 1)
            cell = take(k).astype(jnp.int32)
            weight = take(count + k)
            line = cell // LANES
            lane = cell - line * LANES
            plane = line // width
            row = line - plane * width - first
            inside = (row >= 0) & (row < height)
            target = jnp.where(inside, plane * height + row, -1)
            high = weight.astype(jnp.bfloat16).astype(jnp.float32)
            rest = weight - high
            middle = rest.astype(jnp.bfloat16).astype(jnp.float32)
            low = rest - middle
            hot = jnp.where(rows == target, 1.0, 0.0).astype(jnp.bfloat16)
            here = lanes == lane
            parts = [jnp.where(here, part, 0.0).astype(jnp.bfloat16) for part in (high, middle, low)]
            total += lax.dot_general(
                hot,
                jnp.concatenate(parts, 0),
                (((1,), (1,)), ((), ())),
                preferred_element_type=jnp.float32,
            )
        total = total[:, 0:LANES] + total[:, LANES : 2 * LANES] + total[:, 2 * LANES :]
        out_ref[at] = total.reshape(planes, height, LANES)


def solve_kernel(adjoint, width, where_ref, *refs):
    flow_parts, value_parts = refs[0:4], refs[4:8]
    if adjoint:
        outs, (flow, coef, rhs, start, ping, pong, sems) = refs[8:10], refs[10:]
    else:
        weight_ref, outs, (flow, coef, rhs, start, ping, pong, sems) = refs[8], refs[9:11], refs[11:]
    dirs, depth, height, _ = rhs.shape
    reach = REACH
    own = depth - 2 * reach
    chunks = height // 8
    a, at_bottom, at_top = where_ref[0], where_ref[2], where_ref[3]
    code = [where_ref[4 + k] for k in range(4)]

    def arrivals(parts, into, first):
        up, down, lo, hi = parts
        moves = (
            (lo, into.at[:, 0:reach]),
            (down, into.at[:, reach : 2 * reach]),
            (up.at[:, 2 * reach - own : reach], into.at[:, 2 * reach : reach + own]),
            (hi, into.at[:, reach + own : depth]),
        )
        return [pltpu.make_async_copy(s, t, sems.at[first + k]) for k, (s, t) in enumerate(moves)]

    flow_moves = arrivals(flow_parts, flow, 0)
    value_moves = arrivals(value_parts, start, 4)
    for move in flow_moves + value_moves:
        move.start()

    shape = (8, LANES)
    sub = lax.broadcasted_iota(jnp.int32, shape, 0)
    lane = lax.broadcasted_iota(jnp.int32, shape, 1)
    top_sub, bottom_sub = sub == 7, sub == 0
    last_lane, first_lane = lane == LANES - 1, lane == 0
    zero = jnp.zeros(shape, jnp.float32)
    opened = [jnp.where(c == 0, 1.0, 0.0).astype(jnp.float32) for c in code]
    low_one = jnp.where(bottom_sub & (a == 0), opened[0], 1.0)
    high_one = jnp.where(top_sub & (a == 1), opened[1], 1.0)
    low_two = jnp.where(first_lane, opened[2], 1.0)
    high_two = jnp.where(last_lane, opened[3], 1.0)

    def both(x):
        positive = DIFFUSION + jnp.maximum(x, 0.0)
        return positive, positive - x

    def coefficients(p, carry):
        outside = ((p < reach) & (at_bottom == 1)) | ((p >= reach + own) & (at_top == 1))
        inside = jnp.where(outside, 0.0, 1.0)
        turned = zero
        for r in range(chunks):
            here = slice(r * 8, r * 8 + 8)
            one, two, three = flow[0, p, here, :], flow[1, p, here, :], flow[2, p, here, :]
            one_turned = pltpu.roll(one, 1, 0)
            one_below = jnp.where(bottom_sub, turned, one_turned)
            turned = one_turned
            two_below = jnp.where(first_lane, 0.0, pltpu.roll(two, 1, 1))
            up = [both(x) for x in (one, two, three)]
            down = [both(x) for x in (one_below, two_below, flow[2, p - 1, here, :])]
            first = up[0][0] if r < chunks - 1 else high_one * up[0][0]
            second = down[0][1] if r > 0 else low_one * down[0][1]
            diagonal = (1.0 + first) + (second + high_two * up[1][0])
            diagonal = diagonal + (low_two * down[1][1] + (up[2][0] + down[2][1]))
            inverse = inside / diagonal
            which = 0 if adjoint else 1
            coef[0, p, here, :] = up[0][which] * inverse
            coef[1, p, here, :] = down[0][1 - which] * inverse
            coef[2, p, here, :] = jnp.where(last_lane, 0.0, up[1][which] * inverse)
            coef[3, p, here, :] = jnp.where(first_lane, 0.0, down[1][1 - which] * inverse)
            coef[4, p, here, :] = up[2][which] * inverse
            coef[5, p, here, :] = down[2][1 - which] * inverse
            coef[6, p, here, :] = inverse
        return carry

    for move in flow_moves:
        move.wait()
    lax.fori_loop(1, depth - 1, coefficients, 0, unroll=2)
    for move in value_moves:
        move.wait()

    def sweep(source, lead, low, planes, offset, count, store):
        def rows(r):
            return pl.ds(offset + r * 8, 8)

        def at_planes(k, carry):
            p = low + 2 * k
            each = [(q, d) for q in range(2) for d in range(dirs)]
            value = {(q, d): source[d, p + q, rows(0), :] for q, d in each}
            up = {e: pltpu.roll(v, 7, 0) for e, v in value.items()}
            down = {e: pltpu.roll(v, 1, 0) for e, v in value.items()}
            before = dict.fromkeys(each, zero)
            if count < chunks:
                at = pl.multiple_of(jnp.maximum(offset - 8, 0), 8)
                for q, d in each:
                    outer = pltpu.roll(source[d, p + q, pl.ds(at, 8), :], 1, 0)
                    before[q, d] = jnp.where(a == 0, 0.0, outer)
            for r in range(count):
                c = [[coef[m, p + q, rows(r), :] for m in range(7 if lead else 6)] for q in range(2)]
                plane = {d: [source[d, p - 1, rows(r), :], value[0, d], value[1, d], source[d, p + 2, rows(r), :]] for d in range(dirs)}
                for q, d in each:
                    here = value[q, d]
                    if r + 1 < count:
                        following = source[d, p + q, rows(r + 1), :]
                        next_up, next_down = pltpu.roll(following, 7, 0), pltpu.roll(following, 1, 0)
                    elif count < chunks:
                        at = pl.multiple_of(jnp.minimum(offset + count * 8, height - 8), 8)
                        following = source[d, p + q, pl.ds(at, 8), :]
                        next_up, next_down = jnp.where(a == 1, 0.0, pltpu.roll(following, 7, 0)), zero
                    else:
                        following, next_up, next_down = zero, zero, zero
                    if lead:
                        total = here * c[q][6]
                        rhs[d, p + q, rows(r), :] = total
                    else:
                        total = rhs[d, p + q, rows(r), :]
                    depth_sum = c[q][4] * plane[d][q + 2] + c[q][5] * plane[d][q]
                    first_sum = c[q][0] * jnp.where(top_sub, next_up, up[q, d])
                    first_sum = first_sum + c[q][1] * jnp.where(bottom_sub, before[q, d], down[q, d])
                    second_sum = c[q][2] * pltpu.roll(here, LANES - 1, 1) + c[q][3] * pltpu.roll(here, 1, 1)
                    total = (total + depth_sum) + (first_sum + second_sum)
                    store(d, p + q, rows(r), r, total)
                    value[q, d], up[q, d], before[q, d], down[q, d] = (
                        following, next_up, down[q, d], next_down
                    )
            return carry

        lax.fori_loop(0, planes // 2, at_planes, 0)

    def into(ref):
        def store(d, p, here, r, total):
            ref[d, p, here, :] = total

        return store

    def again(d, p, here, r, total):
        start[d, p, here, :] = total if adjoint else total + start[d, p, here, :]

    def full(source, lead, step, store):
        sweep(source, lead, 1 + step, depth - 2 - 2 * step, 0, chunks, store)

    full(start, True, 0, into(ping))
    full(ping, False, 1, into(pong))
    full(pong, False, 2, again)
    full(start, True, 3, into(ping))
    full(ping, False, 4, into(pong))

    half = own // 2
    if adjoint:
        for out, side in zip(outs, (a, 1 - a)):
            low = reach + side * half

            def finish(d, p, here, r, total, out=out, low=low):
                out[d, p - low, r * 8 : r * 8 + 8, :] = total + start[d, p, here, :]

            shift = pl.multiple_of(a * SPARE, 8)
            sweep(pong, False, low, half, shift, (height - SPARE) // 8, finish)
    else:
        up_out, down_out = outs

        def emit(kinds):
            def finish(d, p, here, r, total):
                i = p - reach
                total = total * weight_ref[i // half, i % half, here, :]
                if "d" in kinds:
                    down_out[d, i, here, :] = total
                if "u" in kinds:
                    up_out[d, i - (own - reach), here, :] = total

            return finish

        for low, high, kinds in ((0, own - reach, "d"), (own - reach, reach, "du"), (reach, own, "u")):
            sweep(pong, False, reach + low, high - low, 0, chunks, emit(kinds))


def solves(adjoint, width, where, planes, flows, values, weight=None):
    dirs, reach, height, _ = values[0].shape
    depth = 2 * planes + 2 * reach
    ins = [where, *flows, *values]
    specs = [ANY] * 8
    if adjoint:
        outs = [floats(dirs, planes, height - SPARE, LANES)] * 2
    else:
        ins.append(weight)
        specs.append(VMEM)
        outs = [floats(*values[0].shape)] * 2
    scratch = [pltpu.VMEM((n, depth, height, LANES), jnp.float32) for n in (3, 7) + (dirs,) * 4]
    scratch.append(pltpu.SemaphoreType.DMA((8,)))
    return call(
        functools.partial(solve_kernel, adjoint, width),
        "adjoint" if adjoint else "forward",
        ins, outs, scratch, 36, 6 * 20 * dirs * depth * height * LANES, specs,
    )


def body(
    directions,
    eigen_basis,
    flow_first,
    flow_second,
    flow_depth,
    face_codes,
    sensor_cells,
    sensor_weight,
):
    dirs, planes, width, _ = directions.shape
    rank = eigen_basis.shape[0]
    count = lax.axis_size("slab")
    height = width // 2 + SPARE
    own, other, above = quad(count)
    me = lax.axis_index("slab")
    a, b = me // 2 % 2, me % 2
    place = [a, b, (me - 2 * a == 0), (me + 2 * (1 - a) == count - 1)]
    where = jnp.concatenate([jnp.stack([x.astype(jnp.int32) for x in place]), face_codes])
    each = dirs // GROUPS

    def regroup(first, second):
        return lax.ppermute(first, "slab", own), lax.ppermute(second, "slab", other)

    def cut(scalars, fields, group, lists=()):
        parts = len(fields) * len(group)
        extra = sum(x.shape[0] for x in lists)
        outs = [floats(parts * planes * height + extra, LANES)] * 2
        scratch = [
            pltpu.VMEM((max(extra, 8), LANES), jnp.float32),
            pltpu.SemaphoreType.DMA((2 * parts * planes + 2,)),
        ]
        kernel = functools.partial(cut_kernel, height, group, len(lists))
        specs = [VMEM] * len(lists) + [ANY] * len(fields)
        return call(kernel, "cut", [scalars, *lists, *fields], outs, scratch, 54, 0, specs, [ANY] * 2)

    def beyond(up, down):
        return up, down, lax.ppermute(up, "slab", above), lax.ppermute(down, "slab", back(above))

    def pack(scalars, pair, parts):
        outs = [floats(parts, REACH, height, LANES)] * 2
        return call(functools.partial(pack_kernel, planes), "pack", [scalars, *pair], outs)

    sensors = [x.reshape(-1, LANES) for x in (sensor_cells, sensor_weight)]
    listed = 2 * sensors[0].shape[0]
    block = planes * height
    basis = eigen_basis.reshape(rank, planes * width, LANES)
    flows = regroup(*cut(where, [flow_first, flow_second, flow_depth], [0]))
    tile, later = gram_tile(where, basis)
    moved = [regroup(*cut(later, [directions], range(each), sensors))]
    for k in range(each, dirs, each):
        moved.append(regroup(*cut(later, [directions], range(k, k + each))))
    flows = beyond(*pack(later, flows, 3))
    weight, last = call(
        functools.partial(sensor_kernel, width, each * block), "sensors", [later, *moved[0]],
        [floats(2, planes, height, LANES), jax.ShapeDtypeStruct(where.shape, where.dtype)],
        work=planes * height * listed * 20, out_specs=[VMEM, SMEM],
    )
    scalars = [later] + [last] * (GROUPS - 1)
    values = [beyond(*pack(s, m, each)) for s, m in zip(scalars, moved)]
    forcing = [beyond(*solves(False, width, where, planes, flows, v, weight)) for v in values]
    summed = [solves(True, width, where, planes, flows, f) for f in forcing]
    returned = [
        (lax.ppermute(s[0], "slab", back(own)), lax.ppermute(s[1], "slab", back(other)))
        for s in summed
    ]
    images = []
    for k, halves in enumerate(returned):
        copies = count if k == GROUPS - 1 else 1
        tile, image = projections(where, basis, directions, k * each, halves, tile, copies)
        images.append(image)
    rem, coeffs, parts = remainders(spread(tile, count), basis, images, count)
    new_directions = scaled(spread(parts, count), rem, planes * count * width * LANES, count)
    return (new_directions.reshape(directions.shape), coeffs)


def solution(mesh):
    return jax.shard_map(
        body,
        mesh=mesh,
        in_specs=(
            P("grp", "slab", None, None),
            P("grp", "slab", None, None),
            P("slab", None, None),
            P("slab", None, None),
            P("slab", None, None),
            P(),
            P(("grp", "slab")),
            P(("grp", "slab")),
        ),
        out_specs=(P("grp", "slab", None, None), P("grp", None)),
        check_vma=False,
    )
```

```python
import functools

import jax
import jax.numpy as jnp
from jax import lax
from jax.experimental import pallas as pl
from jax.experimental.pallas import tpu as pltpu
from jax.sharding import PartitionSpec as P

STEPS = 2
SWEEPS = 3
GROUPS = 2
SPARE = 16
REACH = STEPS * SWEEPS


DIFFUSION = 0.2
GAMMA = 0.5
LANES = 128
PIECES = 8
EXACT = lax.Precision.HIGHEST
SMEM = pl.BlockSpec(memory_space=pltpu.SMEM)
VMEM = pl.BlockSpec(memory_space=pltpu.VMEM)
ANY = pl.BlockSpec(memory_space=pl.ANY)
VECTOR = 150


def floats(*shape):
    return jax.ShapeDtypeStruct(shape, jnp.float32)


def cost(flops, moved):
    return pl.CostEstimate(flops=int(flops), bytes_accessed=int(moved), transcendentals=0)


def lane_sums(stack):
    ones = jnp.ones((8, LANES), jnp.float32)
    return lax.dot_general(
        ones, stack, (((1,), (1,)), ((), ())), precision=EXACT, preferred_element_type=jnp.float32
    )


def chunks_of(source, into, sems, pieces):
    rows = source.shape[1] // pieces
    return [
        pltpu.make_async_copy(
            source.at[:, pl.ds(k * rows, rows)], into.at[:, pl.ds(k * rows, rows)], sems.at[k]
        )
        for k in range(pieces)
    ]


def gram_kernel(where_ref, basis_hbm, out_ref, where_out, basis_ref, acc_ref, sems):
    rank, rows, _ = basis_ref.shape
    tile = 4
    moves = chunks_of(basis_hbm, basis_ref, sems, PIECES)
    for move in moves:
        move.start()
    for k in range(where_ref.shape[0]):
        where_out[k] = where_ref[k]
    acc_ref[...] = jnp.zeros_like(acc_ref)
    part = rows // PIECES
    for piece, move in enumerate(moves):
        move.wait()
        for i0 in range(0, rank, tile):
            for j0 in range(i0, rank, tile):
                pairs = [(i, j) for i in range(i0, i0 + tile) for j in range(j0, j0 + tile) if i <= j]

                def add(k, sums, i0=i0, j0=j0, pairs=pairs, piece=piece):
                    at = pl.ds(pl.multiple_of(piece * part + k * 8, 8), 8)
                    left = {i: basis_ref[i, at, :] for i in range(i0, i0 + tile)}
                    right = left if i0 == j0 else {j: basis_ref[j, at, :] for j in range(j0, j0 + tile)}
                    return [s + left[i] * right[j] for s, (i, j) in zip(sums, pairs)]

                sums = [jnp.zeros((8, LANES), jnp.float32) for _ in pairs]
                sums = lax.fori_loop(0, part // 8, add, sums, unroll=8)
                for (i, j), s in zip(pairs, sums):
                    acc_ref[i, j] += s

    row = lax.broadcasted_iota(jnp.int32, (rank, rank), 0)
    col = lax.broadcasted_iota(jnp.int32, (rank, rank), 1)
    gram = jnp.zeros((rank, rank), jnp.float32)
    for i in range(rank):
        sums = lane_sums(jnp.sum(acc_ref[i], axis=1))
        gram = jnp.where(row == i, jnp.broadcast_to(sums[0:1, :], (rank, rank)), gram)
    upper = jnp.where(col >= row, gram, 0.0)
    strict = jnp.where(col > row, gram, 0.0)
    whole = upper + strict.T
    out_ref[...] = jnp.zeros_like(out_ref)
    for k in range(0, rank, 8):
        at = 2 * rank + k * rank // 8
        out_ref[:, at : at + rank] = whole[k : k + 8]


def gram_tile(where, basis):
    rank, rows, _ = basis.shape
    return call(
        gram_kernel, "gram", [where, basis],
        [floats(8, LANES), jax.ShapeDtypeStruct(where.shape, where.dtype)],
        [
            pltpu.VMEM(basis.shape, jnp.float32),
            pltpu.VMEM((rank, rank, 8, LANES), jnp.float32),
            pltpu.SemaphoreType.DMA((PIECES,)),
        ],
        54, rank * rank * rows * LANES, [ANY], [VMEM, SMEM],
    )


def spread(tile, count):
    return lax.all_to_all(tile, "slab", 0, 0, tiled=True) if count > 1 else tile


def projection_kernel(first, where_ref, basis_in, dirs_hbm, own_hbm, other_hbm, tile_ref, out_ref, image_ref, *refs):
    moves = None
    if first == 0:
        basis_ref, dirs_ref, halves_ref, side_sems, sems = refs
        moves = chunks_of(basis_in, basis_ref, sems, PIECES)
    else:
        basis_ref, (dirs_ref, halves_ref, side_sems) = basis_in, refs
    rank = basis_ref.shape[0]
    dirs, rows, _ = image_ref.shape
    planes, half = halves_ref.shape[2:4]
    b = where_ref[1]
    sides = [
        pltpu.make_async_copy(own_hbm, halves_ref.at[0], side_sems.at[0]),
        pltpu.make_async_copy(other_hbm, halves_ref.at[1], side_sems.at[1]),
        pltpu.make_async_copy(dirs_hbm.at[pl.ds(first, dirs)], dirs_ref, side_sems.at[2]),
    ]
    for move in sides + (moves or []):
        move.start()
    for move in sides:
        move.wait()
    sums = [jnp.zeros((8, LANES), jnp.float32) for _ in range((rank + 1) * dirs)]
    piece = rows // PIECES
    for k in range(2 * planes):
        plane, part = k // 2, k % 2
        which = jnp.where(b == part, 0, 1)
        low = k * half
        if moves:
            for m in range(-(-low // piece), -(-(low + half) // piece)):
                moves[m].wait()

        def add(r, sums, plane=plane, which=which, low=low):
            at = pl.ds(pl.multiple_of(low + r * 8, 8), 8)
            here = pl.ds(pl.multiple_of(r * 8, 8), 8)
            image = []
            for d in range(dirs):
                value = halves_ref[which, d, plane, here, :] + GAMMA * dirs_ref[d, at, :]
                image_ref[d, at, :] = value
                image.append(value)
            out = []
            for i in range(rank):
                q = basis_ref[i, at, :]
                out += [sums[i * dirs + d] + q * image[d] for d in range(dirs)]
            return out + [sums[rank * dirs + d] + image[d] * image[d] for d in range(dirs)]

        sums = lax.fori_loop(0, half // 8, add, sums, unroll=4)

    row = lax.broadcasted_iota(jnp.int32, (8, LANES), 0)
    lane = lax.broadcasted_iota(jnp.int32, (8, LANES), 1)
    lines = [sums[i * dirs + d] for d in range(dirs) for i in range(rank)] + sums[rank * dirs :]
    lines = [jnp.sum(line, axis=0, keepdims=True) for line in lines]
    lines.append(jnp.zeros((LANES - len(lines), LANES), jnp.float32))
    found = lane_sums(jnp.concatenate(lines, 0))
    table = tile_ref[...]
    squares = pltpu.roll(found, (rank + first - rank * dirs) % LANES, 1)
    for d in range(dirs):
        products = pltpu.roll(found, (LANES - d * rank) % LANES, 1) if d else found
        table = jnp.where((row == first + d) & (lane < rank), products, table)
        table = jnp.where((row == first + d) & (lane == rank + first + d), squares, table)
    for r in range(out_ref.shape[0] // 8):
        out_ref[r * 8 : (r + 1) * 8, :] = table


def projections(where, basis, directions, first, halves, tile, count):
    rank, rows, _ = basis.shape
    dirs = halves[0].shape[0]
    outs = [floats(count * 8, LANES), floats(dirs, rows, LANES)]
    scratch = [
        pltpu.VMEM((dirs, rows, LANES), jnp.float32),
        pltpu.VMEM((2, *halves[0].shape), jnp.float32),
        pltpu.SemaphoreType.DMA((3,)),
    ]
    if first == 0:
        outs.append(floats(*basis.shape))
        scratch.append(pltpu.SemaphoreType.DMA((PIECES,)))
    found = call(
        functools.partial(projection_kernel, first), "projections",
        [where, basis, directions.reshape(-1, rows, LANES), *halves, tile],
        outs, scratch, 24, 2 * rank * dirs * rows * LANES,
        [ANY if first == 0 else VMEM] + [ANY] * 3 + [VMEM],
    )
    return (*found, basis)[:3] if first else found


def summed_tile(parts_ref):
    tiles = [parts_ref[r : r + 8, :] for r in range(0, parts_ref.shape[0], 8)]
    while len(tiles) > 1:
        tiles = [sum(tiles[k : k + 2]) for k in range(0, len(tiles), 2)]
    return tiles[0]


def eliminated(tile, rank):
    gram = [tile[:, 2 * rank + k * rank // 8 :][:, :rank] for k in range(0, rank, 8)]
    lane = lax.broadcasted_iota(jnp.int32, (8, LANES), 1)
    table = jnp.concatenate(
        [
            jnp.concatenate(gram, 0),
            tile[:, 0:rank].T,
            jnp.zeros((rank, LANES - rank - 8), jnp.float32),
        ],
        1,
    )
    table = jnp.concatenate([table, jnp.where(lane < rank + 8, tile, 0.0)], 0)
    row = lax.broadcasted_iota(jnp.int32, table.shape, 0)
    for k in range(rank):
        pivot_row = table[k : k + 1, :] / table[k : k + 1, k : k + 1]
        table = jnp.where(row == k, pivot_row, table - table[:, k : k + 1] * pivot_row)
    return table


def inverse_root(value):
    root = lax.rsqrt(value)
    return root * (1.5 - (0.5 * value * root) * root)


def remainder_kernel(dirs, cells, parts_ref, basis_ref, *refs):
    groups = len(refs) - 8
    images = refs[:groups]
    new_hbm, coeffs_ref, scale_out, again_ref, rem_ref, splat_ref, scale_ref, sems = refs[groups:]
    each = dirs // groups
    rank, rows, _ = basis_ref.shape
    tile = 4
    first = summed_tile(parts_ref)
    table = eliminated(first, rank)
    coeffs_ref[...] = table[0:rank, rank : rank + dirs]
    for d in range(dirs):
        for j in range(rank):
            splat_ref[d * rank + j] = jnp.broadcast_to(
                table[j : j + 1, rank + d : rank + d + 1], (8, LANES)
            )
    row = lax.broadcasted_iota(jnp.int32, (8, LANES), 0)
    lane = lax.broadcasted_iota(jnp.int32, (8, LANES), 1)
    energy, square = table[rank : rank + 8, :], first
    unsure = (lane == rank + row) & (row < dirs) & jnp.logical_not(energy >= 0.01 * square)
    again_ref[0] = jnp.max(jnp.where(unsure, 1.0, 0.0)).astype(jnp.int32)
    scale = inverse_root(jnp.maximum(energy, 0.0) / cells + 1e-06)
    scales = jnp.zeros((8, LANES), jnp.float32)
    for d in range(dirs):
        one = jnp.broadcast_to(scale[d : d + 1, rank + d : rank + d + 1], (8, LANES))
        scale_ref[d] = one
        scales = jnp.where(row == d, one, scales)
    scale_out[...] = scales
    part = rows // PIECES
    moves = []
    for piece in range(PIECES):
        for j0 in range(0, rank, tile):
            last = j0 + tile == rank
            weights = [[splat_ref[d * rank + j] for j in range(j0, j0 + tile)] for d in range(dirs)]
            scale = [scale_ref[d] for d in range(dirs)] if last else None

            def take(k, carry, j0=j0, last=last, weights=weights, scale=scale, piece=piece):
                at = pl.ds(pl.multiple_of(piece * part + k * 8, 8), 8)
                basis = [basis_ref[j, at, :] for j in range(j0, j0 + tile)]
                for d in range(dirs):
                    left = images[d // each][d % each, at, :] if j0 == 0 else rem_ref[d, at, :]
                    parts = [w * q for w, q in zip(weights[d], basis)]
                    left = left - ((parts[0] + parts[1]) + (parts[2] + parts[3]))
                    rem_ref[d, at, :] = left * scale[d] if last else left
                return carry

            lax.fori_loop(0, part // 8, take, 0, unroll=4)
        at = pl.ds(piece * part, part)
        moves.append(pltpu.make_async_copy(rem_ref.at[:, at], new_hbm.at[:, at], sems.at[piece]))
        moves[-1].start()
    for move in moves:
        move.wait()


def remainders(parts, basis, images, cells):
    rank, rows, _ = basis.shape
    dirs = sum(i.shape[0] for i in images)
    return call(
        functools.partial(remainder_kernel, dirs, cells), "remainder", [parts, basis, *images],
        [
            floats(dirs, rows, LANES),
            floats(rank, dirs),
            floats(8, LANES),
            jax.ShapeDtypeStruct((1,), jnp.int32),
        ],
        [
            pltpu.VMEM((dirs, rows, LANES), jnp.float32),
            pltpu.VMEM((dirs * rank, 8, LANES), jnp.float32),
            pltpu.VMEM((dirs, 8, LANES), jnp.float32),
            pltpu.SemaphoreType.DMA((PIECES,)),
        ],
        24, 2 * rank * dirs * rows * LANES, first=VMEM, out_specs=[ANY, VMEM, VMEM, SMEM],
    )


def squares_kernel(new_ref, out_ref, sum_ref):
    dirs = new_ref.shape[0]
    row = lax.broadcasted_iota(jnp.int32, (8, LANES), 0)

    @pl.when(pl.program_id(0) == 0)
    def _():
        sum_ref[...] = jnp.zeros_like(sum_ref)

    for d in range(dirs):
        lines = jnp.sum(new_ref[d] * new_ref[d], axis=0, keepdims=True)
        total = jnp.broadcast_to(jnp.sum(lines, axis=1, keepdims=True), (8, LANES))
        sum_ref[...] += jnp.where(row == d, total, 0.0)
    for r in range(out_ref.shape[0] // 8):
        out_ref[r * 8 : (r + 1) * 8, :] = sum_ref[...]


def rescale_kernel(cells, parts_ref, scale_ref, new_ref, out_ref):
    scale = scale_ref[...]
    energy = summed_tile(parts_ref) / scale / scale
    ratio = inverse_root(energy / cells + 1e-06) / scale
    for d in range(new_ref.shape[0]):
        out_ref[d] = new_ref[d] * ratio[d : d + 1, :]


def rescaled(new, scales, cells, count):
    dirs, rows, _ = new.shape
    chunk = 128
    lines = pl.BlockSpec((dirs, chunk, LANES), lambda k: (0, k, 0))
    whole = lambda n: pl.BlockSpec((n, LANES), lambda k: (0, 0))
    parts = pl.pallas_call(
        squares_kernel,
        grid=(rows // chunk,),
        in_specs=[lines],
        out_specs=whole(count * 8),
        out_shape=floats(count * 8, LANES),
        scratch_shapes=[pltpu.VMEM((8, LANES), jnp.float32)],
        compiler_params=pltpu.CompilerParams(vmem_limit_bytes=16 << 20),
        name="squares",
    )(new)
    return pl.pallas_call(
        functools.partial(rescale_kernel, cells),
        grid=(rows // chunk,),
        in_specs=[whole(count * 8), whole(8), lines],
        out_specs=lines,
        out_shape=floats(dirs, rows, LANES),
        compiler_params=pltpu.CompilerParams(vmem_limit_bytes=16 << 20),
        name="rescale",
    )(spread(parts, count), scales, new)


def quad(count):
    own, other, above = [], [], []
    for s in range(count):
        q, a, b = s // 4, s // 2 % 2, s % 2
        own.append((s, 4 * q + 2 * b + a))
        other.append((s, 4 * q + 2 * (1 - b) + a))
        up = s + 1 if b == 0 else s + 3
        if up < count:
            above.append((s, up))
    return own, other, above


def back(pairs):
    return [(target, source) for source, target in pairs]


def call(kernel, name, ins, outs, scratch=(), limit=16, work=0, specs=None, out_specs=None, first=SMEM):
    moved = sum(x.size * 4 for x in ins[1:]) + sum(o.size * 4 for o in outs)
    return pl.pallas_call(
        kernel,
        in_specs=[first] + (specs or [VMEM] * (len(ins) - 1)),
        out_specs=out_specs or [VMEM] * len(outs),
        out_shape=outs,
        scratch_shapes=list(scratch),
        compiler_params=pltpu.CompilerParams(vmem_limit_bytes=limit << 20),
        cost_estimate=cost(VECTOR * work, moved),
        name=name,
    )(*ins)


def cut_kernel(height, group, listed, where_ref, *refs):
    lists, fields = refs[:listed], refs[listed:-3]
    own_ref, other_ref, sems = refs[-3:]
    b = where_ref[1]
    moves = []

    def move(source, target):
        moves.append(pltpu.make_async_copy(source, target, sems.at[len(moves)]))
        moves[-1].start()

    k = 0
    for field in fields:
        start = pl.multiple_of(b * (field.shape[-2] - height), 16)
        rest = pl.multiple_of((1 - b) * (field.shape[-2] - height), 16)
        for d in group:
            for p in range(field.shape[-3]):
                at = (p,) if len(field.shape) == 3 else (d, p)
                for ref, low in ((own_ref, start), (other_ref, rest)):
                    move(field.at[(*at, pl.ds(low, height))], ref.at[pl.ds(k, height)])
                k += height
    for entries in lists:
        rows = entries.shape[0]
        for ref in (own_ref, other_ref):
            ref[k : k + rows, :] = entries[...].astype(jnp.float32)
        k += rows
    for m in moves:
        m.wait()


def pack_kernel(planes, where_ref, own_ref, other_ref, up_ref, down_ref):
    count, reach, height, _ = up_ref.shape
    skip = 2 * planes - reach

    def join(first, second):
        for d in range(count):
            for p in range(2 * planes):
                ref = first if p < planes else second
                at = (d * planes + p % planes) * height
                value = ref[at : at + height, :]
                if p >= skip:
                    up_ref[d, p - skip] = value
                if p < reach:
                    down_ref[d, p] = value

    @pl.when(where_ref[0] == 0)
    def _():
        join(own_ref, other_ref)

    @pl.when(where_ref[0] == 1)
    def _():
        join(other_ref, own_ref)


def sensor_kernel(width, skip, where_ref, own_ref, other_ref, out_ref, where_out):
    for k in range(where_ref.shape[0]):
        where_out[k] = where_ref[k]
    a = where_ref[0]
    _, planes, height, _ = out_ref.shape
    first = a * (width - height)
    count = (own_ref.shape[0] - skip) // 2
    group = 4
    chunk = group * LANES
    targets = planes * height
    rows = lax.broadcasted_iota(jnp.int32, (targets, chunk), 0)
    lanes = lax.broadcasted_iota(jnp.int32, (LANES, chunk), 0)
    for ref, at in ((own_ref, a), (other_ref, 1 - a)):
        total = jnp.zeros((targets, 3 * LANES), jnp.float32)
        for k in range(skip, skip + count, group):
            take = lambda at: jnp.concatenate([ref[at + g : at + g + 1, :] for g in range(group)], 1)
            cell = take(k).astype(jnp.int32)
            weight = take(count + k)
            line = cell // LANES
            lane = cell - line * LANES
            plane = line // width
            row = line - plane * width - first
            inside = (row >= 0) & (row < height)
            target = jnp.where(inside, plane * height + row, -1)
            high = weight.astype(jnp.bfloat16).astype(jnp.float32)
            rest = weight - high
            middle = rest.astype(jnp.bfloat16).astype(jnp.float32)
            low = rest - middle
            hot = jnp.where(rows == target, 1.0, 0.0).astype(jnp.bfloat16)
            here = lanes == lane
            parts = [jnp.where(here, part, 0.0).astype(jnp.bfloat16) for part in (high, middle, low)]
            total += lax.dot_general(
                hot,
                jnp.concatenate(parts, 0),
                (((1,), (1,)), ((), ())),
                preferred_element_type=jnp.float32,
            )
        total = total[:, 0:LANES] + total[:, LANES : 2 * LANES] + total[:, 2 * LANES :]
        out_ref[at] = total.reshape(planes, height, LANES)


def solve_kernel(adjoint, width, where_ref, *refs):
    flow_parts, value_parts = refs[0:4], refs[4:8]
    if adjoint:
        outs, (flow, coef, rhs, start, ping, pong, sems) = refs[8:10], refs[10:]
    else:
        weight_ref, outs, (flow, coef, rhs, start, ping, pong, sems) = refs[8], refs[9:11], refs[11:]
    dirs, depth, height, _ = rhs.shape
    reach = REACH
    own = depth - 2 * reach
    chunks = height // 8
    a, at_bottom, at_top = where_ref[0], where_ref[2], where_ref[3]
    code = [where_ref[4 + k] for k in range(4)]

    def arrivals(parts, into, first):
        up, down, lo, hi = parts
        moves = (
            (lo, into.at[:, 0:reach]),
            (down, into.at[:, reach : 2 * reach]),
            (up.at[:, 2 * reach - own : reach], into.at[:, 2 * reach : reach + own]),
            (hi, into.at[:, reach + own : depth]),
        )
        return [pltpu.make_async_copy(s, t, sems.at[first + k]) for k, (s, t) in enumerate(moves)]

    flow_moves = arrivals(flow_parts, flow, 0)
    value_moves = arrivals(value_parts, start, 4)
    for move in flow_moves + value_moves:
        move.start()

    shape = (8, LANES)
    sub = lax.broadcasted_iota(jnp.int32, shape, 0)
    lane = lax.broadcasted_iota(jnp.int32, shape, 1)
    top_sub, bottom_sub = sub == 7, sub == 0
    last_lane, first_lane = lane == LANES - 1, lane == 0
    zero = jnp.zeros(shape, jnp.float32)
    opened = [jnp.where(c == 0, 1.0, 0.0).astype(jnp.float32) for c in code]
    low_one = jnp.where(bottom_sub & (a == 0), opened[0], 1.0)
    high_one = jnp.where(top_sub & (a == 1), opened[1], 1.0)
    low_two = jnp.where(first_lane, opened[2], 1.0)
    high_two = jnp.where(last_lane, opened[3], 1.0)

    def both(x):
        positive = DIFFUSION + jnp.maximum(x, 0.0)
        return positive, positive - x

    def coefficients(p, carry):
        outside = ((p < reach) & (at_bottom == 1)) | ((p >= reach + own) & (at_top == 1))
        inside = jnp.where(outside, 0.0, 1.0)
        turned = zero
        for r in range(chunks):
            here = slice(r * 8, r * 8 + 8)
            one, two, three = flow[0, p, here, :], flow[1, p, here, :], flow[2, p, here, :]
            one_turned = pltpu.roll(one, 1, 0)
            one_below = jnp.where(bottom_sub, turned, one_turned)
            turned = one_turned
            two_below = jnp.where(first_lane, 0.0, pltpu.roll(two, 1, 1))
            up = [both(x) for x in (one, two, three)]
            down = [both(x) for x in (one_below, two_below, flow[2, p - 1, here, :])]
            first = up[0][0] if r < chunks - 1 else high_one * up[0][0]
            second = down[0][1] if r > 0 else low_one * down[0][1]
            diagonal = (1.0 + first) + (second + high_two * up[1][0])
            diagonal = diagonal + (low_two * down[1][1] + (up[2][0] + down[2][1]))
            inverse = inside / diagonal
            which = 0 if adjoint else 1
            coef[0, p, here, :] = up[0][which] * inverse
            coef[1, p, here, :] = down[0][1 - which] * inverse
            coef[2, p, here, :] = jnp.where(last_lane, 0.0, up[1][which] * inverse)
            coef[3, p, here, :] = jnp.where(first_lane, 0.0, down[1][1 - which] * inverse)
            coef[4, p, here, :] = up[2][which] * inverse
            coef[5, p, here, :] = down[2][1 - which] * inverse
            coef[6, p, here, :] = inverse
        return carry

    for move in flow_moves:
        move.wait()
    lax.fori_loop(1, depth - 1, coefficients, 0, unroll=2)
    for move in value_moves:
        move.wait()

    def sweep(source, lead, low, planes, offset, count, store):
        def rows(r):
            return pl.ds(offset + r * 8, 8)

        def at_planes(k, carry):
            p = low + 2 * k
            each = [(q, d) for q in range(2) for d in range(dirs)]
            value = {(q, d): source[d, p + q, rows(0), :] for q, d in each}
            up = {e: pltpu.roll(v, 7, 0) for e, v in value.items()}
            down = {e: pltpu.roll(v, 1, 0) for e, v in value.items()}
            before = dict.fromkeys(each, zero)
            if count < chunks:
                at = pl.multiple_of(jnp.maximum(offset - 8, 0), 8)
                for q, d in each:
                    outer = pltpu.roll(source[d, p + q, pl.ds(at, 8), :], 1, 0)
                    before[q, d] = jnp.where(a == 0, 0.0, outer)
            for r in range(count):
                c = [[coef[m, p + q, rows(r), :] for m in range(7 if lead else 6)] for q in range(2)]
                plane = {d: [source[d, p - 1, rows(r), :], value[0, d], value[1, d], source[d, p + 2, rows(r), :]] for d in range(dirs)}
                for q, d in each:
                    here = value[q, d]
                    if r + 1 < count:
                        following = source[d, p + q, rows(r + 1), :]
                        next_up, next_down = pltpu.roll(following, 7, 0), pltpu.roll(following, 1, 0)
                    elif count < chunks:
                        at = pl.multiple_of(jnp.minimum(offset + count * 8, height - 8), 8)
                        following = source[d, p + q, pl.ds(at, 8), :]
                        next_up, next_down = jnp.where(a == 1, 0.0, pltpu.roll(following, 7, 0)), zero
                    else:
                        following, next_up, next_down = zero, zero, zero
                    if lead:
                        total = here * c[q][6]
                        rhs[d, p + q, rows(r), :] = total
                    else:
                        total = rhs[d, p + q, rows(r), :]
                    depth_sum = c[q][4] * plane[d][q + 2] + c[q][5] * plane[d][q]
                    first_sum = c[q][0] * jnp.where(top_sub, next_up, up[q, d])
                    first_sum = first_sum + c[q][1] * jnp.where(bottom_sub, before[q, d], down[q, d])
                    second_sum = c[q][2] * pltpu.roll(here, LANES - 1, 1) + c[q][3] * pltpu.roll(here, 1, 1)
                    total = (total + depth_sum) + (first_sum + second_sum)
                    store(d, p + q, rows(r), r, total)
                    value[q, d], up[q, d], before[q, d], down[q, d] = (
                        following, next_up, down[q, d], next_down
                    )
            return carry

        lax.fori_loop(0, planes // 2, at_planes, 0)

    def into(ref):
        def store(d, p, here, r, total):
            ref[d, p, here, :] = total

        return store

    def again(d, p, here, r, total):
        start[d, p, here, :] = total if adjoint else total + start[d, p, here, :]

    def full(source, lead, step, store):
        sweep(source, lead, 1 + step, depth - 2 - 2 * step, 0, chunks, store)

    full(start, True, 0, into(ping))
    full(ping, False, 1, into(pong))
    full(pong, False, 2, again)
    full(start, True, 3, into(ping))
    full(ping, False, 4, into(pong))

    half = own // 2
    if adjoint:
        for out, side in zip(outs, (a, 1 - a)):
            low = reach + side * half

            def finish(d, p, here, r, total, out=out, low=low):
                out[d, p - low, r * 8 : r * 8 + 8, :] = total + start[d, p, here, :]

            shift = pl.multiple_of(a * SPARE, 8)
            sweep(pong, False, low, half, shift, (height - SPARE) // 8, finish)
    else:
        up_out, down_out = outs

        def emit(kinds):
            def finish(d, p, here, r, total):
                i = p - reach
                total = total * weight_ref[i // half, i % half, here, :]
                if "d" in kinds:
                    down_out[d, i, here, :] = total
                if "u" in kinds:
                    up_out[d, i - (own - reach), here, :] = total

            return finish

        for low, high, kinds in ((0, own - reach, "d"), (own - reach, reach, "du"), (reach, own, "u")):
            sweep(pong, False, reach + low, high - low, 0, chunks, emit(kinds))


def solves(adjoint, width, where, planes, flows, values, weight=None):
    dirs, reach, height, _ = values[0].shape
    depth = 2 * planes + 2 * reach
    ins = [where, *flows, *values]
    specs = [ANY] * 8
    if adjoint:
        outs = [floats(dirs, planes, height - SPARE, LANES)] * 2
    else:
        ins.append(weight)
        specs.append(VMEM)
        outs = [floats(*values[0].shape)] * 2
    scratch = [pltpu.VMEM((n, depth, height, LANES), jnp.float32) for n in (3, 7) + (dirs,) * 4]
    scratch.append(pltpu.SemaphoreType.DMA((8,)))
    return call(
        functools.partial(solve_kernel, adjoint, width),
        "adjoint" if adjoint else "forward",
        ins, outs, scratch, 36, 6 * 20 * dirs * depth * height * LANES, specs,
    )


def body(
    directions,
    eigen_basis,
    flow_first,
    flow_second,
    flow_depth,
    face_codes,
    sensor_cells,
    sensor_weight,
):
    dirs, planes, width, _ = directions.shape
    rank = eigen_basis.shape[0]
    count = lax.axis_size("slab")
    height = width // 2 + SPARE
    own, other, above = quad(count)
    me = lax.axis_index("slab")
    a, b = me // 2 % 2, me % 2
    place = [a, b, (me - 2 * a == 0), (me + 2 * (1 - a) == count - 1)]
    where = jnp.concatenate([jnp.stack([x.astype(jnp.int32) for x in place]), face_codes])
    each = dirs // GROUPS

    def regroup(first, second):
        return lax.ppermute(first, "slab", own), lax.ppermute(second, "slab", other)

    def cut(scalars, fields, group, lists=()):
        parts = len(fields) * len(group)
        extra = sum(x.shape[0] for x in lists)
        outs = [floats(parts * planes * height + extra, LANES)] * 2
        scratch = [pltpu.SemaphoreType.DMA((2 * parts * planes,))]
        kernel = functools.partial(cut_kernel, height, group, len(lists))
        specs = [VMEM] * len(lists) + [ANY] * len(fields)
        return call(kernel, "cut", [scalars, *lists, *fields], outs, scratch, 54, 0, specs)

    def beyond(up, down):
        return up, down, lax.ppermute(up, "slab", above), lax.ppermute(down, "slab", back(above))

    def pack(scalars, pair, parts):
        outs = [floats(parts, REACH, height, LANES)] * 2
        return call(functools.partial(pack_kernel, planes), "pack", [scalars, *pair], outs)

    sensors = [x.reshape(-1, LANES) for x in (sensor_cells, sensor_weight)]
    listed = 2 * sensors[0].shape[0]
    block = planes * height
    basis = eigen_basis.reshape(rank, planes * width, LANES)
    flows = regroup(*cut(where, [flow_first, flow_second, flow_depth], [0]))
    tile, later = gram_tile(where, basis)
    moved = [regroup(*cut(later, [directions], range(each), sensors))]
    for k in range(each, dirs, each):
        moved.append(regroup(*cut(later, [directions], range(k, k + each))))
    flows = beyond(*pack(later, flows, 3))
    weight, last = call(
        functools.partial(sensor_kernel, width, each * block), "sensors", [later, *moved[0]],
        [floats(2, planes, height, LANES), jax.ShapeDtypeStruct(where.shape, where.dtype)],
        work=planes * height * listed * 20, out_specs=[VMEM, SMEM],
    )
    scalars = [later] + [last] * (GROUPS - 1)
    values = [beyond(*pack(s, m, each)) for s, m in zip(scalars, moved)]
    forcing = [beyond(*solves(False, width, where, planes, flows, v, weight)) for v in values]
    summed = [solves(True, width, where, planes, flows, f) for f in forcing]
    returned = [
        (lax.ppermute(s[0], "slab", back(own)), lax.ppermute(s[1], "slab", back(other)))
        for s in summed
    ]
    images = []
    for k, halves in enumerate(returned):
        copies = count if k == GROUPS - 1 else 1
        tile, image, basis = projections(where, basis, directions, k * each, halves, tile, copies)
        images.append(image)
    cells = planes * count * width * LANES
    new, coeffs, scales, again = remainders(spread(tile, count), basis, images, cells)
    new, _ = lax.while_loop(
        lambda state: state[1] > 0,
        lambda state: (rescaled(state[0], scales, cells, count), jnp.int32(0)),
        (new, again[0]),
    )
    return (new.reshape(directions.shape), coeffs)


def solution(mesh):
    return jax.shard_map(
        body,
        mesh=mesh,
        in_specs=(
            P("grp", "slab", None, None),
            P("grp", "slab", None, None),
            P("slab", None, None),
            P("slab", None, None),
            P("slab", None, None),
            P(),
            P(("grp", "slab")),
            P(("grp", "slab")),
        ),
        out_specs=(P("grp", "slab", None, None), P("grp", None)),
        check_vma=False,
    )
```

```python
import functools

import jax
import jax.numpy as jnp
from jax import lax
from jax.experimental import pallas as pl
from jax.experimental.pallas import tpu as pltpu
from jax.sharding import PartitionSpec as P

STEPS = 2
SWEEPS = 3
GROUPS = 2
SPARE = 16
REACH = STEPS * SWEEPS


DIFFUSION = 0.2
GAMMA = 0.5
LANES = 128
PIECES = 8
EXACT = lax.Precision.HIGHEST
SMEM = pl.BlockSpec(memory_space=pltpu.SMEM)
VMEM = pl.BlockSpec(memory_space=pltpu.VMEM)
ANY = pl.BlockSpec(memory_space=pl.ANY)
VECTOR = 150


def place():
    me, count = lax.axis_index("slab"), lax.axis_size("slab")
    a, b = lax.rem(me // 2, 2), lax.rem(me, 2)
    return a, b, me - 2 * a == 0, me + 2 * (1 - a) == count - 1


def floats(*shape):
    return jax.ShapeDtypeStruct(shape, jnp.float32)


def cost(flops, moved):
    return pl.CostEstimate(flops=int(flops), bytes_accessed=int(moved), transcendentals=0)


def lane_sums(stack):
    ones = jnp.ones((8, LANES), jnp.float32)
    return lax.dot_general(
        ones, stack, (((1,), (1,)), ((), ())), precision=EXACT, preferred_element_type=jnp.float32
    )


def chunks_of(source, into, sems, pieces):
    rows = source.shape[1] // pieces
    return [
        pltpu.make_async_copy(
            source.at[:, pl.ds(k * rows, rows)], into.at[:, pl.ds(k * rows, rows)], sems.at[k]
        )
        for k in range(pieces)
    ]


def gram_kernel(basis_hbm, out_ref, after_ref, basis_ref, acc_ref, sems):
    rank, rows, _ = basis_ref.shape
    tile = 4
    moves = chunks_of(basis_hbm, basis_ref, sems, PIECES)
    for move in moves:
        move.start()
    after_ref[0] = 0
    acc_ref[...] = jnp.zeros_like(acc_ref)
    part = rows // PIECES
    for piece, move in enumerate(moves):
        move.wait()
        for i0 in range(0, rank, tile):
            for j0 in range(i0, rank, tile):
                pairs = [(i, j) for i in range(i0, i0 + tile) for j in range(j0, j0 + tile) if i <= j]

                def add(k, sums, i0=i0, j0=j0, pairs=pairs, piece=piece):
                    at = pl.ds(pl.multiple_of(piece * part + k * 8, 8), 8)
                    left = {i: basis_ref[i, at, :] for i in range(i0, i0 + tile)}
                    right = left if i0 == j0 else {j: basis_ref[j, at, :] for j in range(j0, j0 + tile)}
                    return [s + left[i] * right[j] for s, (i, j) in zip(sums, pairs)]

                sums = [jnp.zeros((8, LANES), jnp.float32) for _ in pairs]
                sums = lax.fori_loop(0, part // 8, add, sums, unroll=8)
                for (i, j), s in zip(pairs, sums):
                    acc_ref[i, j] += s

    row = lax.broadcasted_iota(jnp.int32, (rank, rank), 0)
    col = lax.broadcasted_iota(jnp.int32, (rank, rank), 1)
    gram = jnp.zeros((rank, rank), jnp.float32)
    for i in range(rank):
        sums = lane_sums(jnp.sum(acc_ref[i], axis=1))
        gram = jnp.where(row == i, jnp.broadcast_to(sums[0:1, :], (rank, rank)), gram)
    upper = jnp.where(col >= row, gram, 0.0)
    strict = jnp.where(col > row, gram, 0.0)
    whole = upper + strict.T
    out_ref[...] = jnp.zeros_like(out_ref)
    for k in range(0, rank, 8):
        at = 2 * rank + k * rank // 8
        out_ref[:, at : at + rank] = whole[k : k + 8]


TOKEN = jax.ShapeDtypeStruct((1,), jnp.int32)


def gram_tile(basis):
    rank, rows, _ = basis.shape
    return call(
        gram_kernel, "gram", [basis], [floats(8, LANES), TOKEN],
        [
            pltpu.VMEM(basis.shape, jnp.float32),
            pltpu.VMEM((rank, rank, 8, LANES), jnp.float32),
            pltpu.SemaphoreType.DMA((PIECES,)),
        ],
        54, rank * rank * rows * LANES, [ANY], [VMEM, SMEM],
    )


def spread(tile, count):
    return lax.all_to_all(tile, "slab", 0, 0, tiled=True) if count > 1 else tile


def projection_kernel(first, basis_in, dirs_hbm, own_hbm, other_hbm, tile_ref, out_ref, image_ref, *refs):
    moves = None
    if first == 0:
        basis_ref, dirs_ref, halves_ref, side_sems, sems = refs
        moves = chunks_of(basis_in, basis_ref, sems, PIECES)
    else:
        basis_ref, (dirs_ref, halves_ref, side_sems) = basis_in, refs
    rank = basis_ref.shape[0]
    dirs, rows, _ = image_ref.shape
    planes, half = halves_ref.shape[2:4]
    b = place()[1]
    sides = [
        pltpu.make_async_copy(own_hbm, halves_ref.at[0], side_sems.at[0]),
        pltpu.make_async_copy(other_hbm, halves_ref.at[1], side_sems.at[1]),
        pltpu.make_async_copy(dirs_hbm.at[pl.ds(first, dirs)], dirs_ref, side_sems.at[2]),
    ]
    for move in sides + (moves or []):
        move.start()
    for move in sides:
        move.wait()
    sums = [jnp.zeros((8, LANES), jnp.float32) for _ in range((rank + 1) * dirs)]
    piece = rows // PIECES
    for k in range(2 * planes):
        plane, part = k // 2, k % 2
        which = jnp.where(b == part, 0, 1)
        low = k * half
        if moves:
            for m in range(-(-low // piece), -(-(low + half) // piece)):
                moves[m].wait()

        def add(r, sums, plane=plane, which=which, low=low):
            at = pl.ds(pl.multiple_of(low + r * 8, 8), 8)
            here = pl.ds(pl.multiple_of(r * 8, 8), 8)
            image = []
            for d in range(dirs):
                value = halves_ref[which, d, plane, here, :] + GAMMA * dirs_ref[d, at, :]
                image_ref[d, at, :] = value
                image.append(value)
            out = []
            for i in range(rank):
                q = basis_ref[i, at, :]
                out += [sums[i * dirs + d] + q * image[d] for d in range(dirs)]
            return out + [sums[rank * dirs + d] + image[d] * image[d] for d in range(dirs)]

        sums = lax.fori_loop(0, half // 8, add, sums, unroll=4)

    row = lax.broadcasted_iota(jnp.int32, (8, LANES), 0)
    lane = lax.broadcasted_iota(jnp.int32, (8, LANES), 1)
    lines = [sums[i * dirs + d] for d in range(dirs) for i in range(rank)] + sums[rank * dirs :]
    lines = [jnp.sum(line, axis=0, keepdims=True) for line in lines]
    lines.append(jnp.zeros((LANES - len(lines), LANES), jnp.float32))
    found = lane_sums(jnp.concatenate(lines, 0))
    table = tile_ref[...]
    squares = pltpu.roll(found, (rank + first - rank * dirs) % LANES, 1)
    for d in range(dirs):
        products = pltpu.roll(found, (LANES - d * rank) % LANES, 1) if d else found
        table = jnp.where((row == first + d) & (lane < rank), products, table)
        table = jnp.where((row == first + d) & (lane == rank + first + d), squares, table)
    for r in range(out_ref.shape[0] // 8):
        out_ref[r * 8 : (r + 1) * 8, :] = table


def projections(basis, directions, first, halves, tile, count):
    rank, rows, _ = basis.shape
    dirs = halves[0].shape[0]
    outs = [floats(count * 8, LANES), floats(dirs, rows, LANES)]
    scratch = [
        pltpu.VMEM((dirs, rows, LANES), jnp.float32),
        pltpu.VMEM((2, *halves[0].shape), jnp.float32),
        pltpu.SemaphoreType.DMA((3,)),
    ]
    if first == 0:
        outs.append(floats(*basis.shape))
        scratch.append(pltpu.SemaphoreType.DMA((PIECES,)))
    found = call(
        functools.partial(projection_kernel, first), "projections",
        [basis, directions.reshape(-1, rows, LANES), *halves, tile],
        outs, scratch, 24, 2 * rank * dirs * rows * LANES,
        [ANY if first == 0 else VMEM] + [ANY] * 3 + [VMEM],
    )
    return (*found, basis)[:3] if first else found


def summed_tile(parts_ref):
    tiles = [parts_ref[r : r + 8, :] for r in range(0, parts_ref.shape[0], 8)]
    while len(tiles) > 1:
        tiles = [sum(tiles[k : k + 2]) for k in range(0, len(tiles), 2)]
    return tiles[0]


def eliminated(tile, rank):
    gram = [tile[:, 2 * rank + k * rank // 8 :][:, :rank] for k in range(0, rank, 8)]
    lane = lax.broadcasted_iota(jnp.int32, (8, LANES), 1)
    table = jnp.concatenate(
        [
            jnp.concatenate(gram, 0),
            tile[:, 0:rank].T,
            jnp.zeros((rank, LANES - rank - 8), jnp.float32),
        ],
        1,
    )
    table = jnp.concatenate([table, jnp.where(lane < rank + 8, tile, 0.0)], 0)
    row = lax.broadcasted_iota(jnp.int32, table.shape, 0)
    for k in range(rank):
        pivot_row = table[k : k + 1, :] / table[k : k + 1, k : k + 1]
        table = jnp.where(row == k, pivot_row, table - table[:, k : k + 1] * pivot_row)
    return table


def inverse_root(value):
    root = lax.rsqrt(value)
    return root * (1.5 - (0.5 * value * root) * root)


def remainder_kernel(dirs, cells, parts_ref, basis_ref, *refs):
    groups = len(refs) - 8
    images = refs[:groups]
    new_hbm, coeffs_ref, scale_out, again_ref, rem_ref, splat_ref, scale_ref, sems = refs[groups:]
    each = dirs // groups
    rank, rows, _ = basis_ref.shape
    tile = 4
    first = summed_tile(parts_ref)
    table = eliminated(first, rank)
    coeffs_ref[...] = table[0:rank, rank : rank + 8].T[0:dirs]
    for d in range(dirs):
        for j in range(rank):
            splat_ref[d * rank + j] = jnp.broadcast_to(
                table[j : j + 1, rank + d : rank + d + 1], (8, LANES)
            )
    row = lax.broadcasted_iota(jnp.int32, (8, LANES), 0)
    lane = lax.broadcasted_iota(jnp.int32, (8, LANES), 1)
    energy, square = table[rank : rank + 8, :], first
    unsure = (lane == rank + row) & (row < dirs) & jnp.logical_not(energy >= 0.01 * square)
    again_ref[0] = jnp.max(jnp.where(unsure, 1.0, 0.0)).astype(jnp.int32)
    scale = inverse_root(jnp.maximum(energy, 0.0) / cells + 1e-06)
    scales = jnp.zeros((8, LANES), jnp.float32)
    for d in range(dirs):
        one = jnp.broadcast_to(scale[d : d + 1, rank + d : rank + d + 1], (8, LANES))
        scale_ref[d] = one
        scales = jnp.where(row == d, one, scales)
    scale_out[...] = scales
    part = rows // PIECES
    moves = []
    for piece in range(PIECES):
        for j0 in range(0, rank, tile):
            last = j0 + tile == rank
            weights = [[splat_ref[d * rank + j] for j in range(j0, j0 + tile)] for d in range(dirs)]
            scale = [scale_ref[d] for d in range(dirs)] if last else None

            def take(k, carry, j0=j0, last=last, weights=weights, scale=scale, piece=piece):
                at = pl.ds(pl.multiple_of(piece * part + k * 8, 8), 8)
                basis = [basis_ref[j, at, :] for j in range(j0, j0 + tile)]
                for d in range(dirs):
                    left = images[d // each][d % each, at, :] if j0 == 0 else rem_ref[d, at, :]
                    parts = [w * q for w, q in zip(weights[d], basis)]
                    left = left - ((parts[0] + parts[1]) + (parts[2] + parts[3]))
                    rem_ref[d, at, :] = left * scale[d] if last else left
                return carry

            lax.fori_loop(0, part // 8, take, 0, unroll=4)
        at = pl.ds(piece * part, part)
        moves.append(pltpu.make_async_copy(rem_ref.at[:, at], new_hbm.at[:, at], sems.at[piece]))
        moves[-1].start()
    for move in moves:
        move.wait()


def remainders(parts, basis, images, cells):
    rank, rows, _ = basis.shape
    dirs = sum(i.shape[0] for i in images)
    return call(
        functools.partial(remainder_kernel, dirs, cells), "remainder", [parts, basis, *images],
        [
            floats(dirs, rows, LANES),
            floats(dirs, rank),
            floats(8, LANES),
            TOKEN,
        ],
        [
            pltpu.VMEM((dirs, rows, LANES), jnp.float32),
            pltpu.VMEM((dirs * rank, 8, LANES), jnp.float32),
            pltpu.VMEM((dirs, 8, LANES), jnp.float32),
            pltpu.SemaphoreType.DMA((PIECES,)),
        ],
        24, 2 * rank * dirs * rows * LANES, out_specs=[ANY, VMEM, VMEM, SMEM],
    )


def squares_kernel(new_ref, out_ref, sum_ref):
    dirs = new_ref.shape[0]
    row = lax.broadcasted_iota(jnp.int32, (8, LANES), 0)

    @pl.when(pl.program_id(0) == 0)
    def _():
        sum_ref[...] = jnp.zeros_like(sum_ref)

    for d in range(dirs):
        lines = jnp.sum(new_ref[d] * new_ref[d], axis=0, keepdims=True)
        total = jnp.broadcast_to(jnp.sum(lines, axis=1, keepdims=True), (8, LANES))
        sum_ref[...] += jnp.where(row == d, total, 0.0)
    for r in range(out_ref.shape[0] // 8):
        out_ref[r * 8 : (r + 1) * 8, :] = sum_ref[...]


def rescale_kernel(cells, parts_ref, scale_ref, new_ref, out_ref):
    scale = scale_ref[...]
    energy = summed_tile(parts_ref) / scale / scale
    ratio = inverse_root(energy / cells + 1e-06) / scale
    for d in range(new_ref.shape[0]):
        out_ref[d] = new_ref[d] * ratio[d : d + 1, :]


def rescaled(new, scales, cells, count):
    dirs, rows, _ = new.shape
    chunk = 128
    lines = pl.BlockSpec((dirs, chunk, LANES), lambda k: (0, k, 0))
    whole = lambda n: pl.BlockSpec((n, LANES), lambda k: (0, 0))
    parts = pl.pallas_call(
        squares_kernel,
        grid=(rows // chunk,),
        in_specs=[lines],
        out_specs=whole(count * 8),
        out_shape=floats(count * 8, LANES),
        scratch_shapes=[pltpu.VMEM((8, LANES), jnp.float32)],
        compiler_params=pltpu.CompilerParams(vmem_limit_bytes=16 << 20),
        name="squares",
    )(new)
    return pl.pallas_call(
        functools.partial(rescale_kernel, cells),
        grid=(rows // chunk,),
        in_specs=[whole(count * 8), whole(8), lines],
        out_specs=lines,
        out_shape=floats(dirs, rows, LANES),
        compiler_params=pltpu.CompilerParams(vmem_limit_bytes=16 << 20),
        name="rescale",
    )(spread(parts, count), scales, new)


def quad(count):
    own, other, above = [], [], []
    for s in range(count):
        q, a, b = s // 4, s // 2 % 2, s % 2
        own.append((s, 4 * q + 2 * b + a))
        other.append((s, 4 * q + 2 * (1 - b) + a))
        up = s + 1 if b == 0 else s + 3
        if up < count:
            above.append((s, up))
    return own, other, above


def back(pairs):
    return [(target, source) for source, target in pairs]


def call(kernel, name, ins, outs, scratch=(), limit=16, work=0, specs=None, out_specs=None, aliases=None):
    moved = sum(x.size * 4 for x in ins) + sum(o.size * 4 for o in outs)
    return pl.pallas_call(
        kernel,
        in_specs=specs or [VMEM] * len(ins),
        out_specs=out_specs or [VMEM] * len(outs),
        out_shape=outs,
        scratch_shapes=list(scratch),
        input_output_aliases=aliases or {},
        compiler_params=pltpu.CompilerParams(vmem_limit_bytes=limit << 20),
        cost_estimate=cost(VECTOR * work, moved),
        name=name,
    )(*ins)


def row_parts(width, height):
    b = place()[1]
    return [pl.multiple_of(part * (width - height), 16) for part in (b, 1 - b)]


def cut_flows_kernel(*refs):
    fields, outs, sems = refs[:-3], refs[-3:-1], refs[-1]
    planes, width, _ = fields[0].shape
    height = outs[0].shape[1]
    moves = []
    for k, field in enumerate(fields):
        for out, low in zip(outs, row_parts(width, height)):
            source, target = field.at[:, pl.ds(low, height)], out.at[pl.ds(k * planes, planes)]
            moves.append(pltpu.make_async_copy(source, target, sems.at[len(moves)]))
            moves[-1].start()
    for move in moves:
        move.wait()


def cut_groups_kernel(height, token_ref, cells_ref, weights_ref, dirs_hbm, *refs):
    outs, after_ref, sems = refs[:-2], refs[-2], refs[-1]
    after_ref[0] = 0
    dirs, planes, width, _ = dirs_hbm.shape
    each = 2 * dirs // len(outs)
    lows = row_parts(width, height)
    moves = []
    for d in range(dirs):
        for p in range(planes):
            at = pl.ds((d % each * planes + p) * height, height)
            for side, low in enumerate(lows):
                source = dirs_hbm.at[d, p, pl.ds(low, height)]
                target = outs[2 * (d // each) + side].at[at]
                moves.append(pltpu.make_async_copy(source, target, sems.at[len(moves)]))
                moves[-1].start()
    low, lines = each * planes * height, cells_ref.shape[0]
    for out in outs[:2]:
        out[low : low + lines, :] = cells_ref[...].astype(jnp.float32)
        out[low + lines : low + 2 * lines, :] = weights_ref[...]
    for move in moves:
        move.wait()


def pack_kernel(planes, held, token_ref, own_ref, other_ref, *refs):
    up_ref, down_ref = refs[held : held + 2]
    count, reach, height, _ = up_ref.shape
    skip = 2 * planes - reach

    def join(first, second):
        for d in range(count):
            for p in range(2 * planes):
                ref = first if p < planes else second
                k = d * planes + p % planes
                value = ref[k] if len(ref.shape) == 3 else ref[k * height : (k + 1) * height, :]
                if p >= skip:
                    up_ref[d, p - skip] = value
                if p < reach:
                    down_ref[d, p] = value

    a = place()[0]

    @pl.when(a == 0)
    def _():
        join(own_ref, other_ref)

    @pl.when(a == 1)
    def _():
        join(other_ref, own_ref)


def sensor_kernel(width, skip, own_ref, other_ref, out_ref, after_ref):
    after_ref[0] = 0
    a = place()[0]
    _, planes, height, _ = out_ref.shape
    first = a * (width - height)
    count = (own_ref.shape[0] - skip) // 2
    group = 4
    chunk = group * LANES
    targets = planes * height
    rows = lax.broadcasted_iota(jnp.int32, (targets, chunk), 0)
    lanes = lax.broadcasted_iota(jnp.int32, (LANES, chunk), 0)
    for ref, at in ((own_ref, a), (other_ref, 1 - a)):
        total = jnp.zeros((targets, 3 * LANES), jnp.float32)
        for k in range(skip, skip + count, group):
            take = lambda at: jnp.concatenate([ref[at + g : at + g + 1, :] for g in range(group)], 1)
            cell = take(k).astype(jnp.int32)
            weight = take(count + k)
            line = cell // LANES
            lane = cell - line * LANES
            plane = line // width
            row = line - plane * width - first
            inside = (row >= 0) & (row < height)
            target = jnp.where(inside, plane * height + row, -1)
            high = weight.astype(jnp.bfloat16).astype(jnp.float32)
            rest = weight - high
            middle = rest.astype(jnp.bfloat16).astype(jnp.float32)
            low = rest - middle
            hot = jnp.where(rows == target, 1.0, 0.0).astype(jnp.bfloat16)
            here = lanes == lane
            parts = [jnp.where(here, part, 0.0).astype(jnp.bfloat16) for part in (high, middle, low)]
            total += lax.dot_general(
                hot,
                jnp.concatenate(parts, 0),
                (((1,), (1,)), ((), ())),
                preferred_element_type=jnp.float32,
            )
        total = total[:, 0:LANES] + total[:, LANES : 2 * LANES] + total[:, 2 * LANES :]
        out_ref[at] = total.reshape(planes, height, LANES)


def arrivals(parts, into, sems):
    up, down, lo, hi = parts
    reach, depth = REACH, into.shape[1]
    own = depth - 2 * reach
    moves = (
        (lo, into.at[:, 0:reach]),
        (down, into.at[:, reach : 2 * reach]),
        (up.at[:, 2 * reach - own : reach], into.at[:, 2 * reach : reach + own]),
        (hi, into.at[:, reach + own : depth]),
    )
    return [pltpu.make_async_copy(s, t, sems.at[k]) for k, (s, t) in enumerate(moves)]


def coefficient_kernel(code_ref, *refs):
    parts, (ahead, behind, inverse_out, flow, sems) = refs[:4], refs[4:]
    _, depth, height, _ = flow.shape
    chunks = height // 8
    own = depth - 2 * REACH
    a, _, at_bottom, at_top = place()
    moves = arrivals(parts, flow, sems)
    for move in moves:
        move.start()

    shape = (8, LANES)
    sub = lax.broadcasted_iota(jnp.int32, shape, 0)
    lane = lax.broadcasted_iota(jnp.int32, shape, 1)
    top_sub, bottom_sub = sub == 7, sub == 0
    last_lane, first_lane = lane == LANES - 1, lane == 0
    opened = [jnp.where(code_ref[k] == 0, 1.0, 0.0).astype(jnp.float32) for k in range(4)]
    low_one = jnp.where(bottom_sub & (a == 0), opened[0], 1.0)
    high_one = jnp.where(top_sub & (a == 1), opened[1], 1.0)
    low_two = jnp.where(first_lane, opened[2], 1.0)
    high_two = jnp.where(last_lane, opened[3], 1.0)

    def both(x):
        positive = DIFFUSION + jnp.maximum(x, 0.0)
        return positive, positive - x

    def at_plane(p, carry):
        outside = ((p < REACH) & at_bottom) | ((p >= REACH + own) & at_top)
        inside = jnp.where(outside, 0.0, 1.0)
        turned = jnp.zeros(shape, jnp.float32)
        for r in range(chunks):
            here = slice(r * 8, r * 8 + 8)
            one, two, three = flow[0, p, here, :], flow[1, p, here, :], flow[2, p, here, :]
            one_turned = pltpu.roll(one, 1, 0)
            one_below = jnp.where(bottom_sub, turned, one_turned)
            turned = one_turned
            two_below = jnp.where(first_lane, 0.0, pltpu.roll(two, 1, 1))
            up = [both(x) for x in (one, two, three)]
            down = [both(x) for x in (one_below, two_below, flow[2, p - 1, here, :])]
            first = up[0][0] if r < chunks - 1 else high_one * up[0][0]
            second = down[0][1] if r > 0 else low_one * down[0][1]
            diagonal = (1.0 + first) + (second + high_two * up[1][0])
            diagonal = diagonal + (low_two * down[1][1] + (up[2][0] + down[2][1]))
            inverse = inside / diagonal
            right, left = jnp.where(last_lane, 0.0, inverse), jnp.where(first_lane, 0.0, inverse)
            for out, w in ((ahead, 1), (behind, 0)):
                out[0, p, here, :] = up[0][w] * inverse
                out[1, p, here, :] = down[0][1 - w] * inverse
                out[2, p, here, :] = up[1][w] * right
                out[3, p, here, :] = down[1][1 - w] * left
                out[4, p, here, :] = up[2][w] * inverse
                out[5, p, here, :] = down[2][1 - w] * inverse
            inverse_out[p, here, :] = inverse
        return carry

    for move in moves:
        move.wait()
    lax.fori_loop(1, depth - 1, at_plane, 0, unroll=2)


def solve_kernel(adjoint, coef, inverse_ref, *refs):
    value_parts = refs[0:4]
    if adjoint:
        outs, (rhs, start, ping, pong, sems) = refs[4:6], refs[6:]
    else:
        weight_ref, outs, (rhs, start, ping, pong, sems) = refs[4], refs[5:7], refs[7:]
    dirs, depth, height, _ = rhs.shape
    reach = REACH
    own = depth - 2 * reach
    chunks = height // 8
    a = place()[0]
    moves = arrivals(value_parts, start, sems)
    for move in moves:
        move.start()

    shape = (8, LANES)
    sub = lax.broadcasted_iota(jnp.int32, shape, 0)
    top_sub, bottom_sub = sub == 7, sub == 0
    zero = jnp.zeros(shape, jnp.float32)

    def sweep(source, lead, low, planes, offset, count, store):
        def rows(r):
            return pl.ds(offset + r * 8, 8)

        def at_planes(k, carry):
            p = low + 2 * k
            each = [(q, d) for q in range(2) for d in range(dirs)]
            value = {(q, d): source[d, p + q, rows(0), :] for q, d in each}
            up = {e: pltpu.roll(v, 7, 0) for e, v in value.items()}
            down = {e: pltpu.roll(v, 1, 0) for e, v in value.items()}
            before = dict.fromkeys(each, zero)
            if count < chunks:
                at = pl.multiple_of(jnp.maximum(offset - 8, 0), 8)
                for q, d in each:
                    outer = pltpu.roll(source[d, p + q, pl.ds(at, 8), :], 1, 0)
                    before[q, d] = jnp.where(a == 0, 0.0, outer)
            for r in range(count):
                c = [[coef[m, p + q, rows(r), :] for m in range(6)] for q in range(2)]
                inverse = [inverse_ref[p + q, rows(r), :] for q in range(2)] if lead else None
                plane = {d: [source[d, p - 1, rows(r), :], value[0, d], value[1, d], source[d, p + 2, rows(r), :]] for d in range(dirs)}
                for q, d in each:
                    here = value[q, d]
                    if r + 1 < count:
                        following = source[d, p + q, rows(r + 1), :]
                        next_up, next_down = pltpu.roll(following, 7, 0), pltpu.roll(following, 1, 0)
                    elif count < chunks:
                        at = pl.multiple_of(jnp.minimum(offset + count * 8, height - 8), 8)
                        following = source[d, p + q, pl.ds(at, 8), :]
                        next_up, next_down = jnp.where(a == 1, 0.0, pltpu.roll(following, 7, 0)), zero
                    else:
                        following, next_up, next_down = zero, zero, zero
                    if lead:
                        total = here * inverse[q]
                        rhs[d, p + q, rows(r), :] = total
                    else:
                        total = rhs[d, p + q, rows(r), :]
                    depth_sum = c[q][4] * plane[d][q + 2] + c[q][5] * plane[d][q]
                    first_sum = c[q][0] * jnp.where(top_sub, next_up, up[q, d])
                    first_sum = first_sum + c[q][1] * jnp.where(bottom_sub, before[q, d], down[q, d])
                    second_sum = c[q][2] * pltpu.roll(here, LANES - 1, 1) + c[q][3] * pltpu.roll(here, 1, 1)
                    total = (total + depth_sum) + (first_sum + second_sum)
                    store(d, p + q, rows(r), r, total)
                    value[q, d], up[q, d], before[q, d], down[q, d] = (
                        following, next_up, down[q, d], next_down
                    )
            return carry

        lax.fori_loop(0, planes // 2, at_planes, 0)

    def into(ref):
        def store(d, p, here, r, total):
            ref[d, p, here, :] = total

        return store

    def again(d, p, here, r, total):
        start[d, p, here, :] = total if adjoint else total + start[d, p, here, :]

    def full(source, lead, step, store):
        sweep(source, lead, 1 + step, depth - 2 - 2 * step, 0, chunks, store)

    low = 1
    for move, present in zip(moves, (reach, 2 * reach, reach + own, depth)):
        move.wait()
        ready = (present - 1 - low) // 2 * 2
        sweep(start, True, low, ready, 0, chunks, into(ping))
        low += ready
    full(ping, False, 1, into(pong))
    full(pong, False, 2, again)
    full(start, True, 3, into(ping))
    full(ping, False, 4, into(pong))

    half = own // 2
    if adjoint:
        for out, side in zip(outs, (a, 1 - a)):
            low = reach + side * half

            def finish(d, p, here, r, total, out=out, low=low):
                out[d, p - low, r * 8 : r * 8 + 8, :] = total + start[d, p, here, :]

            shift = pl.multiple_of(a * SPARE, 8)
            sweep(pong, False, low, half, shift, (height - SPARE) // 8, finish)
    else:
        up_out, down_out = outs

        def emit(kinds):
            def finish(d, p, here, r, total):
                i = p - reach
                total = total * weight_ref[i // half, i % half, here, :]
                if "d" in kinds:
                    down_out[d, i, here, :] = total
                if "u" in kinds:
                    up_out[d, i - (own - reach), here, :] = total

            return finish

        for low, high, kinds in ((0, own - reach, "d"), (own - reach, reach, "du"), (reach, own, "u")):
            sweep(pong, False, reach + low, high - low, 0, chunks, emit(kinds))


def solves(adjoint, planes, coefficients, values, weight=None):
    dirs, reach, height, _ = values[0].shape
    depth = 2 * planes + 2 * reach
    ahead, behind, inverse = coefficients
    ins = [behind if adjoint else ahead, inverse, *values]
    specs = [VMEM] * 2 + [ANY] * 4
    if adjoint:
        outs = [floats(dirs, planes, height - SPARE, LANES)] * 2
    else:
        ins.append(weight)
        specs.append(VMEM)
        outs = [floats(*values[0].shape)] * 2
    scratch = [pltpu.VMEM((dirs, depth, height, LANES), jnp.float32)] * 4
    return call(
        functools.partial(solve_kernel, adjoint),
        "adjoint" if adjoint else "forward",
        ins, outs, scratch + [pltpu.SemaphoreType.DMA((4,))],
        28, 6 * 16 * dirs * depth * height * LANES, specs,
    )


def body(
    directions,
    eigen_basis,
    flow_first,
    flow_second,
    flow_depth,
    face_codes,
    sensor_cells,
    sensor_weight,
):
    dirs, planes, width, _ = directions.shape
    rank = eigen_basis.shape[0]
    count = lax.axis_size("slab")
    height = width // 2 + SPARE
    depth = 2 * planes + 2 * REACH
    own, other, above = quad(count)
    each = dirs // GROUPS
    block = planes * height

    def regroup(first, second):
        return lax.ppermute(first, "slab", own), lax.ppermute(second, "slab", other)

    def beyond(up, down):
        return up, down, lax.ppermute(up, "slab", above), lax.ppermute(down, "slab", back(above))

    def pack(token, pair, parts, held=()):
        outs = [floats(parts, REACH, height, LANES)] * 2 + [floats(*h.shape) for h in held]
        n = len(held)
        found = call(
            functools.partial(pack_kernel, planes, n), "pack", [token, *pair, *held], outs,
            specs=[SMEM, VMEM, VMEM] + [ANY] * n, out_specs=[VMEM] * 2 + [ANY] * n,
            aliases={3 + k: 2 + k for k in range(n)},
        )
        return found[:2], found[2:]

    fields = [flow_first, flow_second, flow_depth]
    flows = regroup(*call(
        cut_flows_kernel, "cut", fields, [floats(len(fields) * planes, height, LANES)] * 2,
        [pltpu.SemaphoreType.DMA((2 * len(fields),))], 54, 0, [ANY] * len(fields),
    ))
    basis = eigen_basis.reshape(rank, planes * width, LANES)
    tile, token = gram_tile(basis)
    sensors = [x.reshape(-1, LANES) for x in (sensor_cells, sensor_weight)]
    listed = 2 * sensors[0].shape[0]
    lines = [each * block + (listed if k == 0 else 0) for k in range(GROUPS)]
    *cuts, token = call(
        functools.partial(cut_groups_kernel, height), "cut", [token, *sensors, directions],
        [floats(n, LANES) for n in lines for _ in range(2)] + [TOKEN],
        [pltpu.SemaphoreType.DMA((2 * dirs * planes,))], 54, 0, [SMEM, VMEM, VMEM, ANY],
        [VMEM] * (2 * GROUPS) + [SMEM],
    )
    moved = [regroup(*cuts[:2])]
    flows, cuts = pack(token, flows, len(fields), cuts[2:])
    flows = beyond(*flows)
    moved += [regroup(*cuts[k : k + 2]) for k in range(0, len(cuts), 2)]
    weight, later = call(
        functools.partial(sensor_kernel, width, each * block), "sensors", [*moved[0]],
        [floats(2, planes, height, LANES), TOKEN],
        work=block * listed * 20, out_specs=[VMEM, SMEM],
    )
    tokens = [token] + [later] * (GROUPS - 1)
    values = [beyond(*pack(t, m, each)[0]) for t, m in zip(tokens, moved)]
    coefficients = call(
        coefficient_kernel, "coefficients", [face_codes, *flows],
        [floats(6, depth, height, LANES)] * 2 + [floats(depth, height, LANES)],
        [pltpu.VMEM((3, depth, height, LANES), jnp.float32), pltpu.SemaphoreType.DMA((4,))],
        26, 80 * depth * height * LANES, [SMEM] + [ANY] * 4,
    )
    forcing = [beyond(*solves(False, planes, coefficients, v, weight)) for v in values]
    summed = [solves(True, planes, coefficients, f) for f in forcing]
    returned = [
        (lax.ppermute(s[0], "slab", back(own)), lax.ppermute(s[1], "slab", back(other)))
        for s in summed
    ]
    images = []
    for k, halves in enumerate(returned):
        copies = count if k == GROUPS - 1 else 1
        tile, image, basis = projections(basis, directions, k * each, halves, tile, copies)
        images.append(image)
    cells = planes * count * width * LANES
    new, coeffs, scales, again = remainders(spread(tile, count), basis, images, cells)
    new, _ = lax.while_loop(
        lambda state: state[1] > 0,
        lambda state: (rescaled(state[0], scales, cells, count), jnp.int32(0)),
        (new, again[0]),
    )
    return (new.reshape(directions.shape), coeffs.T)


def solution(mesh):
    return jax.shard_map(
        body,
        mesh=mesh,
        in_specs=(
            P("grp", "slab", None, None),
            P("grp", "slab", None, None),
            P("slab", None, None),
            P("slab", None, None),
            P("slab", None, None),
            P(),
            P(("grp", "slab")),
            P(("grp", "slab")),
        ),
        out_specs=(P("grp", "slab", None, None), P("grp", None)),
        check_vma=False,
    )
```

```python
import functools

import jax
import jax.numpy as jnp
from jax import lax
from jax.experimental import pallas as pl
from jax.experimental.pallas import tpu as pltpu
from jax.sharding import PartitionSpec as P

STEPS = 2
SWEEPS = 3
GROUPS = 2
SPARE = 16
REACH = STEPS * SWEEPS


DIFFUSION = 0.2
GAMMA = 0.5
LANES = 128
PIECES = 8
EXACT = lax.Precision.HIGHEST
SMEM = pl.BlockSpec(memory_space=pltpu.SMEM)
VMEM = pl.BlockSpec(memory_space=pltpu.VMEM)
ANY = pl.BlockSpec(memory_space=pl.ANY)
VECTOR = 150


def place():
    me, count = lax.axis_index("slab"), lax.axis_size("slab")
    a, b = lax.rem(me // 2, 2), lax.rem(me, 2)
    return a, b, me - 2 * a == 0, me + 2 * (1 - a) == count - 1


def floats(*shape):
    return jax.ShapeDtypeStruct(shape, jnp.float32)


def cost(flops, moved):
    return pl.CostEstimate(flops=int(flops), bytes_accessed=int(moved), transcendentals=0)


def lane_sums(stack):
    ones = jnp.ones((8, LANES), jnp.float32)
    return lax.dot_general(
        ones, stack, (((1,), (1,)), ((), ())), precision=EXACT, preferred_element_type=jnp.float32
    )


def chunks_of(source, into, sems, pieces):
    rows = source.shape[1] // pieces
    return [
        pltpu.make_async_copy(
            source.at[:, pl.ds(k * rows, rows)], into.at[:, pl.ds(k * rows, rows)], sems.at[k]
        )
        for k in range(pieces)
    ]


def gram_kernel(basis_hbm, out_ref, after_ref, basis_ref, acc_ref, sems):
    rank, rows, _ = basis_ref.shape
    tile = 4
    moves = chunks_of(basis_hbm, basis_ref, sems, PIECES)
    for move in moves:
        move.start()
    after_ref[0] = 0
    acc_ref[...] = jnp.zeros_like(acc_ref)
    part = rows // PIECES
    for piece, move in enumerate(moves):
        move.wait()
        for i0 in range(0, rank, tile):
            for j0 in range(i0, rank, tile):
                pairs = [(i, j) for i in range(i0, i0 + tile) for j in range(j0, j0 + tile) if i <= j]

                def add(k, sums, i0=i0, j0=j0, pairs=pairs, piece=piece):
                    at = pl.ds(pl.multiple_of(piece * part + k * 8, 8), 8)
                    left = {i: basis_ref[i, at, :] for i in range(i0, i0 + tile)}
                    right = left if i0 == j0 else {j: basis_ref[j, at, :] for j in range(j0, j0 + tile)}
                    return [s + left[i] * right[j] for s, (i, j) in zip(sums, pairs)]

                sums = [jnp.zeros((8, LANES), jnp.float32) for _ in pairs]
                sums = lax.fori_loop(0, part // 8, add, sums, unroll=8)
                for (i, j), s in zip(pairs, sums):
                    acc_ref[i, j] += s

    row = lax.broadcasted_iota(jnp.int32, (rank, rank), 0)
    col = lax.broadcasted_iota(jnp.int32, (rank, rank), 1)
    gram = jnp.zeros((rank, rank), jnp.float32)
    for i in range(rank):
        sums = lane_sums(jnp.sum(acc_ref[i], axis=1))
        gram = jnp.where(row == i, jnp.broadcast_to(sums[0:1, :], (rank, rank)), gram)
    upper = jnp.where(col >= row, gram, 0.0)
    strict = jnp.where(col > row, gram, 0.0)
    whole = upper + strict.T
    out_ref[...] = jnp.zeros_like(out_ref)
    for k in range(0, rank, 8):
        at = 2 * rank + k * rank // 8
        out_ref[:, at : at + rank] = whole[k : k + 8]


TOKEN = jax.ShapeDtypeStruct((1,), jnp.int32)


def gram_tile(basis):
    rank, rows, _ = basis.shape
    return call(
        gram_kernel, "gram", [basis], [floats(8, LANES), TOKEN],
        [
            pltpu.VMEM(basis.shape, jnp.float32),
            pltpu.VMEM((rank, rank, 8, LANES), jnp.float32),
            pltpu.SemaphoreType.DMA((PIECES,)),
        ],
        54, rank * rank * rows * LANES, [ANY], [VMEM, SMEM],
    )


def spread(tile, count):
    return lax.all_to_all(tile, "slab", 0, 0, tiled=True) if count > 1 else tile


def projection_kernel(first, basis_in, dirs_hbm, own_hbm, other_hbm, tile_ref, out_ref, image_ref, *refs):
    moves = None
    if first == 0:
        basis_ref, dirs_ref, halves_ref, side_sems, sems = refs
        moves = chunks_of(basis_in, basis_ref, sems, PIECES)
    else:
        basis_ref, (dirs_ref, halves_ref, side_sems) = basis_in, refs
    rank = basis_ref.shape[0]
    dirs, rows, _ = image_ref.shape
    planes, half = halves_ref.shape[2:4]
    b = place()[1]
    sides = [
        pltpu.make_async_copy(own_hbm, halves_ref.at[0], side_sems.at[0]),
        pltpu.make_async_copy(other_hbm, halves_ref.at[1], side_sems.at[1]),
        pltpu.make_async_copy(dirs_hbm.at[pl.ds(first, dirs)], dirs_ref, side_sems.at[2]),
    ]
    for move in sides + (moves or []):
        move.start()
    for move in sides:
        move.wait()
    sums = [jnp.zeros((8, LANES), jnp.float32) for _ in range((rank + 1) * dirs)]
    piece = rows // PIECES
    for k in range(2 * planes):
        plane, part = k // 2, k % 2
        which = jnp.where(b == part, 0, 1)
        low = k * half
        if moves:
            for m in range(-(-low // piece), -(-(low + half) // piece)):
                moves[m].wait()

        def add(r, sums, plane=plane, which=which, low=low):
            at = pl.ds(pl.multiple_of(low + r * 8, 8), 8)
            here = pl.ds(pl.multiple_of(r * 8, 8), 8)
            image = []
            for d in range(dirs):
                value = halves_ref[which, d, plane, here, :] + GAMMA * dirs_ref[d, at, :]
                image_ref[d, at, :] = value
                image.append(value)
            out = []
            for i in range(rank):
                q = basis_ref[i, at, :]
                out += [sums[i * dirs + d] + q * image[d] for d in range(dirs)]
            return out + [sums[rank * dirs + d] + image[d] * image[d] for d in range(dirs)]

        sums = lax.fori_loop(0, half // 8, add, sums, unroll=4)

    row = lax.broadcasted_iota(jnp.int32, (8, LANES), 0)
    lane = lax.broadcasted_iota(jnp.int32, (8, LANES), 1)
    lines = [sums[i * dirs + d] for d in range(dirs) for i in range(rank)] + sums[rank * dirs :]
    lines = [jnp.sum(line, axis=0, keepdims=True) for line in lines]
    lines.append(jnp.zeros((LANES - len(lines), LANES), jnp.float32))
    found = lane_sums(jnp.concatenate(lines, 0))
    table = tile_ref[...]
    squares = pltpu.roll(found, (rank + first - rank * dirs) % LANES, 1)
    for d in range(dirs):
        products = pltpu.roll(found, (LANES - d * rank) % LANES, 1) if d else found
        table = jnp.where((row == first + d) & (lane < rank), products, table)
        table = jnp.where((row == first + d) & (lane == rank + first + d), squares, table)
    for r in range(out_ref.shape[0] // 8):
        out_ref[r * 8 : (r + 1) * 8, :] = table


def projections(basis, directions, first, halves, tile, count):
    rank, rows, _ = basis.shape
    dirs = halves[0].shape[0]
    outs = [floats(count * 8, LANES), floats(dirs, rows, LANES)]
    scratch = [
        pltpu.VMEM((dirs, rows, LANES), jnp.float32),
        pltpu.VMEM((2, *halves[0].shape), jnp.float32),
        pltpu.SemaphoreType.DMA((3,)),
    ]
    if first == 0:
        outs.append(floats(*basis.shape))
        scratch.append(pltpu.SemaphoreType.DMA((PIECES,)))
    found = call(
        functools.partial(projection_kernel, first), "projections",
        [basis, directions.reshape(-1, rows, LANES), *halves, tile],
        outs, scratch, 24, 2 * rank * dirs * rows * LANES,
        [ANY if first == 0 else VMEM] + [ANY] * 3 + [VMEM],
    )
    return (*found, basis)[:3] if first else found


def summed_tile(parts_ref):
    tiles = [parts_ref[r : r + 8, :] for r in range(0, parts_ref.shape[0], 8)]
    while len(tiles) > 1:
        tiles = [sum(tiles[k : k + 2]) for k in range(0, len(tiles), 2)]
    return tiles[0]


def eliminated(tile, rank):
    gram = [tile[:, 2 * rank + k * rank // 8 :][:, :rank] for k in range(0, rank, 8)]
    lane = lax.broadcasted_iota(jnp.int32, (8, LANES), 1)
    table = jnp.concatenate(
        [
            jnp.concatenate(gram, 0),
            tile[:, 0:rank].T,
            jnp.zeros((rank, LANES - rank - 8), jnp.float32),
        ],
        1,
    )
    table = jnp.concatenate([table, jnp.where(lane < rank + 8, tile, 0.0)], 0)
    row = lax.broadcasted_iota(jnp.int32, table.shape, 0)
    for k in range(rank):
        pivot_row = table[k : k + 1, :] / table[k : k + 1, k : k + 1]
        table = jnp.where(row == k, pivot_row, table - table[:, k : k + 1] * pivot_row)
    return table


def inverse_root(value):
    root = lax.rsqrt(value)
    return root * (1.5 - (0.5 * value * root) * root)


def remainder_kernel(dirs, cells, parts_ref, basis_ref, *refs):
    groups = len(refs) - 8
    images = refs[:groups]
    new_hbm, coeffs_ref, scale_out, again_ref, rem_ref, splat_ref, scale_ref, sems = refs[groups:]
    each = dirs // groups
    rank, rows, _ = basis_ref.shape
    tile = 4
    first = summed_tile(parts_ref)
    table = eliminated(first, rank)
    coeffs_ref[...] = table[0:rank, rank : rank + 8].T[0:dirs]
    for d in range(dirs):
        for j in range(rank):
            splat_ref[d * rank + j] = jnp.broadcast_to(
                table[j : j + 1, rank + d : rank + d + 1], (8, LANES)
            )
    row = lax.broadcasted_iota(jnp.int32, (8, LANES), 0)
    lane = lax.broadcasted_iota(jnp.int32, (8, LANES), 1)
    energy, square = table[rank : rank + 8, :], first
    unsure = (lane == rank + row) & (row < dirs) & jnp.logical_not(energy >= 0.01 * square)
    again_ref[0] = jnp.max(jnp.where(unsure, 1.0, 0.0)).astype(jnp.int32)
    scale = inverse_root(jnp.maximum(energy, 0.0) / cells + 1e-06)
    scales = jnp.zeros((8, LANES), jnp.float32)
    for d in range(dirs):
        one = jnp.broadcast_to(scale[d : d + 1, rank + d : rank + d + 1], (8, LANES))
        scale_ref[d] = one
        scales = jnp.where(row == d, one, scales)
    scale_out[...] = scales
    part = rows // PIECES
    moves = []
    for piece in range(PIECES):
        for j0 in range(0, rank, tile):
            last = j0 + tile == rank
            weights = [[splat_ref[d * rank + j] for j in range(j0, j0 + tile)] for d in range(dirs)]
            scale = [scale_ref[d] for d in range(dirs)] if last else None

            def take(k, carry, j0=j0, last=last, weights=weights, scale=scale, piece=piece):
                at = pl.ds(pl.multiple_of(piece * part + k * 8, 8), 8)
                basis = [basis_ref[j, at, :] for j in range(j0, j0 + tile)]
                for d in range(dirs):
                    left = images[d // each][d % each, at, :] if j0 == 0 else rem_ref[d, at, :]
                    parts = [w * q for w, q in zip(weights[d], basis)]
                    left = left - ((parts[0] + parts[1]) + (parts[2] + parts[3]))
                    rem_ref[d, at, :] = left * scale[d] if last else left
                return carry

            lax.fori_loop(0, part // 8, take, 0, unroll=4)
        at = pl.ds(piece * part, part)
        moves.append(pltpu.make_async_copy(rem_ref.at[:, at], new_hbm.at[:, at], sems.at[piece]))
        moves[-1].start()
    for move in moves:
        move.wait()


def remainders(parts, basis, images, cells):
    rank, rows, _ = basis.shape
    dirs = sum(i.shape[0] for i in images)
    return call(
        functools.partial(remainder_kernel, dirs, cells), "remainder", [parts, basis, *images],
        [
            floats(dirs, rows, LANES),
            floats(dirs, rank),
            floats(8, LANES),
            TOKEN,
        ],
        [
            pltpu.VMEM((dirs, rows, LANES), jnp.float32),
            pltpu.VMEM((dirs * rank, 8, LANES), jnp.float32),
            pltpu.VMEM((dirs, 8, LANES), jnp.float32),
            pltpu.SemaphoreType.DMA((PIECES,)),
        ],
        24, 2 * rank * dirs * rows * LANES, out_specs=[ANY, VMEM, VMEM, SMEM],
    )


def squares_kernel(new_ref, out_ref, sum_ref):
    dirs = new_ref.shape[0]
    row = lax.broadcasted_iota(jnp.int32, (8, LANES), 0)

    @pl.when(pl.program_id(0) == 0)
    def _():
        sum_ref[...] = jnp.zeros_like(sum_ref)

    for d in range(dirs):
        lines = jnp.sum(new_ref[d] * new_ref[d], axis=0, keepdims=True)
        total = jnp.broadcast_to(jnp.sum(lines, axis=1, keepdims=True), (8, LANES))
        sum_ref[...] += jnp.where(row == d, total, 0.0)
    for r in range(out_ref.shape[0] // 8):
        out_ref[r * 8 : (r + 1) * 8, :] = sum_ref[...]


def rescale_kernel(cells, parts_ref, scale_ref, new_ref, out_ref):
    scale = scale_ref[...]
    energy = summed_tile(parts_ref) / scale / scale
    ratio = inverse_root(energy / cells + 1e-06) / scale
    for d in range(new_ref.shape[0]):
        out_ref[d] = new_ref[d] * ratio[d : d + 1, :]


def rescaled(new, scales, cells, count):
    dirs, rows, _ = new.shape
    chunk = 128
    lines = pl.BlockSpec((dirs, chunk, LANES), lambda k: (0, k, 0))
    whole = lambda n: pl.BlockSpec((n, LANES), lambda k: (0, 0))
    parts = pl.pallas_call(
        squares_kernel,
        grid=(rows // chunk,),
        in_specs=[lines],
        out_specs=whole(count * 8),
        out_shape=floats(count * 8, LANES),
        scratch_shapes=[pltpu.VMEM((8, LANES), jnp.float32)],
        compiler_params=pltpu.CompilerParams(vmem_limit_bytes=16 << 20),
        name="squares",
    )(new)
    return pl.pallas_call(
        functools.partial(rescale_kernel, cells),
        grid=(rows // chunk,),
        in_specs=[whole(count * 8), whole(8), lines],
        out_specs=lines,
        out_shape=floats(dirs, rows, LANES),
        compiler_params=pltpu.CompilerParams(vmem_limit_bytes=16 << 20),
        name="rescale",
    )(spread(parts, count), scales, new)


def quad(count):
    own, other, above = [], [], []
    for s in range(count):
        q, a, b = s // 4, s // 2 % 2, s % 2
        own.append((s, 4 * q + 2 * b + a))
        other.append((s, 4 * q + 2 * (1 - b) + a))
        up = s + 1 if b == 0 else s + 3
        if up < count:
            above.append((s, up))
    return own, other, above


def back(pairs):
    return [(target, source) for source, target in pairs]


def call(kernel, name, ins, outs, scratch=(), limit=16, work=0, specs=None, out_specs=None):
    moved = sum(x.size * 4 for x in ins) + sum(o.size * 4 for o in outs)
    return pl.pallas_call(
        kernel,
        in_specs=specs or [VMEM] * len(ins),
        out_specs=out_specs or [VMEM] * len(outs),
        out_shape=outs,
        scratch_shapes=list(scratch),
        compiler_params=pltpu.CompilerParams(vmem_limit_bytes=limit << 20),
        cost_estimate=cost(VECTOR * work, moved),
        name=name,
    )(*ins)


def row_parts(width, height):
    b = place()[1]
    return [pl.multiple_of(part * (width - height), 16) for part in (b, 1 - b)]


def cut_flows_kernel(*refs):
    fields, outs, sems = refs[:-3], refs[-3:-1], refs[-1]
    planes, width, _ = fields[0].shape
    height = outs[0].shape[1]
    moves = []
    for k, field in enumerate(fields):
        for out, low in zip(outs, row_parts(width, height)):
            source, target = field.at[:, pl.ds(low, height)], out.at[pl.ds(k * planes, planes)]
            moves.append(pltpu.make_async_copy(source, target, sems.at[len(moves)]))
            moves[-1].start()
    for move in moves:
        move.wait()


def cut_group_kernel(height, group, token_ref, *refs):
    sensors, (dirs_hbm, *outs, after_ref, sems) = refs[:-5], refs[-5:]
    after_ref[0] = 0
    _, planes, width, _ = dirs_hbm.shape
    moves, k = [], 0
    lows = row_parts(width, height)
    for d in group:
        for p in range(planes):
            for out, low in zip(outs, lows):
                source, target = dirs_hbm.at[d, p, pl.ds(low, height)], out.at[pl.ds(k, height)]
                moves.append(pltpu.make_async_copy(source, target, sems.at[len(moves)]))
                moves[-1].start()
            k += height
    for ref in sensors:
        lines = ref.shape[0]
        for out in outs:
            out[k : k + lines, :] = ref[...].astype(jnp.float32)
        k += lines
    for move in moves:
        move.wait()


def pack_kernel(planes, token_ref, own_ref, other_ref, up_ref, down_ref):
    count, reach, height, _ = up_ref.shape
    skip = 2 * planes - reach

    def join(first, second):
        for d in range(count):
            for p in range(2 * planes):
                ref = first if p < planes else second
                k = d * planes + p % planes
                value = ref[k] if len(ref.shape) == 3 else ref[k * height : (k + 1) * height, :]
                if p >= skip:
                    up_ref[d, p - skip] = value
                if p < reach:
                    down_ref[d, p] = value

    a = place()[0]

    @pl.when(a == 0)
    def _():
        join(own_ref, other_ref)

    @pl.when(a == 1)
    def _():
        join(other_ref, own_ref)


def sensor_kernel(width, skip, own_ref, other_ref, out_ref, after_ref):
    after_ref[0] = 0
    a = place()[0]
    _, planes, height, _ = out_ref.shape
    first = a * (width - height)
    count = (own_ref.shape[0] - skip) // 2
    group = 4
    chunk = group * LANES
    targets = planes * height
    rows = lax.broadcasted_iota(jnp.int32, (targets, chunk), 0)
    lanes = lax.broadcasted_iota(jnp.int32, (LANES, chunk), 0)
    for ref, at in ((own_ref, a), (other_ref, 1 - a)):
        total = jnp.zeros((targets, 3 * LANES), jnp.float32)
        for k in range(skip, skip + count, group):
            take = lambda at: jnp.concatenate([ref[at + g : at + g + 1, :] for g in range(group)], 1)
            cell = take(k).astype(jnp.int32)
            weight = take(count + k)
            line = cell // LANES
            lane = cell - line * LANES
            plane = line // width
            row = line - plane * width - first
            inside = (row >= 0) & (row < height)
            target = jnp.where(inside, plane * height + row, -1)
            high = weight.astype(jnp.bfloat16).astype(jnp.float32)
            rest = weight - high
            middle = rest.astype(jnp.bfloat16).astype(jnp.float32)
            low = rest - middle
            hot = jnp.where(rows == target, 1.0, 0.0).astype(jnp.bfloat16)
            here = lanes == lane
            parts = [jnp.where(here, part, 0.0).astype(jnp.bfloat16) for part in (high, middle, low)]
            total += lax.dot_general(
                hot,
                jnp.concatenate(parts, 0),
                (((1,), (1,)), ((), ())),
                preferred_element_type=jnp.float32,
            )
        total = total[:, 0:LANES] + total[:, LANES : 2 * LANES] + total[:, 2 * LANES :]
        out_ref[at] = total.reshape(planes, height, LANES)


def arrivals(parts, into, sems):
    up, down, lo, hi = parts
    reach, depth = REACH, into.shape[1]
    own = depth - 2 * reach
    moves = (
        (lo, into.at[:, 0:reach]),
        (down, into.at[:, reach : 2 * reach]),
        (up.at[:, 2 * reach - own : reach], into.at[:, 2 * reach : reach + own]),
        (hi, into.at[:, reach + own : depth]),
    )
    return [pltpu.make_async_copy(s, t, sems.at[k]) for k, (s, t) in enumerate(moves)]


def coefficients(adjoint, code_ref, flow, coef):
    _, depth, height, _ = flow.shape
    chunks = height // 8
    own = depth - 2 * REACH
    a, _, at_bottom, at_top = place()
    shape = (8, LANES)
    sub = lax.broadcasted_iota(jnp.int32, shape, 0)
    lane = lax.broadcasted_iota(jnp.int32, shape, 1)
    top_sub, bottom_sub = sub == 7, sub == 0
    last_lane, first_lane = lane == LANES - 1, lane == 0
    opened = [jnp.where(code_ref[k] == 0, 1.0, 0.0).astype(jnp.float32) for k in range(4)]
    low_one = jnp.where(bottom_sub & (a == 0), opened[0], 1.0)
    high_one = jnp.where(top_sub & (a == 1), opened[1], 1.0)
    low_two = jnp.where(first_lane, opened[2], 1.0)
    high_two = jnp.where(last_lane, opened[3], 1.0)

    def both(x):
        positive = DIFFUSION + jnp.maximum(x, 0.0)
        return positive, positive - x

    def at_plane(p, carry):
        outside = ((p < REACH) & at_bottom) | ((p >= REACH + own) & at_top)
        inside = jnp.where(outside, 0.0, 1.0)
        turned = jnp.zeros(shape, jnp.float32)
        for r in range(chunks):
            here = slice(r * 8, r * 8 + 8)
            one, two, three = flow[0, p, here, :], flow[1, p, here, :], flow[2, p, here, :]
            one_turned = pltpu.roll(one, 1, 0)
            one_below = jnp.where(bottom_sub, turned, one_turned)
            turned = one_turned
            two_below = jnp.where(first_lane, 0.0, pltpu.roll(two, 1, 1))
            up = [both(x) for x in (one, two, three)]
            down = [both(x) for x in (one_below, two_below, flow[2, p - 1, here, :])]
            first = up[0][0] if r < chunks - 1 else high_one * up[0][0]
            second = down[0][1] if r > 0 else low_one * down[0][1]
            diagonal = (1.0 + first) + (second + high_two * up[1][0])
            diagonal = diagonal + (low_two * down[1][1] + (up[2][0] + down[2][1]))
            inverse = inside / diagonal
            which = 0 if adjoint else 1
            coef[0, p, here, :] = up[0][which] * inverse
            coef[1, p, here, :] = down[0][1 - which] * inverse
            coef[2, p, here, :] = jnp.where(last_lane, 0.0, up[1][which] * inverse)
            coef[3, p, here, :] = jnp.where(first_lane, 0.0, down[1][1 - which] * inverse)
            coef[4, p, here, :] = up[2][which] * inverse
            coef[5, p, here, :] = down[2][1 - which] * inverse
            coef[6, p, here, :] = inverse
        return carry

    lax.fori_loop(1, depth - 1, at_plane, 0, unroll=2)


def solve_kernel(adjoint, code_ref, *refs):
    weight_ref = None if adjoint else refs[8]
    refs = refs[:8] + refs[8 if adjoint else 9 :]
    flow_parts, value_parts, outs = refs[0:4], refs[4:8], refs[8:10]
    flow, coef, rhs, start, ping, pong, flow_sems, sems = refs[10:]
    dirs, depth, height, _ = rhs.shape
    reach = REACH
    own = depth - 2 * reach
    chunks = height // 8
    a = place()[0]
    flow_moves = arrivals(flow_parts, flow, flow_sems)
    moves = arrivals(value_parts, start, sems)
    for move in flow_moves + moves:
        move.start()
    for move in flow_moves:
        move.wait()
    coefficients(adjoint, code_ref, flow, coef)

    shape = (8, LANES)
    sub = lax.broadcasted_iota(jnp.int32, shape, 0)
    top_sub, bottom_sub = sub == 7, sub == 0
    zero = jnp.zeros(shape, jnp.float32)

    def sweep(source, lead, low, planes, offset, count, store):
        def rows(r):
            return pl.ds(offset + r * 8, 8)

        def at_planes(k, carry):
            p = low + 2 * k
            each = [(q, d) for q in range(2) for d in range(dirs)]
            value = {(q, d): source[d, p + q, rows(0), :] for q, d in each}
            up = {e: pltpu.roll(v, 7, 0) for e, v in value.items()}
            down = {e: pltpu.roll(v, 1, 0) for e, v in value.items()}
            before = dict.fromkeys(each, zero)
            if count < chunks:
                at = pl.multiple_of(jnp.maximum(offset - 8, 0), 8)
                for q, d in each:
                    outer = pltpu.roll(source[d, p + q, pl.ds(at, 8), :], 1, 0)
                    before[q, d] = jnp.where(a == 0, 0.0, outer)
            for r in range(count):
                c = [[coef[m, p + q, rows(r), :] for m in range(6)] for q in range(2)]
                inverse = [coef[6, p + q, rows(r), :] for q in range(2)] if lead else None
                plane = {d: [source[d, p - 1, rows(r), :], value[0, d], value[1, d], source[d, p + 2, rows(r), :]] for d in range(dirs)}
                for q, d in each:
                    here = value[q, d]
                    if r + 1 < count:
                        following = source[d, p + q, rows(r + 1), :]
                        next_up, next_down = pltpu.roll(following, 7, 0), pltpu.roll(following, 1, 0)
                    elif count < chunks:
                        at = pl.multiple_of(jnp.minimum(offset + count * 8, height - 8), 8)
                        following = source[d, p + q, pl.ds(at, 8), :]
                        next_up, next_down = jnp.where(a == 1, 0.0, pltpu.roll(following, 7, 0)), zero
                    else:
                        following, next_up, next_down = zero, zero, zero
                    if lead:
                        total = here * inverse[q]
                        rhs[d, p + q, rows(r), :] = total
                    else:
                        total = rhs[d, p + q, rows(r), :]
                    depth_sum = c[q][4] * plane[d][q + 2] + c[q][5] * plane[d][q]
                    first_sum = c[q][0] * jnp.where(top_sub, next_up, up[q, d])
                    first_sum = first_sum + c[q][1] * jnp.where(bottom_sub, before[q, d], down[q, d])
                    second_sum = c[q][2] * pltpu.roll(here, LANES - 1, 1) + c[q][3] * pltpu.roll(here, 1, 1)
                    total = (total + depth_sum) + (first_sum + second_sum)
                    store(d, p + q, rows(r), r, total)
                    value[q, d], up[q, d], before[q, d], down[q, d] = (
                        following, next_up, down[q, d], next_down
                    )
            return carry

        lax.fori_loop(0, planes // 2, at_planes, 0)

    def into(ref):
        def store(d, p, here, r, total):
            ref[d, p, here, :] = total

        return store

    def again(d, p, here, r, total):
        start[d, p, here, :] = total if adjoint else total + start[d, p, here, :]

    def full(source, lead, step, store):
        sweep(source, lead, 1 + step, depth - 2 - 2 * step, 0, chunks, store)

    for move in moves:
        move.wait()
    full(start, True, 0, into(ping))
    full(ping, False, 1, into(pong))
    full(pong, False, 2, again)
    full(start, True, 3, into(ping))
    full(ping, False, 4, into(pong))

    half = own // 2
    if adjoint:
        for out, side in zip(outs, (a, 1 - a)):
            low = reach + side * half

            def finish(d, p, here, r, total, out=out, low=low):
                out[d, p - low, r * 8 : r * 8 + 8, :] = total + start[d, p, here, :]

            shift = pl.multiple_of(a * SPARE, 8)
            sweep(pong, False, low, half, shift, (height - SPARE) // 8, finish)
    else:
        up_out, down_out = outs

        def emit(kinds):
            def finish(d, p, here, r, total):
                i = p - reach
                total = total * weight_ref[i // half, i % half, here, :]
                if "d" in kinds:
                    down_out[d, i, here, :] = total
                if "u" in kinds:
                    up_out[d, i - (own - reach), here, :] = total

            return finish

        for low, high, kinds in ((0, own - reach, "d"), (own - reach, reach, "du"), (reach, own, "u")):
            sweep(pong, False, reach + low, high - low, 0, chunks, emit(kinds))


def solves(adjoint, planes, codes, flows, values, weight=None):
    dirs, reach, height, _ = values[0].shape
    depth = 2 * planes + 2 * reach
    ins = [codes, *flows, *values]
    specs = [SMEM] + [ANY] * 8
    if adjoint:
        outs = [floats(dirs, planes, height - SPARE, LANES)] * 2
    else:
        ins.append(weight)
        specs.append(VMEM)
        outs = [floats(*values[0].shape)] * 2
    scratch = [pltpu.VMEM((n, depth, height, LANES), jnp.float32) for n in (3, 7) + (dirs,) * 4]
    return call(
        functools.partial(solve_kernel, adjoint),
        "adjoint" if adjoint else "forward",
        ins, outs, scratch + [pltpu.SemaphoreType.DMA((4,))] * 2,
        36, 6 * 20 * dirs * depth * height * LANES, specs,
    )


def body(
    directions,
    eigen_basis,
    flow_first,
    flow_second,
    flow_depth,
    face_codes,
    sensor_cells,
    sensor_weight,
):
    dirs, planes, width, _ = directions.shape
    rank = eigen_basis.shape[0]
    count = lax.axis_size("slab")
    height = width // 2 + SPARE
    own, other, above = quad(count)
    each = dirs // GROUPS
    block = planes * height

    def regroup(first, second):
        return lax.ppermute(first, "slab", own), lax.ppermute(second, "slab", other)

    def beyond(up, down):
        return up, down, lax.ppermute(up, "slab", above), lax.ppermute(down, "slab", back(above))

    def pack(token, pair, parts):
        outs = [floats(parts, REACH, height, LANES)] * 2
        kernel = functools.partial(pack_kernel, planes)
        return call(kernel, "pack", [token, *pair], outs, specs=[SMEM, VMEM, VMEM])

    fields = [flow_first, flow_second, flow_depth]
    flows = regroup(*call(
        cut_flows_kernel, "cut", fields, [floats(len(fields) * planes, height, LANES)] * 2,
        [pltpu.SemaphoreType.DMA((2 * len(fields),))], 54, 0, [ANY] * len(fields),
    ))
    basis = eigen_basis.reshape(rank, planes * width, LANES)
    tile, token = gram_tile(basis)
    sensors = [x.reshape(-1, LANES) for x in (sensor_cells, sensor_weight)]
    listed = 2 * sensors[0].shape[0]

    def cut(token, group, sensors=()):
        rows = each * block + sum(x.shape[0] for x in sensors)
        n = len(sensors)
        return call(
            functools.partial(cut_group_kernel, height, group), "cut", [token, *sensors, directions],
            [floats(rows, LANES)] * 2 + [TOKEN], [pltpu.SemaphoreType.DMA((2 * each * planes,))],
            54, 0, [SMEM] + [VMEM] * n + [ANY], [VMEM, VMEM, SMEM],
        )

    *parts, _ = cut(token, range(each), sensors)
    moved = [regroup(*parts)]
    for k in range(each, dirs, each):
        *parts, token = cut(token, range(k, k + each))
        moved.append(regroup(*parts))
    flows = beyond(*pack(token, flows, len(fields)))
    weight, later = call(
        functools.partial(sensor_kernel, width, each * block), "sensors", [*moved[0]],
        [floats(2, planes, height, LANES), TOKEN],
        work=block * listed * 20, out_specs=[VMEM, SMEM],
    )
    tokens = [token] + [later] * (GROUPS - 1)
    values = [beyond(*pack(t, m, each)) for t, m in zip(tokens, moved)]
    forcing = [beyond(*solves(False, planes, face_codes, flows, v, weight)) for v in values]
    summed = [solves(True, planes, face_codes, flows, f) for f in forcing]
    returned = [
        (lax.ppermute(s[0], "slab", back(own)), lax.ppermute(s[1], "slab", back(other)))
        for s in summed
    ]
    images = []
    for k, halves in enumerate(returned):
        copies = count if k == GROUPS - 1 else 1
        tile, image, basis = projections(basis, directions, k * each, halves, tile, copies)
        images.append(image)
    cells = planes * count * width * LANES
    new, coeffs, scales, again = remainders(spread(tile, count), basis, images, cells)
    new, _ = lax.while_loop(
        lambda state: state[1] > 0,
        lambda state: (rescaled(state[0], scales, cells, count), jnp.int32(0)),
        (new, again[0]),
    )
    return (new.reshape(directions.shape), coeffs.T)


def solution(mesh):
    return jax.shard_map(
        body,
        mesh=mesh,
        in_specs=(
            P("grp", "slab", None, None),
            P("grp", "slab", None, None),
            P("slab", None, None),
            P("slab", None, None),
            P("slab", None, None),
            P(),
            P(("grp", "slab")),
            P(("grp", "slab")),
        ),
        out_specs=(P("grp", "slab", None, None), P("grp", None)),
        check_vma=False,
    )
```

```python
import functools

import jax
import jax.numpy as jnp
from jax import lax
from jax.experimental import pallas as pl
from jax.experimental.pallas import tpu as pltpu
from jax.sharding import PartitionSpec as P

STEPS = 2
SWEEPS = 3
GROUPS = 2
SPARE = 16
REACH = STEPS * SWEEPS


DIFFUSION = 0.2
GAMMA = 0.5
LANES = 128
PIECES = 8
EXACT = lax.Precision.HIGHEST
SMEM = pl.BlockSpec(memory_space=pltpu.SMEM)
VMEM = pl.BlockSpec(memory_space=pltpu.VMEM)
ANY = pl.BlockSpec(memory_space=pl.ANY)
VECTOR = 150


def place():
    me, count = lax.axis_index("slab"), lax.axis_size("slab")
    a, b = lax.rem(me // 2, 2), lax.rem(me, 2)
    return a, b, me - 2 * a == 0, me + 2 * (1 - a) == count - 1


def floats(*shape):
    return jax.ShapeDtypeStruct(shape, jnp.float32)


def cost(flops, moved):
    return pl.CostEstimate(flops=int(flops), bytes_accessed=int(moved), transcendentals=0)


def lane_sums(stack):
    ones = jnp.ones((8, LANES), jnp.float32)
    return lax.dot_general(
        ones, stack, (((1,), (1,)), ((), ())), precision=EXACT, preferred_element_type=jnp.float32
    )


def chunks_of(source, into, sems, pieces):
    rows = source.shape[1] // pieces
    return [
        pltpu.make_async_copy(
            source.at[:, pl.ds(k * rows, rows)], into.at[:, pl.ds(k * rows, rows)], sems.at[k]
        )
        for k in range(pieces)
    ]


def gram_kernel(basis_hbm, out_ref, after_ref, basis_ref, acc_ref, sems):
    rank, rows, _ = basis_ref.shape
    tile = 4
    moves = chunks_of(basis_hbm, basis_ref, sems, PIECES)
    for move in moves:
        move.start()
    after_ref[0] = 0
    acc_ref[...] = jnp.zeros_like(acc_ref)
    part = rows // PIECES
    for piece, move in enumerate(moves):
        move.wait()
        for i0 in range(0, rank, tile):
            for j0 in range(i0, rank, tile):
                pairs = [(i, j) for i in range(i0, i0 + tile) for j in range(j0, j0 + tile) if i <= j]

                def add(k, sums, i0=i0, j0=j0, pairs=pairs, piece=piece):
                    at = pl.ds(pl.multiple_of(piece * part + k * 8, 8), 8)
                    left = {i: basis_ref[i, at, :] for i in range(i0, i0 + tile)}
                    right = left if i0 == j0 else {j: basis_ref[j, at, :] for j in range(j0, j0 + tile)}
                    return [s + left[i] * right[j] for s, (i, j) in zip(sums, pairs)]

                sums = [jnp.zeros((8, LANES), jnp.float32) for _ in pairs]
                sums = lax.fori_loop(0, part // 8, add, sums, unroll=8)
                for (i, j), s in zip(pairs, sums):
                    acc_ref[i, j] += s

    row = lax.broadcasted_iota(jnp.int32, (rank, rank), 0)
    col = lax.broadcasted_iota(jnp.int32, (rank, rank), 1)
    gram = jnp.zeros((rank, rank), jnp.float32)
    for i in range(rank):
        sums = lane_sums(jnp.sum(acc_ref[i], axis=1))
        gram = jnp.where(row == i, jnp.broadcast_to(sums[0:1, :], (rank, rank)), gram)
    upper = jnp.where(col >= row, gram, 0.0)
    strict = jnp.where(col > row, gram, 0.0)
    whole = upper + strict.T
    out_ref[...] = jnp.zeros_like(out_ref)
    for k in range(0, rank, 8):
        at = 2 * rank + k * rank // 8
        out_ref[:, at : at + rank] = whole[k : k + 8]


TOKEN = jax.ShapeDtypeStruct((1,), jnp.int32)


def gram_tile(basis):
    rank, rows, _ = basis.shape
    return call(
        gram_kernel, "gram", [basis], [floats(8, LANES), TOKEN],
        [
            pltpu.VMEM(basis.shape, jnp.float32),
            pltpu.VMEM((rank, rank, 8, LANES), jnp.float32),
            pltpu.SemaphoreType.DMA((PIECES,)),
        ],
        54, rank * rank * rows * LANES, [ANY], [VMEM, SMEM],
    )


def spread(tile, count):
    return lax.all_gather(tile, "slab", tiled=True) if count > 1 else tile


def projection_kernel(first, basis_in, dirs_hbm, own_hbm, other_hbm, tile_ref, out_ref, image_ref, *refs):
    moves = None
    if first == 0:
        basis_ref, dirs_ref, halves_ref, side_sems, sems = refs
        moves = chunks_of(basis_in, basis_ref, sems, PIECES)
    else:
        basis_ref, (dirs_ref, halves_ref, side_sems) = basis_in, refs
    rank = basis_ref.shape[0]
    dirs, rows, _ = image_ref.shape
    planes, half = halves_ref.shape[2:4]
    b = place()[1]
    sides = [
        pltpu.make_async_copy(own_hbm, halves_ref.at[0], side_sems.at[0]),
        pltpu.make_async_copy(other_hbm, halves_ref.at[1], side_sems.at[1]),
        pltpu.make_async_copy(dirs_hbm.at[pl.ds(first, dirs)], dirs_ref, side_sems.at[2]),
    ]
    for move in sides + (moves or []):
        move.start()
    for move in sides:
        move.wait()
    sums = [jnp.zeros((8, LANES), jnp.float32) for _ in range((rank + 1) * dirs)]
    piece = rows // PIECES
    for k in range(2 * planes):
        plane, part = k // 2, k % 2
        which = jnp.where(b == part, 0, 1)
        low = k * half
        if moves:
            for m in range(-(-low // piece), -(-(low + half) // piece)):
                moves[m].wait()

        def add(r, sums, plane=plane, which=which, low=low):
            at = pl.ds(pl.multiple_of(low + r * 8, 8), 8)
            here = pl.ds(pl.multiple_of(r * 8, 8), 8)
            image = []
            for d in range(dirs):
                value = halves_ref[which, d, plane, here, :] + GAMMA * dirs_ref[d, at, :]
                image_ref[d, at, :] = value
                image.append(value)
            out = []
            for i in range(rank):
                q = basis_ref[i, at, :]
                out += [sums[i * dirs + d] + q * image[d] for d in range(dirs)]
            return out + [sums[rank * dirs + d] + image[d] * image[d] for d in range(dirs)]

        sums = lax.fori_loop(0, half // 8, add, sums, unroll=4)

    row = lax.broadcasted_iota(jnp.int32, (8, LANES), 0)
    lane = lax.broadcasted_iota(jnp.int32, (8, LANES), 1)
    lines = [sums[i * dirs + d] for d in range(dirs) for i in range(rank)] + sums[rank * dirs :]
    lines = [jnp.sum(line, axis=0, keepdims=True) for line in lines]
    lines.append(jnp.zeros((LANES - len(lines), LANES), jnp.float32))
    found = lane_sums(jnp.concatenate(lines, 0))
    table = tile_ref[...]
    squares = pltpu.roll(found, (rank + first - rank * dirs) % LANES, 1)
    for d in range(dirs):
        products = pltpu.roll(found, (LANES - d * rank) % LANES, 1) if d else found
        table = jnp.where((row == first + d) & (lane < rank), products, table)
        table = jnp.where((row == first + d) & (lane == rank + first + d), squares, table)
    for r in range(out_ref.shape[0] // 8):
        out_ref[r * 8 : (r + 1) * 8, :] = table


def projections(basis, directions, first, halves, tile, count):
    rank, rows, _ = basis.shape
    dirs = halves[0].shape[0]
    outs = [floats(count * 8, LANES), floats(dirs, rows, LANES)]
    scratch = [
        pltpu.VMEM((dirs, rows, LANES), jnp.float32),
        pltpu.VMEM((2, *halves[0].shape), jnp.float32),
        pltpu.SemaphoreType.DMA((3,)),
    ]
    if first == 0:
        outs.append(floats(*basis.shape))
        scratch.append(pltpu.SemaphoreType.DMA((PIECES,)))
    found = call(
        functools.partial(projection_kernel, first), "projections",
        [basis, directions.reshape(-1, rows, LANES), *halves, tile],
        outs, scratch, 24, 2 * rank * dirs * rows * LANES,
        [ANY if first == 0 else VMEM] + [ANY] * 3 + [VMEM],
    )
    return (*found, basis)[:3] if first else found


def summed_tile(parts_ref):
    tiles = [parts_ref[r : r + 8, :] for r in range(0, parts_ref.shape[0], 8)]
    while len(tiles) > 1:
        tiles = [sum(tiles[k : k + 2]) for k in range(0, len(tiles), 2)]
    return tiles[0]


def eliminated(tile, rank):
    gram = [tile[:, 2 * rank + k * rank // 8 :][:, :rank] for k in range(0, rank, 8)]
    lane = lax.broadcasted_iota(jnp.int32, (8, LANES), 1)
    table = jnp.concatenate(
        [
            jnp.concatenate(gram, 0),
            tile[:, 0:rank].T,
            jnp.zeros((rank, LANES - rank - 8), jnp.float32),
        ],
        1,
    )
    table = jnp.concatenate([table, jnp.where(lane < rank + 8, tile, 0.0)], 0)
    row = lax.broadcasted_iota(jnp.int32, table.shape, 0)
    for k in range(rank):
        pivot_row = table[k : k + 1, :] / table[k : k + 1, k : k + 1]
        table = jnp.where(row == k, pivot_row, table - table[:, k : k + 1] * pivot_row)
    return table


def inverse_root(value):
    root = lax.rsqrt(value)
    return root * (1.5 - (0.5 * value * root) * root)


def remainder_kernel(dirs, cells, parts_ref, basis_ref, *refs):
    groups = len(refs) - 8
    images = refs[:groups]
    new_hbm, coeffs_ref, scale_out, again_ref, rem_ref, splat_ref, scale_ref, sems = refs[groups:]
    each = dirs // groups
    rank, rows, _ = basis_ref.shape
    tile = 4
    first = summed_tile(parts_ref)
    table = eliminated(first, rank)
    coeffs_ref[...] = table[0:rank, rank : rank + 8].T[0:dirs]
    for d in range(dirs):
        for j in range(rank):
            splat_ref[d * rank + j] = jnp.broadcast_to(
                table[j : j + 1, rank + d : rank + d + 1], (8, LANES)
            )
    row = lax.broadcasted_iota(jnp.int32, (8, LANES), 0)
    lane = lax.broadcasted_iota(jnp.int32, (8, LANES), 1)
    energy, square = table[rank : rank + 8, :], first
    unsure = (lane == rank + row) & (row < dirs) & jnp.logical_not(energy >= 0.01 * square)
    again_ref[0] = jnp.max(jnp.where(unsure, 1.0, 0.0)).astype(jnp.int32)
    scale = inverse_root(jnp.maximum(energy, 0.0) / cells + 1e-06)
    scales = jnp.zeros((8, LANES), jnp.float32)
    for d in range(dirs):
        one = jnp.broadcast_to(scale[d : d + 1, rank + d : rank + d + 1], (8, LANES))
        scale_ref[d] = one
        scales = jnp.where(row == d, one, scales)
    scale_out[...] = scales
    part = rows // PIECES
    moves = []
    for piece in range(PIECES):
        for j0 in range(0, rank, tile):
            last = j0 + tile == rank
            weights = [[splat_ref[d * rank + j] for j in range(j0, j0 + tile)] for d in range(dirs)]
            scale = [scale_ref[d] for d in range(dirs)] if last else None

            def take(k, carry, j0=j0, last=last, weights=weights, scale=scale, piece=piece):
                at = pl.ds(pl.multiple_of(piece * part + k * 8, 8), 8)
                basis = [basis_ref[j, at, :] for j in range(j0, j0 + tile)]
                for d in range(dirs):
                    left = images[d // each][d % each, at, :] if j0 == 0 else rem_ref[d, at, :]
                    parts = [w * q for w, q in zip(weights[d], basis)]
                    left = left - ((parts[0] + parts[1]) + (parts[2] + parts[3]))
                    rem_ref[d, at, :] = left * scale[d] if last else left
                return carry

            lax.fori_loop(0, part // 8, take, 0, unroll=4)
        at = pl.ds(piece * part, part)
        moves.append(pltpu.make_async_copy(rem_ref.at[:, at], new_hbm.at[:, at], sems.at[piece]))
        moves[-1].start()
    for move in moves:
        move.wait()


def remainders(parts, basis, images, cells):
    rank, rows, _ = basis.shape
    dirs = sum(i.shape[0] for i in images)
    return call(
        functools.partial(remainder_kernel, dirs, cells), "remainder", [parts, basis, *images],
        [
            floats(dirs, rows, LANES),
            floats(dirs, rank),
            floats(8, LANES),
            TOKEN,
        ],
        [
            pltpu.VMEM((dirs, rows, LANES), jnp.float32),
            pltpu.VMEM((dirs * rank, 8, LANES), jnp.float32),
            pltpu.VMEM((dirs, 8, LANES), jnp.float32),
            pltpu.SemaphoreType.DMA((PIECES,)),
        ],
        24, 2 * rank * dirs * rows * LANES, out_specs=[ANY, VMEM, VMEM, SMEM],
    )


def squares_kernel(new_ref, out_ref, sum_ref):
    dirs = new_ref.shape[0]
    row = lax.broadcasted_iota(jnp.int32, (8, LANES), 0)

    @pl.when(pl.program_id(0) == 0)
    def _():
        sum_ref[...] = jnp.zeros_like(sum_ref)

    for d in range(dirs):
        lines = jnp.sum(new_ref[d] * new_ref[d], axis=0, keepdims=True)
        total = jnp.broadcast_to(jnp.sum(lines, axis=1, keepdims=True), (8, LANES))
        sum_ref[...] += jnp.where(row == d, total, 0.0)
    for r in range(out_ref.shape[0] // 8):
        out_ref[r * 8 : (r + 1) * 8, :] = sum_ref[...]


def rescale_kernel(cells, parts_ref, scale_ref, new_ref, out_ref):
    scale = scale_ref[...]
    energy = summed_tile(parts_ref) / scale / scale
    ratio = inverse_root(energy / cells + 1e-06) / scale
    for d in range(new_ref.shape[0]):
        out_ref[d] = new_ref[d] * ratio[d : d + 1, :]


def rescaled(new, scales, cells, count):
    dirs, rows, _ = new.shape
    chunk = 128
    lines = pl.BlockSpec((dirs, chunk, LANES), lambda k: (0, k, 0))
    whole = lambda n: pl.BlockSpec((n, LANES), lambda k: (0, 0))
    parts = pl.pallas_call(
        squares_kernel,
        grid=(rows // chunk,),
        in_specs=[lines],
        out_specs=whole(count * 8),
        out_shape=floats(count * 8, LANES),
        scratch_shapes=[pltpu.VMEM((8, LANES), jnp.float32)],
        compiler_params=pltpu.CompilerParams(vmem_limit_bytes=16 << 20),
        name="squares",
    )(new)
    return pl.pallas_call(
        functools.partial(rescale_kernel, cells),
        grid=(rows // chunk,),
        in_specs=[whole(count * 8), whole(8), lines],
        out_specs=lines,
        out_shape=floats(dirs, rows, LANES),
        compiler_params=pltpu.CompilerParams(vmem_limit_bytes=16 << 20),
        name="rescale",
    )(lax.all_to_all(parts, "slab", 0, 0, tiled=True), scales, new)


def quad(count):
    own, other, above = [], [], []
    for s in range(count):
        q, a, b = s // 4, s // 2 % 2, s % 2
        own.append((s, 4 * q + 2 * b + a))
        other.append((s, 4 * q + 2 * (1 - b) + a))
        up = s + 1 if b == 0 else s + 3
        if up < count:
            above.append((s, up))
    return own, other, above


def back(pairs):
    return [(target, source) for source, target in pairs]


def call(kernel, name, ins, outs, scratch=(), limit=16, work=0, specs=None, out_specs=None):
    moved = sum(x.size * 4 for x in ins) + sum(o.size * 4 for o in outs)
    return pl.pallas_call(
        kernel,
        in_specs=specs or [VMEM] * len(ins),
        out_specs=out_specs or [VMEM] * len(outs),
        out_shape=outs,
        scratch_shapes=list(scratch),
        compiler_params=pltpu.CompilerParams(vmem_limit_bytes=limit << 20),
        cost_estimate=cost(VECTOR * work, moved),
        name=name,
    )(*ins)


def row_parts(width, height):
    b = place()[1]
    return [pl.multiple_of(part * (width - height), 16) for part in (b, 1 - b)]


def cut_flows_kernel(*refs):
    fields, outs, sems = refs[:-3], refs[-3:-1], refs[-1]
    planes, width, _ = fields[0].shape
    height = outs[0].shape[1]
    moves = []
    for k, field in enumerate(fields):
        for out, low in zip(outs, row_parts(width, height)):
            source, target = field.at[:, pl.ds(low, height)], out.at[pl.ds(k * planes, planes)]
            moves.append(pltpu.make_async_copy(source, target, sems.at[len(moves)]))
            moves[-1].start()
    for move in moves:
        move.wait()


def cut_group_kernel(height, group, token_ref, *refs):
    sensors, (dirs_hbm, *outs, after_ref, sems) = refs[:-5], refs[-5:]
    after_ref[0] = 0
    _, planes, width, _ = dirs_hbm.shape
    moves, k = [], 0
    lows = row_parts(width, height)
    for d in group:
        for p in range(planes):
            for out, low in zip(outs, lows):
                source, target = dirs_hbm.at[d, p, pl.ds(low, height)], out.at[pl.ds(k, height)]
                moves.append(pltpu.make_async_copy(source, target, sems.at[len(moves)]))
                moves[-1].start()
            k += height
    for ref in sensors:
        lines = ref.shape[0]
        for out in outs:
            out[k : k + lines, :] = ref[...].astype(jnp.float32)
        k += lines
    for move in moves:
        move.wait()


def pack_kernel(planes, token_ref, own_ref, other_ref, up_ref, down_ref):
    count, reach, height, _ = up_ref.shape
    skip = 2 * planes - reach

    def join(first, second):
        for d in range(count):
            for p in range(2 * planes):
                ref = first if p < planes else second
                k = d * planes + p % planes
                value = ref[k] if len(ref.shape) == 3 else ref[k * height : (k + 1) * height, :]
                if p >= skip:
                    up_ref[d, p - skip] = value
                if p < reach:
                    down_ref[d, p] = value

    a = place()[0]

    @pl.when(a == 0)
    def _():
        join(own_ref, other_ref)

    @pl.when(a == 1)
    def _():
        join(other_ref, own_ref)


def sensor_kernel(width, skip, own_ref, other_ref, out_ref, after_ref):
    after_ref[0] = 0
    a = place()[0]
    _, planes, height, _ = out_ref.shape
    first = a * (width - height)
    count = (own_ref.shape[0] - skip) // 2
    group = 4
    chunk = group * LANES
    targets = planes * height
    rows = lax.broadcasted_iota(jnp.int32, (targets, chunk), 0)
    lanes = lax.broadcasted_iota(jnp.int32, (LANES, chunk), 0)
    for ref, at in ((own_ref, a), (other_ref, 1 - a)):
        total = jnp.zeros((targets, 3 * LANES), jnp.float32)
        for k in range(skip, skip + count, group):
            take = lambda at: jnp.concatenate([ref[at + g : at + g + 1, :] for g in range(group)], 1)
            cell = take(k).astype(jnp.int32)
            weight = take(count + k)
            line = cell // LANES
            lane = cell - line * LANES
            plane = line // width
            row = line - plane * width - first
            inside = (row >= 0) & (row < height)
            target = jnp.where(inside, plane * height + row, -1)
            high = weight.astype(jnp.bfloat16).astype(jnp.float32)
            rest = weight - high
            middle = rest.astype(jnp.bfloat16).astype(jnp.float32)
            low = rest - middle
            hot = jnp.where(rows == target, 1.0, 0.0).astype(jnp.bfloat16)
            here = lanes == lane
            parts = [jnp.where(here, part, 0.0).astype(jnp.bfloat16) for part in (high, middle, low)]
            total += lax.dot_general(
                hot,
                jnp.concatenate(parts, 0),
                (((1,), (1,)), ((), ())),
                preferred_element_type=jnp.float32,
            )
        total = total[:, 0:LANES] + total[:, LANES : 2 * LANES] + total[:, 2 * LANES :]
        out_ref[at] = total.reshape(planes, height, LANES)


def arrivals(parts, into, sems):
    up, down, lo, hi = parts
    reach, depth = REACH, into.shape[1]
    own = depth - 2 * reach
    moves = (
        (lo, into.at[:, 0:reach]),
        (down, into.at[:, reach : 2 * reach]),
        (up.at[:, 2 * reach - own : reach], into.at[:, 2 * reach : reach + own]),
        (hi, into.at[:, reach + own : depth]),
    )
    return [pltpu.make_async_copy(s, t, sems.at[k]) for k, (s, t) in enumerate(moves)]


def coefficients(adjoint, code_ref, flow, coef, low, high):
    _, depth, height, _ = flow.shape
    chunks = height // 8
    own = depth - 2 * REACH
    a, _, at_bottom, at_top = place()
    shape = (8, LANES)
    sub = lax.broadcasted_iota(jnp.int32, shape, 0)
    lane = lax.broadcasted_iota(jnp.int32, shape, 1)
    top_sub, bottom_sub = sub == 7, sub == 0
    last_lane, first_lane = lane == LANES - 1, lane == 0
    opened = [jnp.where(code_ref[k] == 0, 1.0, 0.0).astype(jnp.float32) for k in range(4)]
    low_one = jnp.where(bottom_sub & (a == 0), opened[0], 1.0)
    high_one = jnp.where(top_sub & (a == 1), opened[1], 1.0)
    low_two = jnp.where(first_lane, opened[2], 1.0)
    high_two = jnp.where(last_lane, opened[3], 1.0)

    def both(x):
        positive = DIFFUSION + jnp.maximum(x, 0.0)
        return positive, positive - x

    def at_plane(p, carry):
        outside = ((p < REACH) & at_bottom) | ((p >= REACH + own) & at_top)
        inside = jnp.where(outside, 0.0, 1.0)
        turned = jnp.zeros(shape, jnp.float32)
        for r in range(chunks):
            here = slice(r * 8, r * 8 + 8)
            one, two, three = flow[0, p, here, :], flow[1, p, here, :], flow[2, p, here, :]
            one_turned = pltpu.roll(one, 1, 0)
            one_below = jnp.where(bottom_sub, turned, one_turned)
            turned = one_turned
            two_below = jnp.where(first_lane, 0.0, pltpu.roll(two, 1, 1))
            up = [both(x) for x in (one, two, three)]
            down = [both(x) for x in (one_below, two_below, flow[2, p - 1, here, :])]
            first = up[0][0] if r < chunks - 1 else high_one * up[0][0]
            second = down[0][1] if r > 0 else low_one * down[0][1]
            diagonal = (1.0 + first) + (second + high_two * up[1][0])
            diagonal = diagonal + (low_two * down[1][1] + (up[2][0] + down[2][1]))
            inverse = inside / diagonal
            which = 0 if adjoint else 1
            coef[0, p, here, :] = up[0][which] * inverse
            coef[1, p, here, :] = down[0][1 - which] * inverse
            coef[2, p, here, :] = jnp.where(last_lane, 0.0, up[1][which] * inverse)
            coef[3, p, here, :] = jnp.where(first_lane, 0.0, down[1][1 - which] * inverse)
            coef[4, p, here, :] = up[2][which] * inverse
            coef[5, p, here, :] = down[2][1 - which] * inverse
            coef[6, p, here, :] = inverse
        return carry

    lax.fori_loop(low, high, at_plane, 0)


def solve_kernel(adjoint, code_ref, *refs):
    weight_ref = None if adjoint else refs[8]
    refs = refs[:8] + refs[8 if adjoint else 9 :]
    flow_parts, value_parts, outs = refs[0:4], refs[4:8], refs[8:10]
    flow, coef, rhs, start, ping, pong, flow_sems, sems = refs[10:]
    dirs, depth, height, _ = rhs.shape
    reach = REACH
    own = depth - 2 * reach
    chunks = height // 8
    a = place()[0]
    flow_moves = arrivals(flow_parts, flow, flow_sems)
    moves = arrivals(value_parts, start, sems)
    for move in flow_moves:
        move.start()
    low = 1
    for k, (move, present) in enumerate(zip(flow_moves, (reach, 2 * reach, reach + own, depth))):
        move.wait()
        if k == len(moves) - 1:
            for other in moves:
                other.start()
        high = min(present, depth - 1)
        coefficients(adjoint, code_ref, flow, coef, low, high)
        low = high

    shape = (8, LANES)
    sub = lax.broadcasted_iota(jnp.int32, shape, 0)
    top_sub, bottom_sub = sub == 7, sub == 0
    zero = jnp.zeros(shape, jnp.float32)

    def sweep(source, lead, low, planes, offset, count, store):
        def rows(r):
            return pl.ds(offset + r * 8, 8)

        def at_planes(k, carry):
            p = low + 2 * k
            each = [(q, d) for q in range(2) for d in range(dirs)]
            value = {(q, d): source[d, p + q, rows(0), :] for q, d in each}
            up = {e: pltpu.roll(v, 7, 0) for e, v in value.items()}
            down = {e: pltpu.roll(v, 1, 0) for e, v in value.items()}
            before = dict.fromkeys(each, zero)
            if count < chunks - 1:
                at = pl.multiple_of(jnp.maximum(offset - 8, 0), 8)
                for q, d in each:
                    outer = pltpu.roll(source[d, p + q, pl.ds(at, 8), :], 1, 0)
                    before[q, d] = jnp.where(a == 0, 0.0, outer)
            for r in range(count):
                c = [[coef[m, p + q, rows(r), :] for m in range(6)] for q in range(2)]
                inverse = [coef[6, p + q, rows(r), :] for q in range(2)] if lead else None
                plane = {d: [source[d, p - 1, rows(r), :], value[0, d], value[1, d], source[d, p + 2, rows(r), :]] for d in range(dirs)}
                for q, d in each:
                    here = value[q, d]
                    if r + 1 < count:
                        following = source[d, p + q, rows(r + 1), :]
                        next_up, next_down = pltpu.roll(following, 7, 0), pltpu.roll(following, 1, 0)
                    elif count < chunks - 1:
                        at = pl.multiple_of(jnp.minimum(offset + count * 8, height - 8), 8)
                        following = source[d, p + q, pl.ds(at, 8), :]
                        next_up, next_down = jnp.where(a == 1, 0.0, pltpu.roll(following, 7, 0)), zero
                    else:
                        following, next_up, next_down = zero, zero, zero
                    if lead:
                        total = here * inverse[q]
                        rhs[d, p + q, rows(r), :] = total
                    else:
                        total = rhs[d, p + q, rows(r), :]
                    depth_sum = c[q][4] * plane[d][q + 2] + c[q][5] * plane[d][q]
                    first_sum = c[q][0] * jnp.where(top_sub, next_up, up[q, d])
                    first_sum = first_sum + c[q][1] * jnp.where(bottom_sub, before[q, d], down[q, d])
                    second_sum = c[q][2] * pltpu.roll(here, LANES - 1, 1) + c[q][3] * pltpu.roll(here, 1, 1)
                    total = (total + depth_sum) + (first_sum + second_sum)
                    store(d, p + q, rows(r), r, total)
                    value[q, d], up[q, d], before[q, d], down[q, d] = (
                        following, next_up, down[q, d], next_down
                    )
            return carry

        lax.fori_loop(0, planes // 2, at_planes, 0)

    def into(ref):
        def store(d, p, here, r, total):
            ref[d, p, here, :] = total

        return store

    def again(d, p, here, r, total):
        start[d, p, here, :] = total if adjoint else total + start[d, p, here, :]

    def full(source, lead, step, store):
        offset = pl.multiple_of(a * 8, 8) if adjoint else 0
        sweep(source, lead, 1 + step, depth - 2 - 2 * step, offset, chunks - adjoint, store)

    for move in moves:
        move.wait()
    full(start, True, 0, into(ping))
    full(ping, False, 1, into(pong))
    full(pong, False, 2, again)
    full(start, True, 3, into(ping))
    full(ping, False, 4, into(pong))

    half = own // 2
    if adjoint:
        for out, side in zip(outs, (a, 1 - a)):
            low = reach + side * half

            def finish(d, p, here, r, total, out=out, low=low):
                out[d, p - low, r * 8 : r * 8 + 8, :] = total + start[d, p, here, :]

            shift = pl.multiple_of(a * SPARE, 8)
            sweep(pong, False, low, half, shift, (height - SPARE) // 8, finish)
    else:
        up_out, down_out = outs

        def emit(kinds):
            def finish(d, p, here, r, total):
                i = p - reach
                total = total * weight_ref[i // half, i % half, here, :]
                if "d" in kinds:
                    down_out[d, i, here, :] = total
                if "u" in kinds:
                    up_out[d, i - (own - reach), here, :] = total

            return finish

        for low, high, kinds in ((0, own - reach, "d"), (own - reach, reach, "du"), (reach, own, "u")):
            sweep(pong, False, reach + low, high - low, 0, chunks, emit(kinds))


def solves(adjoint, planes, codes, flows, values, weight=None):
    dirs, reach, height, _ = values[0].shape
    depth = 2 * planes + 2 * reach
    ins = [codes, *flows, *values]
    specs = [SMEM] + [ANY] * 8
    if adjoint:
        outs = [floats(dirs, planes, height - SPARE, LANES)] * 2
    else:
        ins.append(weight)
        specs.append(VMEM)
        outs = [floats(*values[0].shape)] * 2
    scratch = [pltpu.VMEM((n, depth, height, LANES), jnp.float32) for n in (3, 7) + (dirs,) * 4]
    return call(
        functools.partial(solve_kernel, adjoint),
        "adjoint" if adjoint else "forward",
        ins, outs, scratch + [pltpu.SemaphoreType.DMA((4,))] * 2,
        36, 6 * 20 * dirs * depth * height * LANES, specs,
    )


def body(
    directions,
    eigen_basis,
    flow_first,
    flow_second,
    flow_depth,
    face_codes,
    sensor_cells,
    sensor_weight,
):
    dirs, planes, width, _ = directions.shape
    rank = eigen_basis.shape[0]
    count = lax.axis_size("slab")
    height = width // 2 + SPARE
    own, other, above = quad(count)
    each = dirs // GROUPS
    block = planes * height

    def regroup(first, second):
        return lax.ppermute(first, "slab", own), lax.ppermute(second, "slab", other)

    def beyond(up, down):
        return up, down, lax.ppermute(up, "slab", above), lax.ppermute(down, "slab", back(above))

    def pack(token, pair, parts):
        outs = [floats(parts, REACH, height, LANES)] * 2
        kernel = functools.partial(pack_kernel, planes)
        return call(kernel, "pack", [token, *pair], outs, specs=[SMEM, VMEM, VMEM])

    fields = [flow_first, flow_second, flow_depth]
    flows = regroup(*call(
        cut_flows_kernel, "cut", fields, [floats(len(fields) * planes, height, LANES)] * 2,
        [pltpu.SemaphoreType.DMA((2 * len(fields),))], 54, 0, [ANY] * len(fields),
    ))
    basis = eigen_basis.reshape(rank, planes * width, LANES)
    tile, token = gram_tile(basis)
    sensors = [x.reshape(-1, LANES) for x in (sensor_cells, sensor_weight)]
    listed = 2 * sensors[0].shape[0]

    def cut(token, group, sensors=()):
        rows = each * block + sum(x.shape[0] for x in sensors)
        n = len(sensors)
        return call(
            functools.partial(cut_group_kernel, height, group), "cut", [token, *sensors, directions],
            [floats(rows, LANES)] * 2 + [TOKEN], [pltpu.SemaphoreType.DMA((2 * each * planes,))],
            54, 0, [SMEM] + [VMEM] * n + [ANY], [VMEM, VMEM, SMEM],
        )

    *parts, _ = cut(token, range(each), sensors)
    moved = [regroup(*parts)]
    for k in range(each, dirs, each):
        *parts, token = cut(token, range(k, k + each))
        moved.append(regroup(*parts))
    flows = beyond(*pack(token, flows, len(fields)))
    weight, later = call(
        functools.partial(sensor_kernel, width, each * block), "sensors", [*moved[0]],
        [floats(2, planes, height, LANES), TOKEN],
        work=block * listed * 20, out_specs=[VMEM, SMEM],
    )
    tokens = [token] + [later] * (GROUPS - 1)
    values = [beyond(*pack(t, m, each)) for t, m in zip(tokens, moved)]
    forcing = [beyond(*solves(False, planes, face_codes, flows, v, weight)) for v in values]
    summed = [solves(True, planes, face_codes, flows, f) for f in forcing]
    returned = [
        (lax.ppermute(s[0], "slab", back(own)), lax.ppermute(s[1], "slab", back(other)))
        for s in summed
    ]
    images = []
    for k, halves in enumerate(returned):
        tile, image, basis = projections(basis, directions, k * each, halves, tile, 1)
        images.append(image)
    cells = planes * count * width * LANES
    new, coeffs, scales, again = remainders(spread(tile, count), basis, images, cells)
    new, _ = lax.while_loop(
        lambda state: state[1] > 0,
        lambda state: (rescaled(state[0], scales, cells, count), jnp.int32(0)),
        (new, again[0]),
    )
    return (new.reshape(directions.shape), coeffs.T)


def solution(mesh):
    return jax.shard_map(
        body,
        mesh=mesh,
        in_specs=(
            P("grp", "slab", None, None),
            P("grp", "slab", None, None),
            P("slab", None, None),
            P("slab", None, None),
            P("slab", None, None),
            P(),
            P(("grp", "slab")),
            P(("grp", "slab")),
        ),
        out_specs=(P("grp", "slab", None, None), P("grp", None)),
        check_vma=False,
    )
```
